32 devices in a mesh: groups: 2 (over y), nodes: 4 (over z), feat: 4 (over x, core).
Axes of the slice: x: 2, y: 2, z: 4, core: 2. Of those that a mesh axis runs over, the one named last changes fastest.
Arguments:
- latent: bfloat16 [128, 512], P(('groups', 'nodes'), 'feat'), parts along dimension 0, may hold values from -6 to 6
- edge_state: bfloat16 [2048, 512], P(('groups', 'nodes'), 'feat'), parts along dimension 0, may hold values from -6 to 6
- send_rows: int32 [8, 4, 8], P('groups'), parts along dimension 0, may hold values from 0 to 15, as said below
- sender_slot: int32 [2048], P(('groups', 'nodes')), parts along dimension 0, may hold values from 0 to 47, as said below
- receiver_row: int32 [2048], P(('groups', 'nodes')), parts along dimension 0, may hold values from 0 to 15
- edge_in_weight: bfloat16 [512, 1536], P('feat'), may hold values from -0.15625 to 0.15625
- edge_out_weight: bfloat16 [512, 512], P('feat'), may hold values from -0.25 to 0.25
- edge_gain: bfloat16 [512], P('feat'), may hold values from 0.5 to 1.5
- node_in_weight: bfloat16 [512, 1024], P('feat'), may hold values from -0.1875 to 0.1875
- node_out_weight: bfloat16 [512, 512], P('feat'), may hold values from -0.25 to 0.25
- node_gain: bfloat16 [512], P('feat'), may hold values from 0.5 to 1.5
- edge_cot: bfloat16 [2048, 512], P(('groups', 'nodes'), 'feat'), parts along dimension 0, may hold values from -6 to 6
- node_cot: bfloat16 [128, 512], P(('groups', 'nodes'), 'feat'), parts along dimension 0, may hold values from -6 to 6
Outputs:
- edge_next: bfloat16 [2048, 512], P(('groups', 'nodes'), 'feat'), parts along dimension 0
- node_next: bfloat16 [128, 512], P(('groups', 'nodes'), 'feat'), parts along dimension 0
- edge_grad: bfloat16 [2048, 512], P(('groups', 'nodes'), 'feat'), parts along dimension 0
- node_grad: bfloat16 [128, 512], P(('groups', 'nodes'), 'feat'), parts along dimension 0
The draws below stay inside these ranges and needn't reach their ends.
There are 2 independent parts, one for each index of `groups`. The reference program is written for one: setup_inputs(seed, part) draws one part's arguments, and reference() takes and returns one part's arrays. A program takes and returns all parts, laid end to end along the dimension named above; an argument that names none is the same for every part. Nothing has to cross between parts.
Inputs may be any that keep to these rules, and one draw needn't show every extreme that they name: The 8 rows send_rows[s, d, 0:8] of one pair are distinct rows of block s. `sender_slot`: for an edge of block b, an entry at or above 16 is 16 + s * 8 + k with s != b; the entries of block b that refer to pair (s, b) use its first slots only; blocks next to b along the curve fill all 8 slots.
All inputs are finite; a program needn't handle non-finite values.
Results may differ from the reference program's by a relative error of at most 0.015.
Values may be sent and summed in bfloat16 or wider, within the bound.
No kernel may reach another device: no remote copies, remote signals or barrier semaphores. Data moves between devices by JAX's collectives and lax.ppermute only.
A program may use at most 64 MiB of HBM per device.

```python
import jax
import jax.numpy as jnp
from jax import lax

D = 512
HID = 512
NODE_DEV = 16
EDGE_DEV = 256
SLOTS = 8
NODES = 64
EDGES = 1024
N_NODES = 4


def draw_send_rows(key, part):
    key = jax.random.fold_in(key, 5)
    pair_keys = jax.random.split(key, N_NODES * N_NODES)
    orders = jax.vmap(lambda pair_key: jax.random.permutation(pair_key, NODE_DEV))(pair_keys)
    return orders[:, :SLOTS].reshape(N_NODES, N_NODES, SLOTS).astype(jnp.int32)


def draw_sender_slot(key, part):
    key = jax.random.fold_in(key, 11)
    key_far, key_local, key_order = jax.random.split(key, 3)
    src_index = jnp.arange(N_NODES, dtype=jnp.int32)[:, None]
    dst_index = jnp.arange(N_NODES, dtype=jnp.int32)[None, :]
    distance = jnp.abs(src_index - dst_index)
    far_counts = jax.random.randint(key_far, (N_NODES, N_NODES), 1, SLOTS // 2 + 1)
    counts = jnp.where(distance == 1, SLOTS, jnp.where(distance == 0, 0, far_counts)).astype(jnp.int32)
    end_marks = jnp.cumsum(counts, axis=0).T
    start_marks = end_marks - counts.T
    position = jnp.arange(EDGE_DEV, dtype=jnp.int32)
    source_dev = jnp.sum((end_marks[:, None, :] <= position[None, :, None]).astype(jnp.int32), axis=2)
    clipped = jnp.minimum(source_dev, N_NODES - 1).astype(jnp.int32)
    begins = jnp.take_along_axis(start_marks, clipped, axis=1)
    remote_slot = NODE_DEV + clipped * SLOTS + position[None, :] - begins
    local_rows = jax.random.randint(key_local, (N_NODES, EDGE_DEV), 0, NODE_DEV)
    chosen = jnp.where(position[None, :] < end_marks[:, -1:], remote_slot, local_rows)
    shuffled = jax.vmap(jax.random.permutation)(jax.random.split(key_order, N_NODES), chosen)
    return shuffled.reshape(-1).astype(jnp.int32)


def plant(array, key, low, largest):
    extent = array.shape
    index_at = [jax.random.randint(jax.random.fold_in(key, axis), (), 0, extent[axis]) for axis in range(len(extent))]
    array = array.at[tuple(index_at)].set(low)
    longest = extent.index(max(extent))
    index_at[longest] = (index_at[longest] + 1) % extent[longest]
    return array.at[tuple(index_at)].set(largest)


def shard_levels(key, extent, shards, least, top_value):
    loudness, own = 1.0, jax.random.fold_in(key, 6)
    for dim, shards_of in shards:
        steps = jnp.exp(jax.random.uniform(jax.random.fold_in(own, dim), (shards_of,), jnp.float32, least / len(shards), top_value / len(shards)))
        loudness = loudness * jnp.repeat(steps, extent[dim] // shards_of).reshape([-1 if axis == dim else 1 for axis in range(len(extent))])
    return loudness


def gaussian(own_key, dims, scale, reach, shards=(), held_as=jnp.bfloat16):
    drawn = jax.random.normal(own_key, dims, jnp.float32) * scale
    if len(shards) > 0:
        drawn = shard_levels(own_key, dims, shards, -0.22, 0.18) * drawn
    return jnp.clip(drawn, min=-reach, max=reach).astype(held_as)


def setup_inputs(seed: int = 0, part: int = 0) -> dict:
    key_of = jax.random.split(jax.random.key(seed), 14)
    own_keys = jax.random.split(jax.random.fold_in(key_of[13], part), 14)
    latent = gaussian(own_keys[0], (NODES, D), 1.0, 6.0, ((0, 4), (1, 4)))
    edge_state = gaussian(own_keys[1], (EDGES, D), 1.0, 6.0, ((0, 4), (1, 4)))
    send_rows = draw_send_rows(jax.random.fold_in(jax.random.fold_in(key_of[13], part), 71), part)
    sender_slot = draw_sender_slot(jax.random.fold_in(jax.random.fold_in(key_of[13], part), 71), part)
    receiver_row = plant(jax.random.randint(own_keys[4], (EDGES,), 0, NODE_DEV), jax.random.fold_in(own_keys[4], 1), 0, NODE_DEV - 1).astype(jnp.int32)
    edge_in_weight = gaussian(key_of[5], (HID, 3 * D), (3 * D) ** -0.5, 0.15625, ((0, 4),))
    edge_out_weight = gaussian(key_of[6], (HID, D), HID ** -0.5, 0.25, ((0, 4),))
    edge_gain = jnp.clip(1.0 + 0.1 * jax.random.normal(key_of[7], (D,), jnp.float32), 0.5, 1.5).astype(jnp.bfloat16)
    node_in_weight = gaussian(key_of[8], (HID, 2 * D), (2 * D) ** -0.5, 0.1875, ((0, 4),))
    node_out_weight = gaussian(key_of[9], (HID, D), HID ** -0.5, 0.25, ((0, 4),))
    node_gain = jnp.clip(1.0 + 0.1 * jax.random.normal(key_of[10], (D,), jnp.float32), 0.5, 1.5).astype(jnp.bfloat16)
    edge_cot = gaussian(own_keys[11], (EDGES, D), 1.0, 6.0, ((0, 4), (1, 4)))
    node_cot = gaussian(own_keys[12], (NODES, D), 1.0, 6.0, ((0, 4), (1, 4)))
    return dict(latent=latent, edge_state=edge_state, send_rows=send_rows, sender_slot=sender_slot, receiver_row=receiver_row, edge_in_weight=edge_in_weight, edge_out_weight=edge_out_weight, edge_gain=edge_gain, node_in_weight=node_in_weight, node_out_weight=node_out_weight, node_gain=node_gain, edge_cot=edge_cot, node_cot=node_cot)


epsilon = 1e-05

def normalize(values):
    row_mean = lax.optimization_barrier(jnp.mean(values, axis=1, keepdims=True))
    row_square = lax.optimization_barrier(jnp.mean(values * values, axis=1, keepdims=True))
    inverse = lax.rsqrt(row_square - row_mean * row_mean + epsilon)
    return ((values - row_mean) * inverse, inverse)

def norm_back(grad_normed, normed, inverse):
    row_total = lax.optimization_barrier(jnp.mean(grad_normed, axis=1, keepdims=True))
    row_cross = lax.optimization_barrier(jnp.mean(grad_normed * normed, axis=1, keepdims=True))
    return inverse * (grad_normed - row_total - normed * row_cross)

def swish_slope(pre_act):
    sigma = jax.nn.sigmoid(pre_act)
    return sigma * (1.0 + pre_act * (1.0 - sigma))

def contract_rows(grads, weight):
    return lax.dot_general(grads, weight, (((1,), (1,)), ((), ())), preferred_element_type=jnp.float32)

def reference(latent, edge_state, send_rows, sender_slot, receiver_row, edge_in_weight, edge_out_weight, edge_gain, node_in_weight, node_out_weight, node_gain, edge_cot, node_cot):
    device_of = (jnp.arange(EDGES, dtype=jnp.int32) // EDGE_DEV).astype(jnp.int32)
    remote_slot = jnp.maximum(sender_slot - NODE_DEV, 0)
    source_dev = remote_slot // SLOTS
    source_k = remote_slot % SLOTS
    far_rows = send_rows[source_dev, device_of, source_k]
    sender = jnp.where(sender_slot < NODE_DEV, device_of * NODE_DEV + sender_slot, source_dev * NODE_DEV + far_rows).astype(jnp.int32)
    receiver = (device_of * NODE_DEV + receiver_row).astype(jnp.int32)
    sender_rows = jnp.take(latent, sender, axis=0)
    receiver_rows = jnp.take(latent, receiver, axis=0)
    edge_pre = contract_rows(edge_state, edge_in_weight[:, :D])
    edge_pre = edge_pre + contract_rows(sender_rows, edge_in_weight[:, D:2 * D])
    edge_pre = edge_pre + contract_rows(receiver_rows, edge_in_weight[:, 2 * D:])
    edge_act = jax.nn.silu(edge_pre).astype(jnp.bfloat16)
    edge_normed, edge_inverse = normalize(jnp.dot(edge_act, edge_out_weight, preferred_element_type=jnp.float32))
    edge_next = (edge_state.astype(jnp.float32) + edge_normed * edge_gain.astype(jnp.float32)).astype(jnp.bfloat16)
    aggregate = jax.ops.segment_sum(edge_next.astype(jnp.float32), receiver, num_segments=NODES).astype(jnp.bfloat16)
    node_pre = contract_rows(latent, node_in_weight[:, :D])
    node_pre = node_pre + contract_rows(aggregate, node_in_weight[:, D:])
    node_act = jax.nn.silu(node_pre).astype(jnp.bfloat16)
    node_normed, node_inverse = normalize(jnp.dot(node_act, node_out_weight, preferred_element_type=jnp.float32))
    node_next = (latent.astype(jnp.float32) + node_normed * node_gain.astype(jnp.float32)).astype(jnp.bfloat16)
    node_grad_in = node_cot.astype(jnp.float32)
    node_dy = norm_back(node_grad_in * node_gain.astype(jnp.float32), node_normed, node_inverse).astype(jnp.bfloat16)
    node_dpre = (contract_rows(node_dy, node_out_weight) * swish_slope(node_pre)).astype(jnp.bfloat16)
    node_dx = jnp.dot(node_dpre, node_in_weight, preferred_element_type=jnp.float32)
    node_dh = node_dx[:, :D]
    agg_grad = node_dx[:, D:]
    edge_total = edge_cot.astype(jnp.float32) + jnp.take(agg_grad, receiver, axis=0)
    edge_dy = norm_back(edge_total * edge_gain.astype(jnp.float32), edge_normed, edge_inverse).astype(jnp.bfloat16)
    edge_dpre = (contract_rows(edge_dy, edge_out_weight) * swish_slope(edge_pre)).astype(jnp.bfloat16)
    edge_dx = jnp.dot(edge_dpre, edge_in_weight, preferred_element_type=jnp.float32)
    edge_grad = (edge_total + edge_dx[:, :D]).astype(jnp.bfloat16)
    node_sum = node_grad_in + node_dh
    node_sum = node_sum + jax.ops.segment_sum(edge_dx[:, 2 * D:], receiver, num_segments=NODES)
    node_sum = node_sum + jax.ops.segment_sum(edge_dx[:, D:2 * D], sender, num_segments=NODES)
    node_grad = node_sum.astype(jnp.bfloat16)
    return (edge_next, node_next, edge_grad, node_grad)
```

```python
import jax
import jax.numpy as jnp
from jax import lax
from jax.sharding import PartitionSpec as P

epsilon = 1e-05
f32 = jnp.float32
bf16 = jnp.bfloat16


def one_hot(indices, classes):
    return (indices[:, None] == jnp.arange(classes, dtype=jnp.int32)[None, :]).astype(bf16)


def dot(left, right):
    return jnp.dot(left, right, preferred_element_type=f32)


def dot_rows(left, right):
    return lax.dot_general(left, right, (((1,), (1,)), ((), ())), preferred_element_type=f32)


def dot_cols(left, right):
    return lax.dot_general(left, right, (((0,), (0,)), ((), ())), preferred_element_type=f32)


def split(values):
    high = values.astype(bf16)
    return high, (values - high.astype(f32)).astype(bf16)


def swish_slope(pre_act):
    sigma = jax.nn.sigmoid(pre_act)
    return sigma * (1.0 + pre_act * (1.0 - sigma))


def normalize(values):
    mean = jnp.mean(values, axis=1, keepdims=True)
    square = jnp.mean(values * values, axis=1, keepdims=True)
    inverse = lax.rsqrt(square - mean * mean + epsilon)
    return (values - mean) * inverse, inverse


def norm_back(grad, normed, inverse):
    total = jnp.mean(grad, axis=1, keepdims=True)
    cross = jnp.mean(grad * normed, axis=1, keepdims=True)
    return inverse * (grad - total - normed * cross)


def side_by_side(blocks):
    count, rows, width = blocks.shape
    return blocks.transpose(1, 0, 2).reshape(rows, count * width)


def shards(
    latent,
    edge_state,
    send_rows,
    sender_slot,
    receiver_row,
    edge_in_weight,
    edge_out_weight,
    edge_gain,
    node_in_weight,
    node_out_weight,
    node_gain,
    edge_cot,
    node_cot,
):
    node_dev, width = latent.shape
    edge_dev = edge_state.shape[0]
    blocks = send_rows.shape[0]
    slots = send_rows.shape[2]
    feats = lax.axis_size("feat")
    features = width * feats
    block = lax.axis_index("nodes")
    feat = lax.axis_index("feat")

    def ring_gather(values):
        held = [values]
        for step in range(1, feats):
            held.append(
                lax.ppermute(
                    values, "feat", [(i, (i + step) % feats) for i in range(feats)]
                )
            )
        rising = jnp.stack(held[::-1] + held[::-1])
        return lax.dynamic_slice_in_dim(rising, feats - 1 - feat, feats, axis=0)

    def gather(values):
        return lax.all_gather(values, "feat", axis=0)

    gains = lax.all_gather(jnp.stack([edge_gain, node_gain]), "feat", axis=1, tiled=True).astype(f32)
    cots = side_by_side(ring_gather(jnp.concatenate([edge_cot, node_cot])))
    edge_cot_full, node_cot_full = cots[:edge_dev].astype(f32), cots[edge_dev:].astype(f32)
    out_full = ring_gather(edge_out_weight).reshape(-1, features)

    table = lax.all_gather(latent, ("nodes", "feat"), axis=0)
    table = table.reshape(blocks, feats, node_dev, width).transpose(0, 2, 1, 3)
    table = table.reshape(blocks * node_dev, features)
    state = side_by_side(gather(edge_state))
    own = lax.dynamic_slice_in_dim(table, block * node_dev, node_dev, axis=0)

    lent = lax.dynamic_index_in_dim(send_rows, block, axis=1, keepdims=False)
    lent = lent + node_dev * jnp.arange(blocks, dtype=jnp.int32)[:, None]
    rows_of = jnp.concatenate(
        [block * node_dev + jnp.arange(node_dev, dtype=jnp.int32), lent.reshape(-1)]
    )
    pick = dot(
        one_hot(sender_slot, node_dev + blocks * slots), one_hot(rows_of, blocks * node_dev)
    ).astype(bf16)
    take = one_hot(receiver_row, node_dev)

    sender_rows = dot(pick, table).astype(bf16)
    receiver_rows = dot(take, own).astype(bf16)
    edge_pre = dot_rows(jnp.concatenate([state, sender_rows, receiver_rows], axis=1), edge_in_weight)
    edge_act = jax.nn.silu(edge_pre).astype(bf16)

    act_full = side_by_side(gather(edge_act))
    edge_normed, edge_inverse = normalize(dot(act_full, out_full))
    edge_next_full = (state.astype(f32) + edge_normed * gains[0]).astype(bf16)
    edge_next = lax.dynamic_slice_in_dim(edge_next_full, feat * width, width, axis=1)
    aggregate = dot_cols(take, edge_next_full).astype(bf16)
    node_pre = dot_rows(jnp.concatenate([own, aggregate], axis=1), node_in_weight)
    node_act = jax.nn.silu(node_pre).astype(bf16)

    node_out = jnp.sum(gather(dot(node_act, node_out_weight).astype(bf16)).astype(f32), axis=0)
    node_normed, node_inverse = normalize(node_out)
    node_next_full = (own.astype(f32) + node_normed * gains[1]).astype(bf16)
    node_next = lax.dynamic_slice_in_dim(node_next_full, feat * width, width, axis=1)
    node_dy = norm_back(node_cot_full * gains[1], node_normed, node_inverse).astype(bf16)
    node_dpre = (dot_rows(node_dy, node_out_weight) * swish_slope(node_pre)).astype(bf16)
    node_dx = dot(node_dpre, node_in_weight)

    agg_grad = jnp.sum(gather(node_dx[:, features:].astype(bf16)).astype(f32), axis=0)
    high, low = split(agg_grad)
    edge_total = edge_cot_full + dot(take, high) + dot(take, low)
    edge_dy = norm_back(edge_total * gains[0], edge_normed, edge_inverse).astype(bf16)
    edge_dpre = (dot_rows(edge_dy, edge_out_weight) * swish_slope(edge_pre)).astype(bf16)

    edge_de = dot(edge_dpre, edge_in_weight[:, :features]).astype(bf16)
    edge_de = edge_de.reshape(edge_dev, feats, width).transpose(1, 0, 2)
    edge_share = jnp.sum(lax.all_to_all(edge_de, "feat", 0, 0).astype(f32), axis=0)
    own_total = lax.dynamic_slice_in_dim(edge_total, feat * width, width, axis=1)
    edge_grad = (own_total + edge_share).astype(bf16)

    sent_high, sent_low = split(dot_cols(pick, edge_dpre))
    sender_weight = edge_in_weight[:, features : 2 * features]
    sent = dot(sent_high, sender_weight) + dot(sent_low, sender_weight)
    got_high, got_low = split(dot_cols(take, edge_dpre))
    receiver_weight = edge_in_weight[:, 2 * features :]
    home = dot(got_high, receiver_weight) + dot(got_low, receiver_weight) + node_dx[:, :features]
    sent = sent.reshape(blocks, node_dev, features)
    is_home = (jnp.arange(blocks) == block)[:, None, None]
    sent = (sent + jnp.where(is_home, home[None], 0.0)).astype(bf16)
    sent = sent.reshape(blocks, node_dev, feats, width).transpose(0, 2, 1, 3)
    sent = sent.reshape(blocks * feats, node_dev, width)
    node_share = jnp.sum(lax.all_to_all(sent, ("nodes", "feat"), 0, 0).astype(f32), axis=0)
    node_grad = (node_cot.astype(f32) + node_share).astype(bf16)
    return (edge_next, node_next, edge_grad, node_grad)


def solution(mesh):
    rows = P(("groups", "nodes"), "feat")
    flat = P(("groups", "nodes"))
    matrix = P("feat", None)
    vector = P("feat")
    return jax.shard_map(
        shards,
        mesh=mesh,
        in_specs=(
            rows,
            rows,
            P("groups", None, None),
            flat,
            flat,
            matrix,
            matrix,
            vector,
            matrix,
            matrix,
            vector,
            rows,
            rows,
        ),
        out_specs=(rows, rows, rows, rows),
        check_vma=False,
    )
```

```python
import jax
import jax.numpy as jnp
from jax import lax
from jax.sharding import PartitionSpec as P

epsilon = 1e-05
f32 = jnp.float32
bf16 = jnp.bfloat16


def one_hot(indices, classes):
    return (indices[:, None] == jnp.arange(classes, dtype=jnp.int32)[None, :]).astype(bf16)


def dot(left, right):
    return jnp.dot(left, right, preferred_element_type=f32)


def dot_rows(left, right):
    return lax.dot_general(left, right, (((1,), (1,)), ((), ())), preferred_element_type=f32)


def dot_cols(left, right):
    return lax.dot_general(left, right, (((0,), (0,)), ((), ())), preferred_element_type=f32)


def split(values):
    high = values.astype(bf16)
    return high, (values - high.astype(f32)).astype(bf16)


def swish_slope(pre_act):
    sigma = jax.nn.sigmoid(pre_act)
    return sigma * (1.0 + pre_act * (1.0 - sigma))


def normalize(values):
    mean = jnp.mean(values, axis=1, keepdims=True)
    square = jnp.mean(values * values, axis=1, keepdims=True)
    inverse = lax.rsqrt(square - mean * mean + epsilon)
    return (values - mean) * inverse, inverse


def norm_back(grad, normed, inverse):
    total = jnp.mean(grad, axis=1, keepdims=True)
    cross = jnp.mean(grad * normed, axis=1, keepdims=True)
    return inverse * (grad - total - normed * cross)


def side_by_side(blocks):
    count, rows, width = blocks.shape
    return blocks.transpose(1, 0, 2).reshape(rows, count * width)


def shards(
    latent,
    edge_state,
    send_rows,
    sender_slot,
    receiver_row,
    edge_in_weight,
    edge_out_weight,
    edge_gain,
    node_in_weight,
    node_out_weight,
    node_gain,
    edge_cot,
    node_cot,
):
    node_dev, width = latent.shape
    edge_dev = edge_state.shape[0]
    blocks = send_rows.shape[0]
    slots = send_rows.shape[2]
    feats = lax.axis_size("feat")
    features = width * feats
    block = lax.axis_index("nodes")
    feat = lax.axis_index("feat")

    def shifted(values, axis, step):
        count = lax.axis_size(axis)
        return lax.ppermute(values, axis, [(i, (i + step) % count) for i in range(count)])

    def ring(values):
        return [values] + [shifted(values, "feat", step) for step in range(1, feats)]

    def rising(held):
        twice = jnp.stack(held[::-1] + held[::-1])
        return lax.dynamic_slice_in_dim(twice, feats - 1 - feat, feats, axis=0)

    def total_over_feat(partial):
        return sum(part.astype(f32) for part in ring(partial.astype(bf16)))

    state_weight = edge_in_weight[:, :features]
    sender_weight = edge_in_weight[:, features : 2 * features]
    receiver_weight = edge_in_weight[:, 2 * features :]

    first = side_by_side(rising(ring(jnp.concatenate([latent, edge_state]))))
    own, state = first[:node_dev], first[node_dev:]
    lent_rows = jnp.stack(split(dot_rows(own, sender_weight)))
    tables = [lent_rows] + [shifted(lent_rows, "nodes", step) for step in range(1, blocks)]

    held_out = ring(edge_out_weight)
    extra = jnp.concatenate([edge_cot, node_cot, edge_gain[None], node_gain[None]])
    extra = side_by_side(rising(ring(extra))).astype(f32)
    edge_cot_full = extra[:edge_dev]
    node_cot_full = extra[edge_dev : edge_dev + node_dev]
    edge_gains = extra[edge_dev + node_dev : edge_dev + node_dev + 1]
    node_gains = extra[edge_dev + node_dev + 1 :]

    lent = lax.dynamic_index_in_dim(send_rows, block, axis=1, keepdims=False)
    steps = (block - jnp.arange(blocks, dtype=jnp.int32)) % blocks
    rows_of = jnp.concatenate(
        [jnp.arange(node_dev, dtype=jnp.int32), (lent + node_dev * steps[:, None]).reshape(-1)]
    )
    pick = dot(
        one_hot(sender_slot, node_dev + blocks * slots), one_hot(rows_of, blocks * node_dev)
    ).astype(bf16)
    take = one_hot(receiver_row, node_dev)

    edge_pre = dot_rows(state, state_weight)
    high, low = split(dot_rows(own, receiver_weight))
    edge_pre = edge_pre + dot(take, high) + dot(take, low)
    lent_high = jnp.concatenate([part[0] for part in tables])
    lent_low = jnp.concatenate([part[1] for part in tables])
    edge_pre = edge_pre + dot(pick, lent_high) + dot(pick, lent_low)
    edge_act = jax.nn.silu(edge_pre).astype(bf16)

    edge_out = sum(dot(act, weight) for act, weight in zip(ring(edge_act), held_out))
    edge_normed, edge_inverse = normalize(edge_out)
    edge_next_full = (state.astype(f32) + edge_normed * edge_gains).astype(bf16)
    edge_next = lax.dynamic_slice_in_dim(edge_next_full, feat * width, width, axis=1)
    aggregate = dot_cols(take, edge_next_full).astype(bf16)
    node_pre = dot_rows(jnp.concatenate([own, aggregate], axis=1), node_in_weight)
    node_act = jax.nn.silu(node_pre).astype(bf16)

    node_normed, node_inverse = normalize(total_over_feat(dot(node_act, node_out_weight)))
    node_next_full = (own.astype(f32) + node_normed * node_gains).astype(bf16)
    node_next = lax.dynamic_slice_in_dim(node_next_full, feat * width, width, axis=1)
    node_dy = norm_back(node_cot_full * node_gains, node_normed, node_inverse).astype(bf16)
    node_dpre = (dot_rows(node_dy, node_out_weight) * swish_slope(node_pre)).astype(bf16)

    high, low = split(total_over_feat(dot(node_dpre, node_in_weight[:, features:])))
    edge_total = edge_cot_full + dot(take, high) + dot(take, low)
    edge_dy = norm_back(edge_total * edge_gains, edge_normed, edge_inverse).astype(bf16)
    edge_dpre = (dot_rows(edge_dy, edge_out_weight) * swish_slope(edge_pre)).astype(bf16)

    def scatter(partial):
        rows = partial.shape[0]
        partial = partial.astype(bf16).reshape(rows, feats, width).transpose(1, 0, 2)
        total = lax.dynamic_index_in_dim(partial, feat, axis=0, keepdims=False).astype(f32)
        for step in range(1, feats):
            sent = lax.dynamic_index_in_dim(partial, (feat + step) % feats, axis=0, keepdims=False)
            total = total + shifted(sent, "feat", step).astype(f32)
        return total

    parts = dot_cols(pick, edge_dpre).reshape(blocks, node_dev, -1)
    sent = parts[0]
    for step in range(1, blocks):
        got = shifted(jnp.stack(split(parts[step])), "nodes", blocks - step).astype(f32)
        sent = sent + got[0] + got[1]
    edge_share = scatter(dot(edge_dpre, state_weight))
    own_total = lax.dynamic_slice_in_dim(edge_total, feat * width, width, axis=1)
    edge_grad = (own_total + edge_share).astype(bf16)

    got_high, got_low = split(dot_cols(take, edge_dpre))
    home = dot(node_dpre, node_in_weight[:, :features])
    home = home + dot(got_high, receiver_weight) + dot(got_low, receiver_weight)
    sent_high, sent_low = split(sent)
    home = home + dot(sent_high, sender_weight) + dot(sent_low, sender_weight)
    node_grad = (node_cot.astype(f32) + scatter(home)).astype(bf16)
    return (edge_next, node_next, edge_grad, node_grad)


def solution(mesh):
    rows = P(("groups", "nodes"), "feat")
    flat = P(("groups", "nodes"))
    matrix = P("feat", None)
    vector = P("feat")
    return jax.shard_map(
        shards,
        mesh=mesh,
        in_specs=(
            rows,
            rows,
            P("groups", None, None),
            flat,
            flat,
            matrix,
            matrix,
            vector,
            matrix,
            matrix,
            vector,
            rows,
            rows,
        ),
        out_specs=(rows, rows, rows, rows),
        check_vma=False,
    )
```

```python
import functools

import jax
import jax.numpy as jnp
from jax import lax
from jax.experimental import pallas as pl
from jax.experimental.pallas import tpu as pltpu
from jax.sharding import PartitionSpec as P

epsilon = 1e-05
f32 = jnp.float32
bf16 = jnp.bfloat16
cores = 2


def dot(left, right):
    return jnp.dot(left, right, preferred_element_type=f32)


def dot_rows(left, right):
    return lax.dot_general(left, right, (((1,), (1,)), ((), ())), preferred_element_type=f32)


def dot_cols(left, right):
    return lax.dot_general(left, right, (((0,), (0,)), ((), ())), preferred_element_type=f32)


def split(values):
    high = values.astype(bf16)
    return high, (values - high.astype(f32)).astype(bf16)


def sigmoid(values):
    return 1.0 / (1.0 + jnp.exp(-values))


def swish_slope(pre_act):
    sigma = sigmoid(pre_act)
    return sigma * (1.0 + pre_act * (1.0 - sigma))


def normalize(values):
    mean = jnp.mean(values, axis=1, keepdims=True)
    square = jnp.mean(values * values, axis=1, keepdims=True)
    inverse = lax.rsqrt(square - mean * mean + epsilon)
    return (values - mean) * inverse, inverse


def norm_back(grad, normed, inverse):
    total = jnp.mean(grad, axis=1, keepdims=True)
    cross = jnp.mean(grad * normed, axis=1, keepdims=True)
    return inverse * (grad - total - normed * cross)


def to_hidden(rows, mine, other):
    return jnp.concatenate([dot_rows(rows, mine), dot_rows(rows, other)], axis=1)


def from_hidden(hidden, mine, other):
    half = mine.shape[0]
    return dot(hidden[:, :half], mine) + dot(hidden[:, half:], other)


def place():
    feat = lax.axis_index("feat")
    return feat // cores, feat % cores


def pair(mine, other, core):
    return jnp.where(core == 0, jnp.concatenate([mine, other], 1), jnp.concatenate([other, mine], 1))


def lanes(group, width):
    return pl.ds(pl.multiple_of(group * width, width), width)


def put_groups(full_ref, parts):
    group, _ = place()
    width = parts[0].shape[1]
    for step, part in enumerate(parts):
        full_ref[:, lanes(group ^ step, width)] = part[...]


def stage(kernel, outs, operands, scalars=0, flops=1 << 24):
    specs = [pl.BlockSpec(memory_space=pltpu.VMEM)] * (len(operands) - scalars)
    specs += [pl.BlockSpec(memory_space=pltpu.SMEM)] * scalars
    moved = sum(o.size * o.dtype.itemsize for o in operands)
    return pl.pallas_call(
        kernel,
        out_shape=[jax.ShapeDtypeStruct(shape, kind) for shape, kind in outs],
        in_specs=specs,
        out_specs=[pl.BlockSpec(memory_space=pltpu.VMEM)] * len(outs),
        cost_estimate=pl.CostEstimate(flops=flops, bytes_accessed=moved, transcendentals=0),
    )(*operands)


def merge_inputs(latent, latent2, state, state2, edge_cot, node_cot, gain_e, gain_n, pack, extra):
    _, core = place()
    nodes = latent.shape[0]
    half = state.shape[0] // cores
    mine = pl.ds(pl.multiple_of(core * half, half), half)
    theirs = pl.ds(pl.multiple_of((1 - core) * half, half), half)
    pack[:nodes] = pair(latent[...], latent2[...], core)
    pack[nodes:] = pair(state[mine], state2[mine], core)
    extra[:half] = edge_cot[theirs]
    extra[half : half + nodes] = node_cot[...]
    extra[half + nodes :] = gains(gain_e, gain_n, nodes)


def gains(gain_e, gain_n, rows):
    shape = (rows, gain_e.shape[1])
    row = lax.broadcasted_iota(jnp.int32, shape, 0)
    e = jnp.broadcast_to(gain_e[...].astype(f32), shape)
    n = jnp.broadcast_to(gain_n[...].astype(f32), shape)
    return jnp.where(row == 0, e, n).astype(bf16)


def lend_rows(groups, *refs):
    packs, (mine, other, full, lent) = refs[:groups], refs[groups:]
    put_groups(full, packs)
    features = full.shape[1]
    nodes = lent.shape[0] // 2
    sender = slice(features, 2 * features)
    high, low = split(to_hidden(full[:nodes], mine[:, sender], other[:, sender]))
    lent[:nodes] = high
    lent[nodes:] = low


def start_edges(
    full, mine, other, extra2, edge_cot, node_cot, gain_e, gain_n, slot, receiver, send_rows, pre, pick, take, extra
):
    _, core = place()
    block = lax.axis_index("nodes")
    features = full.shape[1]
    nodes, half = take.shape
    blocks, _, slots = send_rows.shape

    own = pl.ds(pl.multiple_of(core * half, half), half)
    my_extra = jnp.concatenate(
        [edge_cot[own], node_cot[...], gains(gain_e, gain_n, nodes)], axis=0
    )
    extra[...] = pair(my_extra, extra2[...], core)

    slot_row = slot[pl.ds(core, 1)]
    sender = slot_row
    for source in range(blocks):
        for k in range(slots):
            row = (source ^ block) * nodes + send_rows[source, block, k]
            sender = jnp.where(slot_row == nodes + source * slots + k, row, sender)
    table = pick.shape[0]
    pick[...] = (lax.broadcasted_iota(jnp.int32, (table, half), 0) == sender).astype(f32).astype(bf16)
    here = receiver[pl.ds(core, 1)]
    take_rows = (lax.broadcasted_iota(jnp.int32, (nodes, half), 0) == here).astype(f32).astype(bf16)
    take[...] = take_rows

    last = slice(2 * features, 3 * features)
    high, low = split(to_hidden(full[:nodes], mine[:, last], other[:, last]))
    state = full[nodes:]
    pre[...] = (
        to_hidden(state, mine[:, :features], other[:, :features])
        + dot_cols(take_rows, high)
        + dot_cols(take_rows, low)
    )


def finish_edges(blocks, *refs):
    tables, (pre, pick, mine, other, edge_pre, part, sent) = refs[:blocks], refs[blocks:]
    nodes = tables[0].shape[0] // 2
    high = jnp.concatenate([t[:nodes] for t in tables], axis=0)
    low = jnp.concatenate([t[nodes:] for t in tables], axis=0)
    value = pre[...] + dot_cols(pick[...], high) + dot_cols(pick[...], low)
    edge_pre[...] = value
    out = from_hidden((value * sigmoid(value)).astype(bf16), mine[...], other[...])
    part[...] = out
    sent[...] = out.astype(bf16)


def total(refs):
    value = refs[0][...]
    for ref in refs[1:]:
        value = value + ref[...].astype(f32)
    return value


def update_edges(groups, *refs):
    parts, extras = refs[:groups], refs[groups : 2 * groups]
    full, take, normed, inverse, kept, lent, aggregate, extra, next_all = refs[2 * groups :]
    group, core = place()
    put_groups(extra, extras)
    nodes, half = take.shape
    width = kept.shape[1]
    normed_rows, inverse_rows = normalize(total(parts))
    normed[...] = normed_rows
    inverse[...] = inverse_rows
    gain = extra[half + nodes :].astype(f32)[0:1]
    rows = (full[nodes:].astype(f32) + normed_rows * gain).astype(bf16)
    aggregate[...] = dot(take[...], rows)
    next_all[...] = rows
    mine = next_all[:, lanes(group, width * cores)]
    kept[...] = jnp.where(core == 0, mine[:, :width], mine[:, width:])
    lent[...] = jnp.where(core == 0, mine[:, width:], mine[:, :width])


def start_nodes(aggregate, aggregate2, full, in_mine, in_other, out_mine, out_other, node_pre, part, sent):
    nodes = aggregate.shape[0]
    together = (aggregate[...] + aggregate2[...]).astype(bf16)
    rows = jnp.concatenate([full[:nodes], together], axis=1)
    pre = to_hidden(rows, in_mine[...], in_other[...])
    node_pre[...] = pre
    out = from_hidden((pre * sigmoid(pre)).astype(bf16), out_mine[...], out_other[...])
    part[...] = out
    sent[...] = out.astype(bf16)


def turn_nodes(groups, *refs):
    parts = refs[:groups]
    full, extra, node_pre, in_mine, in_other, out_mine, out_other, node_next, dpre, part, sent, next_all = refs[groups:]
    group, core = place()
    nodes, features = part.shape
    half = extra.shape[0] - 2 * nodes
    width = node_next.shape[1]
    gain = extra[half + nodes :].astype(f32)[1:2]
    normed, inverse = normalize(total(parts))
    next_all[...] = (full[:nodes].astype(f32) + normed * gain).astype(bf16)
    mine = next_all[:, lanes(group, width * cores)]
    node_next[...] = jnp.where(core == 0, mine[:, :width], mine[:, width:])
    cot = extra[half : half + nodes].astype(f32)
    dy = norm_back(cot * gain, normed, inverse).astype(bf16)
    hidden = to_hidden(dy, out_mine[...], out_other[...])
    hidden = (hidden * swish_slope(node_pre[...])).astype(bf16)
    dpre[...] = hidden
    out = from_hidden(hidden, in_mine[:, features:], in_other[:, features:])
    part[...] = out
    sent[...] = out.astype(bf16)


def turn_edges(groups, *refs):
    parts = refs[:groups]
    take, pick, extra, normed, inverse, edge_pre, node_dpre = refs[groups : groups + 7]
    e_mine, e_other, out_mine, out_other, in_mine, in_other, kept, *sents, grads = refs[groups + 7 :]
    group, _ = place()
    nodes, half = take.shape
    features = extra.shape[1]
    width = kept.shape[1]
    high, low = split(total(parts))
    edge_total = extra[:half].astype(f32) + dot_cols(take[...], high) + dot_cols(take[...], low)
    gain = extra[half + nodes :].astype(f32)[0:1]
    dy = norm_back(edge_total * gain, normed[...], inverse[...]).astype(bf16)
    hidden = to_hidden(dy, out_mine[...], out_other[...])
    dpre = (hidden * swish_slope(edge_pre[...])).astype(bf16)

    def weighted(values, first):
        columns = slice(first * features, (first + 1) * features)
        return from_hidden(values, e_mine[:, columns], e_other[:, columns])

    grads[:half] = weighted(dpre, 0)
    high, low = split(dot(pick[...], dpre))
    grads[half:] = weighted(high, 1) + weighted(low, 1)
    high, low = split(dot(take[...], dpre))
    home = weighted(high, 2) + weighted(low, 2)
    home = home + 0.5 * from_hidden(node_dpre[...], in_mine[:, :features], in_other[:, :features])
    grads[half : half + nodes] += home
    for step, sent in enumerate(sents, 1):
        sent[...] = grads[:, lanes(group ^ step, width)].astype(bf16)
    grads[:half] += edge_total
    kept[...] = grads[:, lanes(group, width)]


def add_groups(groups, *refs):
    parts, (rows, table, sent) = refs[:groups], refs[groups:]
    _, core = place()
    half, width = rows.shape
    value = total(parts)
    mine = jnp.where(core == 0, value[:, :width], value[:, width:])
    sent[...] = jnp.where(core == 0, value[:, width:], value[:, :width]).astype(bf16)
    rows[...] = mine[:half].astype(bf16)
    table[...] = mine[half:]


def add_cores(table, came, own, *sents):
    nodes = own.shape[0]
    half = came.shape[0] - table.shape[0]
    value = table[...] + came[half:].astype(f32)
    own[...] = value[:nodes]
    for step, sent in enumerate(sents, 1):
        sent[...] = value[step * nodes : (step + 1) * nodes].astype(bf16)


def assemble(next_mine, next_came, grad_mine, came, edge_next, edge_grad):
    _, core = place()
    half = next_mine.shape[0]
    mine = pl.ds(pl.multiple_of(core * half, half), half)
    theirs = pl.ds(pl.multiple_of((1 - core) * half, half), half)
    edge_next[mine] = next_mine[...]
    edge_next[theirs] = next_came[...]
    edge_grad[mine] = grad_mine[...]
    edge_grad[theirs] = came[:half]


def shards(
    latent,
    edge_state,
    send_rows,
    sender_slot,
    receiver_row,
    edge_in_weight,
    edge_out_weight,
    edge_gain,
    node_in_weight,
    node_out_weight,
    node_gain,
    edge_cot,
    node_cot,
):
    nodes, width = latent.shape
    edge_dev = edge_state.shape[0]
    half = edge_dev // cores
    blocks = send_rows.shape[0]
    feats = lax.axis_size("feat")
    groups = feats // cores
    features = width * feats
    wide = width * cores
    hidden = edge_in_weight.shape[0] * cores
    table = blocks * nodes

    def swapped(values, axis, bits):
        count = lax.axis_size(axis)
        return lax.ppermute(values, axis, [(i, i ^ bits) for i in range(count)])

    def over_cores(values):
        return swapped(values, "feat", 1)

    def over_groups(values):
        return [swapped(values, "feat", cores * step) for step in range(1, groups)]

    def over_nodes(values):
        return [swapped(values, "nodes", step) for step in range(1, blocks)]

    gain_e, gain_n = edge_gain.reshape(1, width), node_gain.reshape(1, width)
    slot_rows = sender_slot.reshape(cores, half)
    receiver_rows = receiver_row.reshape(cores, half)

    latent2, state2 = over_cores(latent), over_cores(edge_state)
    e_in = (edge_in_weight, over_cores(edge_in_weight))
    pack, extra_sent = stage(
        merge_inputs,
        [((nodes + half, wide), bf16), ((half + 2 * nodes, width), bf16)],
        [latent, latent2, edge_state, state2, edge_cot, node_cot, gain_e, gain_n],
    )
    packs = [pack] + over_groups(pack)
    extra2 = over_cores(extra_sent)
    full, lent = stage(
        functools.partial(lend_rows, groups),
        [((nodes + half, features), bf16), ((2 * nodes, hidden), bf16)],
        [*packs, *e_in],
    )
    tables = [lent] + over_nodes(lent)
    pre, pick, take, extra = stage(
        start_edges,
        [((half, hidden), f32), ((table, half), bf16), ((nodes, half), bf16), ((half + 2 * nodes, wide), bf16)],
        [full, *e_in, extra2, edge_cot, node_cot, gain_e, gain_n, slot_rows, receiver_rows, send_rows],
        scalars=1,
    )
    extras = [extra] + over_groups(extra)
    e_out = (edge_out_weight, over_cores(edge_out_weight))
    edge_pre, part, sent = stage(
        functools.partial(finish_edges, blocks),
        [((half, hidden), f32), ((half, features), f32), ((half, features), bf16)],
        [*tables, pre, pick, *e_out],
    )
    parts = [part] + over_groups(sent)
    normed, inverse, next_mine, next_sent, aggregate, extra_full, _ = stage(
        functools.partial(update_edges, groups),
        [
            ((half, features), f32),
            ((half, 1), f32),
            ((half, width), bf16),
            ((half, width), bf16),
            ((nodes, features), f32),
            ((half + 2 * nodes, features), bf16),
            ((half, features), bf16),
        ],
        [*parts, *extras, full, take],
    )
    aggregate2 = over_cores(aggregate)
    next_came = over_cores(next_sent)
    n_in = (node_in_weight, over_cores(node_in_weight))
    n_out = (node_out_weight, over_cores(node_out_weight))
    node_pre, part, sent = stage(
        start_nodes,
        [((nodes, hidden), f32), ((nodes, features), f32), ((nodes, features), bf16)],
        [aggregate, aggregate2, full, *n_in, *n_out],
    )
    parts = [part] + over_groups(sent)
    node_next, node_dpre, part, sent, _ = stage(
        functools.partial(turn_nodes, groups),
        [
            ((nodes, width), bf16),
            ((nodes, hidden), bf16),
            ((nodes, features), f32),
            ((nodes, features), bf16),
            ((nodes, features), bf16),
        ],
        [*parts, full, extra_full, node_pre, *n_in, *n_out],
    )
    parts = [part] + over_groups(sent)
    kept, *sents, _ = stage(
        functools.partial(turn_edges, groups),
        [((half + table, wide), f32)]
        + [((half + table, wide), bf16)] * (groups - 1)
        + [((half + table, features), f32)],
        [*parts, take, pick, extra_full, normed, inverse, edge_pre, node_dpre, *e_in, *e_out, *n_in],
    )
    parts = [kept] + [swapped(s, "feat", cores * k) for k, s in enumerate(sents, 1)]
    grad_mine, table_mine, sent = stage(
        functools.partial(add_groups, groups),
        [((half, width), bf16), ((table, width), f32), ((half + table, width), bf16)],
        parts,
    )
    came = over_cores(sent)
    own, *sents = stage(
        add_cores,
        [((nodes, width), f32)] + [((nodes, width), bf16)] * (blocks - 1),
        [table_mine, came],
    )
    share = own
    for step, sent in enumerate(sents, 1):
        share = share + swapped(sent, "nodes", step).astype(f32)
    edge_next, edge_grad = stage(
        assemble,
        [((edge_dev, width), bf16), ((edge_dev, width), bf16)],
        [next_mine, next_came, grad_mine, came],
    )
    node_grad = (node_cot.astype(f32) + share).astype(bf16)
    return (edge_next, node_next, edge_grad, node_grad)


def solution(mesh):
    rows = P(("groups", "nodes"), "feat")
    flat = P(("groups", "nodes"))
    matrix = P("feat", None)
    vector = P("feat")
    return jax.shard_map(
        shards,
        mesh=mesh,
        in_specs=(
            rows,
            rows,
            P("groups", None, None),
            flat,
            flat,
            matrix,
            matrix,
            vector,
            matrix,
            matrix,
            vector,
            rows,
            rows,
        ),
        out_specs=(rows, rows, rows, rows),
        check_vma=False,
    )
```

```python
import functools

import jax
import jax.numpy as jnp
from jax import lax
from jax.experimental import pallas as pl
from jax.experimental.pallas import tpu as pltpu
from jax.sharding import PartitionSpec as P

epsilon = 1e-05
f32 = jnp.float32
bf16 = jnp.bfloat16
cores = 2
kernel_vmem = 8 << 20


def dot(left, right):
    return jnp.dot(left, right, preferred_element_type=f32)


def dot_rows(left, right):
    return lax.dot_general(left, right, (((1,), (1,)), ((), ())), preferred_element_type=f32)


def dot_cols(left, right):
    return lax.dot_general(left, right, (((0,), (0,)), ((), ())), preferred_element_type=f32)


def split(values):
    high = values.astype(bf16)
    return high, (values - high.astype(f32)).astype(bf16)


def sigmoid(values):
    return 1.0 / (1.0 + jnp.exp(-values))


def swish_slope(pre_act):
    sigma = sigmoid(pre_act)
    return sigma * (1.0 + pre_act * (1.0 - sigma))


def normalize(values):
    mean = jnp.mean(values, axis=1, keepdims=True)
    square = jnp.mean(values * values, axis=1, keepdims=True)
    inverse = lax.rsqrt(square - mean * mean + epsilon)
    return (values - mean) * inverse, inverse


def norm_back(grad, normed, inverse):
    total = jnp.mean(grad, axis=1, keepdims=True)
    cross = jnp.mean(grad * normed, axis=1, keepdims=True)
    return inverse * (grad - total - normed * cross)


def to_hidden(rows, mine, other):
    return jnp.concatenate([dot_rows(rows, mine), dot_rows(rows, other)], axis=1)


def from_hidden(hidden, mine, other):
    half = mine.shape[0]
    return dot(hidden[:, :half], mine) + dot(hidden[:, half:], other)


def place():
    feat = lax.axis_index("feat")
    return feat // cores, feat % cores


def pair(mine, other, core):
    return jnp.where(core == 0, jnp.concatenate([mine, other], 1), jnp.concatenate([other, mine], 1))


def lanes(group, width):
    return pl.ds(pl.multiple_of(group * width, width), width)


def put_groups(full_ref, parts):
    group, _ = place()
    width = parts[0].shape[1]
    for step, part in enumerate(parts):
        full_ref[:, lanes(group ^ step, width)] = part[...]


def stage(kernel, outs, operands, scalars=0, flops=1 << 24):
    specs = [pl.BlockSpec(memory_space=pltpu.VMEM)] * (len(operands) - scalars)
    specs += [pl.BlockSpec(memory_space=pltpu.SMEM)] * scalars
    moved = sum(o.size * o.dtype.itemsize for o in operands)
    return pl.pallas_call(
        kernel,
        out_shape=[jax.ShapeDtypeStruct(shape, kind) for shape, kind in outs],
        in_specs=specs,
        out_specs=[pl.BlockSpec(memory_space=pltpu.VMEM)] * len(outs),
        cost_estimate=pl.CostEstimate(flops=flops, bytes_accessed=moved, transcendentals=0),
        compiler_params=pltpu.CompilerParams(vmem_limit_bytes=kernel_vmem),
    )(*operands)


def merge_inputs(latent, latent2, state, state2, edge_cot, node_cot, gain_e, gain_n, pack, extra):
    _, core = place()
    nodes = latent.shape[0]
    half = state.shape[0] // cores
    mine = pl.ds(pl.multiple_of(core * half, half), half)
    theirs = pl.ds(pl.multiple_of((1 - core) * half, half), half)
    pack[:nodes] = pair(latent[...], latent2[...], core)
    pack[nodes:] = pair(state[mine], state2[mine], core)
    extra[:half] = edge_cot[theirs]
    extra[half : half + nodes] = node_cot[...]
    extra[half + nodes :] = gains(gain_e, gain_n, nodes)


def gains(gain_e, gain_n, rows):
    shape = (rows, gain_e.shape[1])
    row = lax.broadcasted_iota(jnp.int32, shape, 0)
    e = jnp.broadcast_to(gain_e[...].astype(f32), shape)
    n = jnp.broadcast_to(gain_n[...].astype(f32), shape)
    return jnp.where(row == 0, e, n).astype(bf16)


def lend_rows(groups, *refs):
    packs, (mine, other, full, lent) = refs[:groups], refs[groups:]
    put_groups(full, packs)
    features = full.shape[1]
    nodes = lent.shape[0] // 2
    sender = slice(features, 2 * features)
    high, low = split(to_hidden(full[:nodes], mine[:, sender], other[:, sender]))
    lent[:nodes] = high
    lent[nodes:] = low


def start_edges(
    full, mine, other, extra2, edge_cot, node_cot, gain_e, gain_n, slot, receiver, send_rows, pre, pick, take, extra
):
    _, core = place()
    block = lax.axis_index("nodes")
    features = full.shape[1]
    nodes, half = take.shape
    blocks, _, slots = send_rows.shape

    own = pl.ds(pl.multiple_of(core * half, half), half)
    my_extra = jnp.concatenate(
        [edge_cot[own], node_cot[...], gains(gain_e, gain_n, nodes)], axis=0
    )
    extra[...] = pair(my_extra, extra2[...], core)

    slot_row = slot[pl.ds(core, 1)]
    sender = slot_row
    for source in range(blocks):
        for k in range(slots):
            row = (source ^ block) * nodes + send_rows[source, block, k]
            sender = jnp.where(slot_row == nodes + source * slots + k, row, sender)
    table = pick.shape[0]
    pick[...] = (lax.broadcasted_iota(jnp.int32, (table, half), 0) == sender).astype(f32).astype(bf16)
    here = receiver[pl.ds(core, 1)]
    take_rows = (lax.broadcasted_iota(jnp.int32, (nodes, half), 0) == here).astype(f32).astype(bf16)
    take[...] = take_rows

    last = slice(2 * features, 3 * features)
    high, low = split(to_hidden(full[:nodes], mine[:, last], other[:, last]))
    state = full[nodes:]
    pre[...] = (
        to_hidden(state, mine[:, :features], other[:, :features])
        + dot_cols(take_rows, high)
        + dot_cols(take_rows, low)
    )


def finish_edges(blocks, *refs):
    tables, (pre, pick, mine, other, edge_pre, part, sent) = refs[:blocks], refs[blocks:]
    nodes = tables[0].shape[0] // 2
    high = jnp.concatenate([t[:nodes] for t in tables], axis=0)
    low = jnp.concatenate([t[nodes:] for t in tables], axis=0)
    value = pre[...] + dot_cols(pick[...], high) + dot_cols(pick[...], low)
    edge_pre[...] = value
    out = from_hidden((value * sigmoid(value)).astype(bf16), mine[...], other[...])
    part[...] = out
    sent[...] = out.astype(bf16)


def total(refs):
    value = refs[0][...]
    for ref in refs[1:]:
        value = value + ref[...].astype(f32)
    return value


def update_edges(groups, *refs):
    parts, extras = refs[:groups], refs[groups : 2 * groups]
    full, take, normed, inverse, kept, lent, aggregate, extra, next_all = refs[2 * groups :]
    group, core = place()
    put_groups(extra, extras)
    nodes, half = take.shape
    width = kept.shape[1]
    normed_rows, inverse_rows = normalize(total(parts))
    normed[...] = normed_rows
    inverse[...] = inverse_rows
    gain = extra[half + nodes :].astype(f32)[0:1]
    rows = (full[nodes:].astype(f32) + normed_rows * gain).astype(bf16)
    aggregate[...] = dot(take[...], rows)
    next_all[...] = rows
    mine = next_all[:, lanes(group, width * cores)]
    kept[...] = jnp.where(core == 0, mine[:, :width], mine[:, width:])
    lent[...] = jnp.where(core == 0, mine[:, width:], mine[:, :width])


def start_nodes(aggregate, aggregate2, full, in_mine, in_other, out_mine, out_other, node_pre, part, sent):
    nodes = aggregate.shape[0]
    together = (aggregate[...] + aggregate2[...]).astype(bf16)
    rows = jnp.concatenate([full[:nodes], together], axis=1)
    pre = to_hidden(rows, in_mine[...], in_other[...])
    node_pre[...] = pre
    out = from_hidden((pre * sigmoid(pre)).astype(bf16), out_mine[...], out_other[...])
    part[...] = out
    sent[...] = out.astype(bf16)


def turn_nodes(groups, *refs):
    parts = refs[:groups]
    full, extra, node_pre, in_mine, in_other, out_mine, out_other, node_next, dpre, part, sent, next_all = refs[groups:]
    group, core = place()
    nodes, features = part.shape
    half = extra.shape[0] - 2 * nodes
    width = node_next.shape[1]
    gain = extra[half + nodes :].astype(f32)[1:2]
    normed, inverse = normalize(total(parts))
    next_all[...] = (full[:nodes].astype(f32) + normed * gain).astype(bf16)
    mine = next_all[:, lanes(group, width * cores)]
    node_next[...] = jnp.where(core == 0, mine[:, :width], mine[:, width:])
    cot = extra[half : half + nodes].astype(f32)
    dy = norm_back(cot * gain, normed, inverse).astype(bf16)
    hidden = to_hidden(dy, out_mine[...], out_other[...])
    hidden = (hidden * swish_slope(node_pre[...])).astype(bf16)
    dpre[...] = hidden
    out = from_hidden(hidden, in_mine[:, features:], in_other[:, features:])
    part[...] = out
    sent[...] = out.astype(bf16)


def turn_edges(groups, *refs):
    parts = refs[:groups]
    take, pick, extra, normed, inverse, edge_pre, node_dpre = refs[groups : groups + 7]
    e_mine, e_other, out_mine, out_other, in_mine, in_other, kept, *sents, grads = refs[groups + 7 :]
    group, _ = place()
    nodes, half = take.shape
    features = extra.shape[1]
    width = kept.shape[1]
    high, low = split(total(parts))
    edge_total = extra[:half].astype(f32) + dot_cols(take[...], high) + dot_cols(take[...], low)
    gain = extra[half + nodes :].astype(f32)[0:1]
    dy = norm_back(edge_total * gain, normed[...], inverse[...]).astype(bf16)
    hidden = to_hidden(dy, out_mine[...], out_other[...])
    dpre = (hidden * swish_slope(edge_pre[...])).astype(bf16)

    def weighted(values, first):
        columns = slice(first * features, (first + 1) * features)
        return from_hidden(values, e_mine[:, columns], e_other[:, columns])

    grads[:half] = weighted(dpre, 0)
    high, low = split(dot(pick[...], dpre))
    grads[half:] = weighted(high, 1) + weighted(low, 1)
    high, low = split(dot(take[...], dpre))
    home = weighted(high, 2) + weighted(low, 2)
    home = home + 0.5 * from_hidden(node_dpre[...], in_mine[:, :features], in_other[:, :features])
    grads[half : half + nodes] += home
    for step, sent in enumerate(sents, 1):
        sent[...] = grads[:, lanes(group ^ step, width)].astype(bf16)
    grads[:half] += edge_total
    kept[...] = grads[:, lanes(group, width)]


def add_groups(groups, *refs):
    parts, (rows, table, sent) = refs[:groups], refs[groups:]
    _, core = place()
    half, width = rows.shape
    value = total(parts)
    mine = jnp.where(core == 0, value[:, :width], value[:, width:])
    sent[...] = jnp.where(core == 0, value[:, width:], value[:, :width]).astype(bf16)
    rows[...] = mine[:half].astype(bf16)
    table[...] = mine[half:]


def add_cores(table, came, own, *sents):
    nodes = own.shape[0]
    half = came.shape[0] - table.shape[0]
    value = table[...] + came[half:].astype(f32)
    own[...] = value[:nodes]
    for step, sent in enumerate(sents, 1):
        sent[...] = value[step * nodes : (step + 1) * nodes].astype(bf16)


def assemble(next_mine, next_came, grad_mine, came, edge_next, edge_grad):
    _, core = place()
    half = next_mine.shape[0]
    mine = pl.ds(pl.multiple_of(core * half, half), half)
    theirs = pl.ds(pl.multiple_of((1 - core) * half, half), half)
    edge_next[mine] = next_mine[...]
    edge_next[theirs] = next_came[...]
    edge_grad[mine] = grad_mine[...]
    edge_grad[theirs] = came[:half]


def shards(
    latent,
    edge_state,
    send_rows,
    sender_slot,
    receiver_row,
    edge_in_weight,
    edge_out_weight,
    edge_gain,
    node_in_weight,
    node_out_weight,
    node_gain,
    edge_cot,
    node_cot,
):
    nodes, width = latent.shape
    edge_dev = edge_state.shape[0]
    half = edge_dev // cores
    blocks = send_rows.shape[0]
    feats = lax.axis_size("feat")
    groups = feats // cores
    features = width * feats
    wide = width * cores
    hidden = edge_in_weight.shape[0] * cores
    table = blocks * nodes

    def swapped(values, axis, bits):
        count = lax.axis_size(axis)
        return lax.ppermute(values, axis, [(i, i ^ bits) for i in range(count)])

    def over_cores(values):
        return swapped(values, "feat", 1)

    def over_groups(values):
        return [swapped(values, "feat", cores * step) for step in range(1, groups)]

    def over_nodes(values):
        return [swapped(values, "nodes", step) for step in range(1, blocks)]

    gain_e, gain_n = edge_gain.reshape(1, width), node_gain.reshape(1, width)
    slot_rows = sender_slot.reshape(cores, half)
    receiver_rows = receiver_row.reshape(cores, half)

    latent2, state2 = over_cores(latent), over_cores(edge_state)
    e_in = (edge_in_weight, over_cores(edge_in_weight))
    pack, extra_sent = stage(
        merge_inputs,
        [((nodes + half, wide), bf16), ((half + 2 * nodes, width), bf16)],
        [latent, latent2, edge_state, state2, edge_cot, node_cot, gain_e, gain_n],
    )
    packs = [pack] + over_groups(pack)
    extra2 = over_cores(extra_sent)
    full, lent = stage(
        functools.partial(lend_rows, groups),
        [((nodes + half, features), bf16), ((2 * nodes, hidden), bf16)],
        [*packs, *e_in],
    )
    tables = [lent] + over_nodes(lent)
    pre, pick, take, extra = stage(
        start_edges,
        [((half, hidden), f32), ((table, half), bf16), ((nodes, half), bf16), ((half + 2 * nodes, wide), bf16)],
        [full, *e_in, extra2, edge_cot, node_cot, gain_e, gain_n, slot_rows, receiver_rows, send_rows],
        scalars=1,
    )
    extras = [extra] + over_groups(extra)
    e_out = (edge_out_weight, over_cores(edge_out_weight))
    edge_pre, part, sent = stage(
        functools.partial(finish_edges, blocks),
        [((half, hidden), f32), ((half, features), f32), ((half, features), bf16)],
        [*tables, pre, pick, *e_out],
    )
    parts = [part] + over_groups(sent)
    normed, inverse, next_mine, next_sent, aggregate, extra_full, _ = stage(
        functools.partial(update_edges, groups),
        [
            ((half, features), f32),
            ((half, 1), f32),
            ((half, width), bf16),
            ((half, width), bf16),
            ((nodes, features), f32),
            ((half + 2 * nodes, features), bf16),
            ((half, features), bf16),
        ],
        [*parts, *extras, full, take],
    )
    aggregate2 = over_cores(aggregate)
    next_came = over_cores(next_sent)
    n_in = (node_in_weight, over_cores(node_in_weight))
    n_out = (node_out_weight, over_cores(node_out_weight))
    node_pre, part, sent = stage(
        start_nodes,
        [((nodes, hidden), f32), ((nodes, features), f32), ((nodes, features), bf16)],
        [aggregate, aggregate2, full, *n_in, *n_out],
    )
    parts = [part] + over_groups(sent)
    node_next, node_dpre, part, sent, _ = stage(
        functools.partial(turn_nodes, groups),
        [
            ((nodes, width), bf16),
            ((nodes, hidden), bf16),
            ((nodes, features), f32),
            ((nodes, features), bf16),
            ((nodes, features), bf16),
        ],
        [*parts, full, extra_full, node_pre, *n_in, *n_out],
    )
    parts = [part] + over_groups(sent)
    kept, *sents, _ = stage(
        functools.partial(turn_edges, groups),
        [((half + table, wide), f32)]
        + [((half + table, wide), bf16)] * (groups - 1)
        + [((half + table, features), f32)],
        [*parts, take, pick, extra_full, normed, inverse, edge_pre, node_dpre, *e_in, *e_out, *n_in],
    )
    parts = [kept] + [swapped(s, "feat", cores * k) for k, s in enumerate(sents, 1)]
    grad_mine, table_mine, sent = stage(
        functools.partial(add_groups, groups),
        [((half, width), bf16), ((table, width), f32), ((half + table, width), bf16)],
        parts,
    )
    came = over_cores(sent)
    own, *sents = stage(
        add_cores,
        [((nodes, width), f32)] + [((nodes, width), bf16)] * (blocks - 1),
        [table_mine, came],
    )
    share = own
    for step, sent in enumerate(sents, 1):
        share = share + swapped(sent, "nodes", step).astype(f32)
    edge_next, edge_grad = stage(
        assemble,
        [((edge_dev, width), bf16), ((edge_dev, width), bf16)],
        [next_mine, next_came, grad_mine, came],
    )
    node_grad = (node_cot.astype(f32) + share).astype(bf16)
    return (edge_next, node_next, edge_grad, node_grad)


def solution(mesh):
    rows = P(("groups", "nodes"), "feat")
    flat = P(("groups", "nodes"))
    matrix = P("feat", None)
    vector = P("feat")
    return jax.shard_map(
        shards,
        mesh=mesh,
        in_specs=(
            rows,
            rows,
            P("groups", None, None),
            flat,
            flat,
            matrix,
            matrix,
            vector,
            matrix,
            matrix,
            vector,
            rows,
            rows,
        ),
        out_specs=(rows, rows, rows, rows),
        check_vma=False,
    )
```

```python
import functools

import jax
import jax.numpy as jnp
from jax import lax
from jax.experimental import pallas as pl
from jax.experimental.pallas import tpu as pltpu
from jax.sharding import PartitionSpec as P

epsilon = 1e-05
f32 = jnp.float32
bf16 = jnp.bfloat16
cores = 2
kernel_vmem = 8 << 20


def dot(left, right):
    return jnp.dot(left, right, preferred_element_type=f32)


def dot_rows(left, right):
    return lax.dot_general(left, right, (((1,), (1,)), ((), ())), preferred_element_type=f32)


def dot_cols(left, right):
    return lax.dot_general(left, right, (((0,), (0,)), ((), ())), preferred_element_type=f32)


def split(values):
    high = values.astype(bf16)
    return high, (values - high.astype(f32)).astype(bf16)


def sigmoid(values):
    return 1.0 / (1.0 + jnp.exp(-values))


def swish_slope(pre_act):
    sigma = sigmoid(pre_act)
    return sigma * (1.0 + pre_act * (1.0 - sigma))


def normalize(values):
    mean = jnp.mean(values, axis=1, keepdims=True)
    square = jnp.mean(values * values, axis=1, keepdims=True)
    inverse = lax.rsqrt(square - mean * mean + epsilon)
    return (values - mean) * inverse, inverse


def norm_back(grad, normed, inverse):
    total = jnp.mean(grad, axis=1, keepdims=True)
    cross = jnp.mean(grad * normed, axis=1, keepdims=True)
    return inverse * (grad - total - normed * cross)


def place():
    feat = lax.axis_index("feat")
    return feat // cores, feat % cores


def pair(mine, other, core):
    return jnp.where(core == 0, jnp.concatenate([mine, other], 1), jnp.concatenate([other, mine], 1))


def lanes(group, width):
    return pl.ds(pl.multiple_of(group * width, width), width)


def put_groups(full_ref, parts):
    group, _ = place()
    width = parts[0].shape[1]
    for step, part in enumerate(parts):
        full_ref[:, lanes(group ^ step, width)] = part[...]


def stage(kernel, outs, operands, scalars=0, in_hbm=0, scratch=(), flops=1 << 24):
    specs = [pl.BlockSpec(memory_space=pltpu.HBM)] * in_hbm
    specs += [pl.BlockSpec(memory_space=pltpu.VMEM)] * (len(operands) - scalars - in_hbm)
    specs += [pl.BlockSpec(memory_space=pltpu.SMEM)] * scalars
    moved = sum(o.size * o.dtype.itemsize for o in operands)
    return pl.pallas_call(
        kernel,
        out_shape=[jax.ShapeDtypeStruct(shape, kind) for shape, kind in outs],
        in_specs=specs,
        out_specs=[pl.BlockSpec(memory_space=pltpu.VMEM)] * len(outs),
        scratch_shapes=scratch,
        cost_estimate=pl.CostEstimate(flops=flops, bytes_accessed=moved, transcendentals=0),
        compiler_params=pltpu.CompilerParams(vmem_limit_bytes=kernel_vmem),
    )(*operands)


def gains(gain_e, gain_n, rows):
    shape = (rows, gain_e.shape[1])
    row = lax.broadcasted_iota(jnp.int32, shape, 0)
    e = jnp.broadcast_to(gain_e[...].astype(f32), shape)
    n = jnp.broadcast_to(gain_n[...].astype(f32), shape)
    return jnp.where(row == 0, e, n).astype(bf16)


def total(refs):
    value = refs[0][...]
    for ref in refs[1:]:
        value = value + ref[...].astype(f32)
    return value


def merge_inputs(state, edge_cot, node_cot, state2, gain_e, gain_n, pack, extra, extra_sent, held, cots, node, sems):
    _, core = place()
    half = pack.shape[0]
    nodes = node.shape[0]
    mine = pl.ds(pl.multiple_of(core * half, half), half)
    theirs = pl.ds(pl.multiple_of((1 - core) * half, half), half)
    copies = [
        pltpu.make_async_copy(state.at[mine], held, sems.at[0]),
        pltpu.make_async_copy(edge_cot, cots, sems.at[1]),
        pltpu.make_async_copy(node_cot, node, sems.at[2]),
    ]
    for copy in copies:
        copy.start()
    for copy in copies:
        copy.wait()
    pack[...] = pair(held[...], state2[mine], core)
    for rows, ref in ((mine, extra), (theirs, extra_sent)):
        ref[:half] = cots[rows]
        ref[half : half + nodes] = node[...]
        ref[half + nodes :] = gains(gain_e, gain_n, nodes)


def prepare_edges(groups, *refs):
    packs = refs[:groups]
    mine, other, extra_mine, extra2, slot, receiver, send_rows, state, pre, pick, take, extra = refs[groups:]
    _, core = place()
    block = lax.axis_index("nodes")
    features = state.shape[1]
    nodes, half = take.shape
    blocks, _, slots = send_rows.shape
    put_groups(state, packs)
    extra[...] = pair(extra_mine[...], extra2[...], core)

    slot_row = slot[pl.ds(core, 1)]
    sender = block * nodes + slot_row
    for source in range(blocks):
        for k in range(slots):
            row = source * nodes + send_rows[source, block, k]
            sender = jnp.where(slot_row == nodes + source * slots + k, row, sender)
    pick[...] = (lax.broadcasted_iota(jnp.int32, pick.shape, 0) == sender).astype(f32).astype(bf16)
    here = receiver[pl.ds(core, 1)]
    take[...] = (lax.broadcasted_iota(jnp.int32, take.shape, 0) == here).astype(f32).astype(bf16)
    weight = jnp.concatenate([mine[:, :features], other[:, :features]], axis=0)
    pre[...] = dot_rows(state[...], weight)


def finish_edges(came, pre, pick, take, mine, other, out_mine, out_other, n_mine, n_other, edge_pre, part, sent, own, lat, table):
    block = lax.axis_index("nodes")
    count, nodes, width = came.shape
    rows, features = table.shape
    half, hidden = pre.shape
    feats = features // width
    for source in range(count):
        first, column = source // feats * nodes, source % feats * width
        table[first : first + nodes, column : column + width] = came[source]
    latent = table[pl.ds(pl.multiple_of(block * nodes, nodes), nodes)]
    own[...] = latent

    def weight(index):
        columns = slice(index * features, (index + 1) * features)
        return jnp.concatenate([mine[:, columns], other[:, columns]], axis=0)

    high, low = split(dot_rows(table[...], weight(1)))
    here_high, here_low = split(dot_rows(latent, weight(2)))
    chosen = jnp.concatenate([pick[...], pick[...], take[...], take[...]], axis=0)
    value = pre[...] + dot_cols(chosen, jnp.concatenate([high, low, here_high, here_low], axis=0))
    edge_pre[...] = value
    act = (value * sigmoid(value)).astype(bf16)
    out = dot(act, jnp.concatenate([out_mine[...], out_other[...]], axis=0))
    part[...] = out
    sent[:half] = out.astype(bf16)
    nodes_pre = dot_rows(latent, jnp.concatenate([n_mine[:, :features], n_other[:, :features]], axis=0))
    lat[...] = nodes_pre
    high, low = split(nodes_pre)
    sent[half:] = jnp.zeros((nodes, features), bf16)
    sent[half:, :hidden] = high
    sent[half:, hidden : 2 * hidden] = low


def update_edges(groups, *refs):
    part, lat, came, extras = refs[0], refs[1], refs[2 : groups + 1], refs[groups + 1 : 2 * groups + 1]
    state, take, normed, inverse, kept, lent, aggregate, extra, lat_all, next_all = refs[2 * groups + 1 :]
    group, core = place()
    put_groups(extra, extras)
    nodes, half = take.shape
    width = kept.shape[1]
    hidden = lat.shape[1]
    value = part[...]
    lat_all[:, :hidden] = lat[...]
    for step, ref in enumerate(came, 1):
        value = value + ref[:half].astype(f32)
        high, low = ref[half:, :hidden], ref[half:, hidden : 2 * hidden]
        lat_all[:, step * hidden : (step + 1) * hidden] = high.astype(f32) + low.astype(f32)
    normed_rows, inverse_rows = normalize(value)
    normed[...] = normed_rows
    inverse[...] = inverse_rows
    gain = extra[half + nodes :].astype(f32)[0:1]
    rows = (state[...].astype(f32) + normed_rows * gain).astype(bf16)
    aggregate[...] = dot(take[...], rows)
    next_all[...] = rows
    mine = next_all[:, lanes(group, width * cores)]
    kept[...] = jnp.where(core == 0, mine[:, :width], mine[:, width:])
    lent[...] = jnp.where(core == 0, mine[:, width:], mine[:, :width])


def turn(groups, *refs):
    far, refs = refs[: 2 * (groups - 1)], refs[2 * (groups - 1) :]
    aggregate, aggregate2, own, lat_all, extra, take, pick, normed, inverse, edge_pre = refs[:10]
    e_mine, e_other, out_mine, out_other, in_mine, in_other, n_mine, n_other = refs[10:18]
    node_next, kept, *sents, spread, next_all, grads = refs[18:]
    group, core = place()
    block = lax.axis_index("nodes")
    nodes, half = take.shape
    features = extra.shape[1]
    hidden = edge_pre.shape[1]
    wide = kept.shape[1]
    width = node_next.shape[1]
    gain_rows = extra[half + nodes :].astype(f32)
    edge_gain, node_gain = gain_rows[0:1], gain_rows[1:2]

    from_agg = jnp.concatenate(
        [in_mine[:, features:], in_other[:, features:]] + [f[:, :features] for f in far], axis=0
    )
    to_out = jnp.concatenate([n_mine[...], n_other[...]] + [f[:, features:] for f in far], axis=0)
    together = (aggregate[...] + aggregate2[...]).astype(bf16)
    pre = lat_all[...] + dot_rows(together, from_agg)
    act = (pre * sigmoid(pre)).astype(bf16)
    node_normed, node_inverse = normalize(dot(act, to_out))
    next_all[...] = (own[...].astype(f32) + node_normed * node_gain).astype(bf16)
    mine = next_all[:, lanes(group, wide)]
    node_next[...] = jnp.where(core == 0, mine[:, :width], mine[:, width:])
    cot = extra[half : half + nodes].astype(f32)
    node_dy = norm_back(cot * node_gain, node_normed, node_inverse).astype(bf16)
    node_dpre = (dot_rows(node_dy, to_out) * swish_slope(pre)).astype(bf16)
    high, low = split(dot(node_dpre, from_agg))

    taken = take[...]
    edge_total = extra[:half].astype(f32) + dot_cols(
        jnp.concatenate([taken, taken], axis=0), jnp.concatenate([high, low], axis=0)
    )
    dy = norm_back(edge_total * edge_gain, normed[...], inverse[...]).astype(bf16)
    back = dot_rows(dy, jnp.concatenate([out_mine[...], out_other[...]], axis=0))
    dpre = (back * swish_slope(edge_pre[...])).astype(bf16)

    def weight(index):
        columns = slice(index * features, (index + 1) * features)
        return jnp.concatenate([e_mine[:, columns], e_other[:, columns]], axis=0)

    def weighted(values, index):
        both = dot(jnp.concatenate(split(values), axis=0), weight(index))
        return both[: values.shape[0]] + both[values.shape[0] :]

    rows = spread.shape[0] * nodes // (features // width)
    grads[:half] = dot(dpre, weight(0))
    for step, sent in enumerate(sents, 1):
        sent[...] = grads[:half, lanes(group ^ step, wide)].astype(bf16)
    grads[:half] += edge_total
    kept[...] = grads[:half, lanes(group, wide)]
    grads[half : half + rows] = weighted(dot(pick[...], dpre), 1)
    home = weighted(dot(taken, dpre), 2)
    node_weight = jnp.concatenate([in_mine[:, :features], in_other[:, :features]], axis=0)
    home = home + 0.5 * dot(node_dpre[:, :hidden], node_weight)
    grads[pl.ds(pl.multiple_of(half + block * nodes, nodes), nodes)] += home
    feats = features // width
    for target in range(spread.shape[0]):
        first, column = half + target // feats * nodes, target % feats * width
        spread[target] = grads[first : first + nodes, column : column + width].astype(bf16)


def add_groups(groups, *refs):
    parts, (kept, sent) = refs[:groups], refs[groups:]
    _, core = place()
    width = kept.shape[1]
    value = total(parts)
    kept[...] = jnp.where(core == 0, value[:, :width], value[:, width:]).astype(bf16)
    sent[...] = jnp.where(core == 0, value[:, width:], value[:, :width]).astype(bf16)


def assemble(next_mine, next_came, grad_mine, grad_came, edge_next, edge_grad):
    _, core = place()
    half = next_mine.shape[0]
    mine = pl.ds(pl.multiple_of(core * half, half), half)
    theirs = pl.ds(pl.multiple_of((1 - core) * half, half), half)
    edge_next[mine] = next_mine[...]
    edge_next[theirs] = next_came[...]
    edge_grad[mine] = grad_mine[...]
    edge_grad[theirs] = grad_came[...]


def shards(
    latent,
    edge_state,
    send_rows,
    sender_slot,
    receiver_row,
    edge_in_weight,
    edge_out_weight,
    edge_gain,
    node_in_weight,
    node_out_weight,
    node_gain,
    edge_cot,
    node_cot,
):
    nodes, width = latent.shape
    edge_dev = edge_state.shape[0]
    half = edge_dev // cores
    blocks = send_rows.shape[0]
    feats = lax.axis_size("feat")
    groups = feats // cores
    features = width * feats
    wide = width * cores
    hidden = edge_in_weight.shape[0] * cores
    table = blocks * nodes
    everyone = ("nodes", "feat")

    def swapped(values, bits):
        return lax.ppermute(values, "feat", [(i, i ^ bits) for i in range(feats)])

    def over_cores(values):
        return swapped(values, 1)

    def over_groups(values):
        return [swapped(values, cores * step) for step in range(1, groups)]

    gain_e, gain_n = edge_gain.reshape(1, width), node_gain.reshape(1, width)
    slot_rows = sender_slot.reshape(cores, half)
    receiver_rows = receiver_row.reshape(cores, half)

    state2 = over_cores(edge_state)
    latents = lax.all_to_all(
        jnp.broadcast_to(latent[None], (blocks * feats, nodes, width)), everyone, 0, 0
    )
    e_in = (edge_in_weight, over_cores(edge_in_weight))
    e_out = (edge_out_weight, over_cores(edge_out_weight))
    n_in = (node_in_weight, over_cores(node_in_weight))
    n_out = (node_out_weight, over_cores(node_out_weight))
    pack, extra_mine, extra_sent = stage(
        merge_inputs,
        [((half, wide), bf16), ((half + 2 * nodes, width), bf16), ((half + 2 * nodes, width), bf16)],
        [edge_state, edge_cot, node_cot, state2, gain_e, gain_n],
        in_hbm=3,
        scratch=[
            pltpu.VMEM((half, width), bf16),
            pltpu.VMEM((edge_dev, width), bf16),
            pltpu.VMEM((nodes, width), bf16),
            pltpu.SemaphoreType.DMA((3,)),
        ],
    )
    packs = [pack] + over_groups(pack)
    far = []
    for came in over_groups(jnp.concatenate([node_in_weight[:, features:], node_out_weight], axis=1)):
        far += [came, over_cores(came)]
    extra2 = over_cores(extra_sent)
    state, pre, pick, take, extra = stage(
        functools.partial(prepare_edges, groups),
        [
            ((half, features), bf16),
            ((half, hidden), f32),
            ((table, half), bf16),
            ((nodes, half), bf16),
            ((half + 2 * nodes, wide), bf16),
        ],
        [*packs, *e_in, extra_mine, extra2, slot_rows, receiver_rows, send_rows],
        scalars=1,
    )
    extras = [extra] + over_groups(extra)
    edge_pre, part, sent, own, lat, _ = stage(
        finish_edges,
        [
            ((half, hidden), f32),
            ((half, features), f32),
            ((half + nodes, features), bf16),
            ((nodes, features), bf16),
            ((nodes, hidden), f32),
            ((table, features), bf16),
        ],
        [latents, pre, pick, take, *e_in, *e_out, *n_in],
    )
    normed, inverse, next_mine, next_sent, aggregate, extra_full, lat_all, _ = stage(
        functools.partial(update_edges, groups),
        [
            ((half, features), f32),
            ((half, 1), f32),
            ((half, width), bf16),
            ((half, width), bf16),
            ((nodes, features), f32),
            ((half + 2 * nodes, features), bf16),
            ((nodes, features), f32),
            ((half, features), bf16),
        ],
        [part, lat, *over_groups(sent), *extras, state, take],
    )
    aggregate2 = over_cores(aggregate)
    next_came = over_cores(next_sent)
    node_next, kept, *sents, spread, _, _ = stage(
        functools.partial(turn, groups),
        [((nodes, width), bf16), ((half, wide), f32)]
        + [((half, wide), bf16)] * (groups - 1)
        + [
            ((blocks * feats, nodes, width), bf16),
            ((nodes, features), bf16),
            ((half + table, features), f32),
        ],
        [*far, aggregate, aggregate2, own, lat_all, extra_full, take, pick, normed, inverse, edge_pre]
        + [*e_in, *e_out, *n_in, *n_out],
    )
    shares = lax.all_to_all(spread, everyone, 0, 0)
    grad_mine, grad_sent = stage(
        functools.partial(add_groups, groups),
        [((half, width), bf16), ((half, width), bf16)],
        [kept] + [swapped(s, cores * k) for k, s in enumerate(sents, 1)],
    )
    edge_next, edge_grad = stage(
        assemble,
        [((edge_dev, width), bf16), ((edge_dev, width), bf16)],
        [next_mine, next_came, grad_mine, over_cores(grad_sent)],
    )
    node_grad = (node_cot.astype(f32) + jnp.sum(shares.astype(f32), axis=0)).astype(bf16)
    return (edge_next, node_next, edge_grad, node_grad)


def solution(mesh):
    rows = P(("groups", "nodes"), "feat")
    flat = P(("groups", "nodes"))
    matrix = P("feat", None)
    vector = P("feat")
    return jax.shard_map(
        shards,
        mesh=mesh,
        in_specs=(
            rows,
            rows,
            P("groups", None, None),
            flat,
            flat,
            matrix,
            matrix,
            vector,
            matrix,
            matrix,
            vector,
            rows,
            rows,
        ),
        out_specs=(rows, rows, rows, rows),
        check_vma=False,
    )
```

```python
import functools

import jax
import jax.numpy as jnp
from jax import lax
from jax.experimental import pallas as pl
from jax.experimental.pallas import tpu as pltpu
from jax.sharding import PartitionSpec as P

epsilon = 1e-05
f32 = jnp.float32
bf16 = jnp.bfloat16
cores = 2
kernel_vmem = 8 << 20


def dot(left, right):
    return jnp.dot(left, right, preferred_element_type=f32)


def dot_rows(left, right):
    return lax.dot_general(left, right, (((1,), (1,)), ((), ())), preferred_element_type=f32)


def dot_cols(left, right):
    return lax.dot_general(left, right, (((0,), (0,)), ((), ())), preferred_element_type=f32)


def split(values):
    high = values.astype(bf16)
    return high, (values - high.astype(f32)).astype(bf16)


def sigmoid(values):
    return 1.0 / (1.0 + jnp.exp(-values))


def swish_slope(pre_act):
    sigma = sigmoid(pre_act)
    return sigma * (1.0 + pre_act * (1.0 - sigma))


def normalize(values):
    mean = jnp.mean(values, axis=1, keepdims=True)
    square = jnp.mean(values * values, axis=1, keepdims=True)
    inverse = lax.rsqrt(square - mean * mean + epsilon)
    return (values - mean) * inverse, inverse


def norm_back(grad, normed, inverse):
    total = jnp.mean(grad, axis=1, keepdims=True)
    cross = jnp.mean(grad * normed, axis=1, keepdims=True)
    return inverse * (grad - total - normed * cross)


def place():
    feat = lax.axis_index("feat")
    return feat // cores, feat % cores


def pair(mine, other, core):
    return jnp.where(core == 0, jnp.concatenate([mine, other], 1), jnp.concatenate([other, mine], 1))


def lanes(group, width):
    return pl.ds(pl.multiple_of(group * width, width), width)


def stage(kernel, outs, operands, scalars=0, in_hbm=0, scratch=(), flops=1 << 24):
    specs = [pl.BlockSpec(memory_space=pltpu.HBM)] * in_hbm
    specs += [pl.BlockSpec(memory_space=pltpu.VMEM)] * (len(operands) - scalars - in_hbm)
    specs += [pl.BlockSpec(memory_space=pltpu.SMEM)] * scalars
    moved = sum(o.size * o.dtype.itemsize for o in operands)
    return pl.pallas_call(
        kernel,
        out_shape=[jax.ShapeDtypeStruct(shape, kind) for shape, kind in outs],
        in_specs=specs,
        out_specs=[pl.BlockSpec(memory_space=pltpu.VMEM)] * len(outs),
        scratch_shapes=scratch,
        cost_estimate=pl.CostEstimate(flops=flops, bytes_accessed=moved, transcendentals=0),
        compiler_params=pltpu.CompilerParams(vmem_limit_bytes=kernel_vmem),
    )(*operands)


def gains(gain_e, gain_n, rows):
    shape = (rows, gain_e.shape[1])
    row = lax.broadcasted_iota(jnp.int32, shape, 0)
    e = jnp.broadcast_to(gain_e[...].astype(f32), shape)
    n = jnp.broadcast_to(gain_n[...].astype(f32), shape)
    return jnp.where(row == 0, e, n).astype(bf16)


def total(refs):
    value = refs[0][...]
    for ref in refs[1:]:
        value = value + ref[...].astype(f32)
    return value


def pack_inputs(state, edge_cot, node_cot, latent, gain_e, gain_n, pack, held, sems):
    edge_dev = state.shape[0]
    nodes = latent.shape[0]
    copies = [
        pltpu.make_async_copy(state, pack.at[pl.ds(0, edge_dev)], sems.at[0]),
        pltpu.make_async_copy(edge_cot, pack.at[pl.ds(edge_dev, edge_dev)], sems.at[1]),
        pltpu.make_async_copy(node_cot, pack.at[pl.ds(2 * edge_dev, nodes)], sems.at[2]),
        pltpu.make_async_copy(latent, held, sems.at[3]),
    ]
    for copy in copies:
        copy.start()
    pack[2 * edge_dev + nodes :] = gains(gain_e, gain_n, nodes)
    for copy in copies:
        copy.wait()


def spread_latent(latent, spread):
    spread[...] = jnp.broadcast_to(latent[...][None], spread.shape)


def half_rows(pack, core, half):
    first = pl.multiple_of(core * half, half)
    return [pack[pl.ds(first, half)], pack[pl.ds(cores * half + first, half)], pack[2 * cores * half :]]


def send_half(groups, *refs):
    packs, sent = refs[:groups], refs[groups]
    _, core = place()
    width = packs[0].shape[1]
    half = packs[0].shape[0] - sent.shape[0] >> 1
    for step, pack in enumerate(packs):
        sent[:, step * width : (step + 1) * width] = jnp.concatenate(half_rows(pack, 1 - core, half), axis=0)


def prepare_edges(groups, *refs):
    packs = refs[:groups]
    came, mine, other, slot, receiver, send_rows, state, pre, pick, take, extra = refs[groups:]
    group, core = place()
    block = lax.axis_index("nodes")
    features = state.shape[1]
    nodes, half = take.shape
    width = features // (groups * cores)
    blocks, _, slots = send_rows.shape
    for step, pack in enumerate(packs):
        columns = lanes(group ^ step, width * cores)
        theirs = came[:, step * width : (step + 1) * width]
        ours = half_rows(pack, core, half)
        state[:, columns] = pair(ours[0], theirs[:half], core)
        extra[:, columns] = pair(jnp.concatenate(ours[1:], axis=0), theirs[half:], core)

    slot_row = slot[pl.ds(core, 1)]
    sender = block * nodes + slot_row
    for source in range(blocks):
        for k in range(slots):
            row = source * nodes + send_rows[source, block, k]
            sender = jnp.where(slot_row == nodes + source * slots + k, row, sender)
    pick[...] = (lax.broadcasted_iota(jnp.int32, pick.shape, 0) == sender).astype(f32).astype(bf16)
    here = receiver[pl.ds(core, 1)]
    take[...] = (lax.broadcasted_iota(jnp.int32, take.shape, 0) == here).astype(f32).astype(bf16)
    weight = jnp.concatenate([mine[:, :features], other[:, :features]], axis=0)
    pre[...] = dot_rows(state[...], weight)


def finish_edges(came, pre, pick, take, mine, other, out_mine, out_other, n_mine, n_other, edge_pre, part, sent, own, lat, table):
    block = lax.axis_index("nodes")
    count, nodes, width = came.shape
    rows, features = table.shape
    half, hidden = pre.shape
    feats = features // width
    for source in range(count):
        first, column = source // feats * nodes, source % feats * width
        table[first : first + nodes, column : column + width] = came[source]
    latent = table[pl.ds(pl.multiple_of(block * nodes, nodes), nodes)]
    own[...] = latent

    def weight(index):
        columns = slice(index * features, (index + 1) * features)
        return jnp.concatenate([mine[:, columns], other[:, columns]], axis=0)

    high, low = split(dot_rows(table[...], weight(1)))
    here_high, here_low = split(dot_rows(latent, weight(2)))
    chosen = jnp.concatenate([pick[...], pick[...], take[...], take[...]], axis=0)
    value = pre[...] + dot_cols(chosen, jnp.concatenate([high, low, here_high, here_low], axis=0))
    edge_pre[...] = value
    act = (value * sigmoid(value)).astype(bf16)
    out = dot(act, jnp.concatenate([out_mine[...], out_other[...]], axis=0))
    part[...] = out
    sent[:half] = out.astype(bf16)
    nodes_pre = dot_rows(latent, jnp.concatenate([n_mine[:, :features], n_other[:, :features]], axis=0))
    lat[...] = nodes_pre
    high, low = split(nodes_pre)
    sent[half:] = jnp.zeros((nodes, features), bf16)
    sent[half:, :hidden] = high
    sent[half:, hidden : 2 * hidden] = low


def update_edges(groups, *refs):
    part, lat, came = refs[0], refs[1], refs[2 : groups + 1]
    extra, state, take, normed, inverse, kept, lent, aggregate, lat_all, next_all = refs[groups + 1 :]
    group, core = place()
    nodes, half = take.shape
    width = kept.shape[1]
    hidden = lat.shape[1]
    value = part[...]
    lat_all[:, :hidden] = lat[...]
    for step, ref in enumerate(came, 1):
        value = value + ref[:half].astype(f32)
        high, low = ref[half:, :hidden], ref[half:, hidden : 2 * hidden]
        lat_all[:, step * hidden : (step + 1) * hidden] = high.astype(f32) + low.astype(f32)
    normed_rows, inverse_rows = normalize(value)
    normed[...] = normed_rows
    inverse[...] = inverse_rows
    gain = extra[half + nodes :].astype(f32)[0:1]
    rows = (state[...].astype(f32) + normed_rows * gain).astype(bf16)
    aggregate[...] = dot(take[...], rows)
    next_all[...] = rows
    mine = next_all[:, lanes(group, width * cores)]
    kept[...] = jnp.where(core == 0, mine[:, :width], mine[:, width:])
    lent[...] = jnp.where(core == 0, mine[:, width:], mine[:, :width])


def turn(groups, *refs):
    far, refs = refs[: 2 * (groups - 1)], refs[2 * (groups - 1) :]
    aggregate, aggregate2, own, lat_all, extra, take, normed, inverse, edge_pre = refs[:9]
    e_mine, e_other, out_mine, out_other, in_mine, in_other, n_mine, n_other = refs[9:17]
    node_next, kept, *sents, dpre_ref, node_dpre_ref, next_all, grads = refs[17:]
    group, core = place()
    nodes, half = take.shape
    features = extra.shape[1]
    hidden = edge_pre.shape[1]
    wide = kept.shape[1]
    width = node_next.shape[1]
    gain_rows = extra[half + nodes :].astype(f32)
    edge_gain, node_gain = gain_rows[0:1], gain_rows[1:2]

    from_agg = jnp.concatenate(
        [in_mine[:, features:], in_other[:, features:]] + [f[:, :features] for f in far], axis=0
    )
    to_out = jnp.concatenate([n_mine[...], n_other[...]] + [f[:, features:] for f in far], axis=0)
    together = (aggregate[...] + aggregate2[...]).astype(bf16)
    pre = lat_all[...] + dot_rows(together, from_agg)
    act = (pre * sigmoid(pre)).astype(bf16)
    node_normed, node_inverse = normalize(dot(act, to_out))
    next_all[...] = (own[...].astype(f32) + node_normed * node_gain).astype(bf16)
    mine = next_all[:, lanes(group, wide)]
    node_next[...] = jnp.where(core == 0, mine[:, :width], mine[:, width:])
    cot = extra[half : half + nodes].astype(f32)
    node_dy = norm_back(cot * node_gain, node_normed, node_inverse).astype(bf16)
    node_dpre = (dot_rows(node_dy, to_out) * swish_slope(pre)).astype(bf16)
    high, low = split(dot(node_dpre, from_agg))

    taken = take[...]
    edge_total = extra[:half].astype(f32) + dot_cols(
        jnp.concatenate([taken, taken], axis=0), jnp.concatenate([high, low], axis=0)
    )
    dy = norm_back(edge_total * edge_gain, normed[...], inverse[...]).astype(bf16)
    back = dot_rows(dy, jnp.concatenate([out_mine[...], out_other[...]], axis=0))
    dpre = (back * swish_slope(edge_pre[...])).astype(bf16)

    dpre_ref[...] = dpre
    node_dpre_ref[...] = node_dpre[:, :hidden]
    grads[...] = dot(dpre, jnp.concatenate([e_mine[:, :features], e_other[:, :features]], axis=0))
    for step, sent in enumerate(sents, 1):
        sent[...] = grads[:, lanes(group ^ step, wide)].astype(bf16)
    grads[...] += edge_total
    kept[...] = grads[:, lanes(group, wide)]


def spread_nodes(dpre, node_dpre, pick, take, e_mine, e_other, in_mine, in_other, spread, grads):
    block = lax.axis_index("nodes")
    count, nodes, width = spread.shape
    features = grads.shape[1]
    feats = features // width

    def weighted(values, index):
        columns = slice(index * features, (index + 1) * features)
        weight = jnp.concatenate([e_mine[:, columns], e_other[:, columns]], axis=0)
        both = dot(jnp.concatenate(split(values), axis=0), weight)
        return both[: values.shape[0]] + both[values.shape[0] :]

    grads[...] = weighted(dot(pick[...], dpre[...]), 1)
    home = weighted(dot(take[...], dpre[...]), 2)
    node_weight = jnp.concatenate([in_mine[:, :features], in_other[:, :features]], axis=0)
    home = home + 0.5 * dot(node_dpre[...], node_weight)
    grads[pl.ds(pl.multiple_of(block * nodes, nodes), nodes)] += home
    for target in range(count):
        first, column = target // feats * nodes, target % feats * width
        spread[target] = grads[first : first + nodes, column : column + width].astype(bf16)


def add_groups(groups, *refs):
    parts, (kept, sent) = refs[:groups], refs[groups:]
    _, core = place()
    width = kept.shape[1]
    value = total(parts)
    kept[...] = jnp.where(core == 0, value[:, :width], value[:, width:]).astype(bf16)
    sent[...] = jnp.where(core == 0, value[:, width:], value[:, :width]).astype(bf16)


def assemble(next_mine, next_came, grad_mine, grad_came, edge_next, edge_grad):
    _, core = place()
    half = next_mine.shape[0]
    mine = pl.ds(pl.multiple_of(core * half, half), half)
    theirs = pl.ds(pl.multiple_of((1 - core) * half, half), half)
    edge_next[mine] = next_mine[...]
    edge_next[theirs] = next_came[...]
    edge_grad[mine] = grad_mine[...]
    edge_grad[theirs] = grad_came[...]


def shards(
    latent,
    edge_state,
    send_rows,
    sender_slot,
    receiver_row,
    edge_in_weight,
    edge_out_weight,
    edge_gain,
    node_in_weight,
    node_out_weight,
    node_gain,
    edge_cot,
    node_cot,
):
    nodes, width = latent.shape
    edge_dev = edge_state.shape[0]
    half = edge_dev // cores
    blocks = send_rows.shape[0]
    feats = lax.axis_size("feat")
    groups = feats // cores
    features = width * feats
    wide = width * cores
    hidden = edge_in_weight.shape[0] * cores
    table = blocks * nodes
    everyone = ("nodes", "feat")

    def swapped(values, bits):
        return lax.ppermute(values, "feat", [(i, i ^ bits) for i in range(feats)])

    def over_cores(values):
        return swapped(values, 1)

    def over_groups(values):
        return [swapped(values, cores * step) for step in range(1, groups)]

    gain_e, gain_n = edge_gain.reshape(1, width), node_gain.reshape(1, width)
    slot_rows = sender_slot.reshape(cores, half)
    receiver_rows = receiver_row.reshape(cores, half)

    rows = 2 * edge_dev + 2 * nodes
    pack, held = stage(
        pack_inputs,
        [((rows, width), bf16), ((nodes, width), bf16)],
        [edge_state, edge_cot, node_cot, latent, gain_e, gain_n],
        in_hbm=4,
        scratch=[pltpu.SemaphoreType.DMA((4,))],
    )
    packs = [pack] + over_groups(pack)
    (spread,) = stage(spread_latent, [((blocks * feats, nodes, width), bf16)], [held])
    latents = lax.all_to_all(spread, everyone, 0, 0)
    e_in = (edge_in_weight, over_cores(edge_in_weight))
    e_out = (edge_out_weight, over_cores(edge_out_weight))
    (sent,) = stage(
        functools.partial(send_half, groups), [((rows - 2 * half, groups * width), bf16)], packs
    )
    came = over_cores(sent)
    sent, node_in_weight, node_out_weight = lax.optimization_barrier((sent, node_in_weight, node_out_weight))
    n_in = (node_in_weight, over_cores(node_in_weight))
    n_out = (node_out_weight, over_cores(node_out_weight))
    far = []
    for weights in over_groups(jnp.concatenate([node_in_weight[:, features:], node_out_weight], axis=1)):
        far += [weights, over_cores(weights)]
    state, pre, pick, take, extra = stage(
        functools.partial(prepare_edges, groups),
        [
            ((half, features), bf16),
            ((half, hidden), f32),
            ((table, half), bf16),
            ((nodes, half), bf16),
            ((half + 2 * nodes, features), bf16),
        ],
        [*packs, came, *e_in, slot_rows, receiver_rows, send_rows],
        scalars=1,
    )
    edge_pre, part, sent, own, lat, _ = stage(
        finish_edges,
        [
            ((half, hidden), f32),
            ((half, features), f32),
            ((half + nodes, features), bf16),
            ((nodes, features), bf16),
            ((nodes, hidden), f32),
            ((table, features), bf16),
        ],
        [latents, pre, pick, take, *e_in, *e_out, *n_in],
    )
    normed, inverse, next_mine, next_sent, aggregate, lat_all, _ = stage(
        functools.partial(update_edges, groups),
        [
            ((half, features), f32),
            ((half, 1), f32),
            ((half, width), bf16),
            ((half, width), bf16),
            ((nodes, features), f32),
            ((nodes, features), f32),
            ((half, features), bf16),
        ],
        [part, lat, *over_groups(sent), extra, state, take],
    )
    aggregate2 = over_cores(aggregate)
    next_came = over_cores(next_sent)
    node_next, kept, *sents, dpre, node_dpre, _, _ = stage(
        functools.partial(turn, groups),
        [((nodes, width), bf16), ((half, wide), f32)]
        + [((half, wide), bf16)] * (groups - 1)
        + [
            ((half, hidden), bf16),
            ((nodes, hidden), bf16),
            ((nodes, features), bf16),
            ((half, features), f32),
        ],
        [*far, aggregate, aggregate2, own, lat_all, extra, take, normed, inverse, edge_pre]
        + [*e_in, *e_out, *n_in, *n_out],
    )
    sents = [swapped(s, cores * k) for k, s in enumerate(sents, 1)]
    spread, _ = stage(
        spread_nodes,
        [((blocks * feats, nodes, width), bf16), ((table, features), f32)],
        [dpre, node_dpre, pick, take, *e_in, *n_in],
    )
    shares = lax.all_to_all(spread, everyone, 0, 0)
    grad_mine, grad_sent = stage(
        functools.partial(add_groups, groups),
        [((half, width), bf16), ((half, width), bf16)],
        [kept, *sents],
    )
    edge_next, edge_grad = stage(
        assemble,
        [((edge_dev, width), bf16), ((edge_dev, width), bf16)],
        [next_mine, next_came, grad_mine, over_cores(grad_sent)],
    )
    node_grad = (node_cot.astype(f32) + jnp.sum(shares.astype(f32), axis=0)).astype(bf16)
    return (edge_next, node_next, edge_grad, node_grad)


def solution(mesh):
    rows = P(("groups", "nodes"), "feat")
    flat = P(("groups", "nodes"))
    matrix = P("feat", None)
    vector = P("feat")
    return jax.shard_map(
        shards,
        mesh=mesh,
        in_specs=(
            rows,
            rows,
            P("groups", None, None),
            flat,
            flat,
            matrix,
            matrix,
            vector,
            matrix,
            matrix,
            vector,
            rows,
            rows,
        ),
        out_specs=(rows, rows, rows, rows),
        check_vma=False,
    )
```

```python
import functools

import jax
import jax.numpy as jnp
from jax import lax
from jax.experimental import pallas as pl
from jax.experimental.pallas import tpu as pltpu
from jax.sharding import PartitionSpec as P

epsilon = 1e-05
f32 = jnp.float32
bf16 = jnp.bfloat16
cores = 2
kernel_vmem = 8 << 20


def dot(left, right):
    return jnp.dot(left, right, preferred_element_type=f32)


def dot_rows(left, right):
    return lax.dot_general(left, right, (((1,), (1,)), ((), ())), preferred_element_type=f32)


def dot_cols(left, right):
    return lax.dot_general(left, right, (((0,), (0,)), ((), ())), preferred_element_type=f32)


def split(values):
    high = values.astype(bf16)
    return high, (values - high.astype(f32)).astype(bf16)


def sigmoid(values):
    return 1.0 / (1.0 + jnp.exp(-values))


def swish_slope(pre_act):
    sigma = sigmoid(pre_act)
    return sigma * (1.0 + pre_act * (1.0 - sigma))


def normalize(values):
    mean = jnp.mean(values, axis=1, keepdims=True)
    square = jnp.mean(values * values, axis=1, keepdims=True)
    inverse = lax.rsqrt(square - mean * mean + epsilon)
    return (values - mean) * inverse, inverse


def norm_back(grad, normed, inverse):
    total = jnp.mean(grad, axis=1, keepdims=True)
    cross = jnp.mean(grad * normed, axis=1, keepdims=True)
    return inverse * (grad - total - normed * cross)


def place():
    feat = lax.axis_index("feat")
    return feat // cores, feat % cores


def pair(mine, other, core):
    return jnp.where(core == 0, jnp.concatenate([mine, other], 1), jnp.concatenate([other, mine], 1))


def lanes(group, width):
    return pl.ds(pl.multiple_of(group * width, width), width)


def stage(kernel, outs, operands, scalars=0, flops=1 << 24):
    specs = [pl.BlockSpec(memory_space=pltpu.VMEM)] * (len(operands) - scalars)
    specs += [pl.BlockSpec(memory_space=pltpu.SMEM)] * scalars
    moved = sum(o.size * o.dtype.itemsize for o in operands)
    return pl.pallas_call(
        kernel,
        out_shape=[jax.ShapeDtypeStruct(shape, kind) for shape, kind in outs],
        in_specs=specs,
        out_specs=[pl.BlockSpec(memory_space=pltpu.VMEM)] * len(outs),
        cost_estimate=pl.CostEstimate(flops=flops, bytes_accessed=moved, transcendentals=0),
        compiler_params=pltpu.CompilerParams(vmem_limit_bytes=kernel_vmem),
    )(*operands)


def gains(gain_e, gain_n, rows):
    shape = (rows, gain_e.shape[1])
    row = lax.broadcasted_iota(jnp.int32, shape, 0)
    e = jnp.broadcast_to(gain_e[...].astype(f32), shape)
    n = jnp.broadcast_to(gain_n[...].astype(f32), shape)
    return jnp.where(row == 0, e, n).astype(bf16)


def total(refs):
    value = refs[0][...]
    for ref in refs[1:]:
        value = value + ref[...].astype(f32)
    return value


def pack_extra(edge_cot, node_cot, gain_e, gain_n, pack):
    edge_dev = edge_cot.shape[0]
    nodes = node_cot.shape[0]
    pack[:edge_dev] = edge_cot[...]
    pack[edge_dev : edge_dev + nodes] = node_cot[...]
    pack[edge_dev + nodes :] = gains(gain_e, gain_n, nodes)


def half_rows(pack, core, half):
    first = pl.multiple_of(core * half, half)
    return jnp.concatenate([pack[pl.ds(first, half)], pack[cores * half :]], axis=0)


def send_half(groups, *refs):
    packs, sent = refs[:groups], refs[groups]
    _, core = place()
    width = packs[0].shape[1]
    half = packs[0].shape[0] - sent.shape[0]
    for step, pack in enumerate(packs):
        sent[:, step * width : (step + 1) * width] = half_rows(pack, 1 - core, half)


def prepare_edges(feats, *refs):
    states = refs[:feats]
    mine, other, slot, receiver, send_rows, state, pre, pick, take = refs[feats:]
    group, core = place()
    block = lax.axis_index("nodes")
    features = state.shape[1]
    nodes, half = take.shape
    blocks, _, slots = send_rows.shape
    rows = pl.ds(pl.multiple_of(core * half, half), half)
    for step in range(feats // cores):
        ours, theirs = states[cores * step][rows], states[cores * step + 1][rows]
        state[:, lanes(group ^ step, features * cores // feats)] = pair(ours, theirs, core)

    slot_row = slot[pl.ds(core, 1)]
    sender = block * nodes + slot_row
    for source in range(blocks):
        for k in range(slots):
            row = source * nodes + send_rows[source, block, k]
            sender = jnp.where(slot_row == nodes + source * slots + k, row, sender)
    pick[...] = (lax.broadcasted_iota(jnp.int32, pick.shape, 0) == sender).astype(f32).astype(bf16)
    here = receiver[pl.ds(core, 1)]
    take[...] = (lax.broadcasted_iota(jnp.int32, take.shape, 0) == here).astype(f32).astype(bf16)
    weight = jnp.concatenate([mine[:, :features], other[:, :features]], axis=0)
    pre[...] = dot_rows(state[...], weight)


def finish_edges(came, pre, pick, take, mine, other, out_mine, out_other, n_mine, n_other, edge_pre, part, sent, own, lat, table):
    block = lax.axis_index("nodes")
    count, nodes, width = came.shape
    rows, features = table.shape
    half, hidden = pre.shape
    feats = features // width
    for source in range(count):
        first, column = source // feats * nodes, source % feats * width
        table[first : first + nodes, column : column + width] = came[source]
    latent = table[pl.ds(pl.multiple_of(block * nodes, nodes), nodes)]
    own[...] = latent

    def weight(index):
        columns = slice(index * features, (index + 1) * features)
        return jnp.concatenate([mine[:, columns], other[:, columns]], axis=0)

    high, low = split(dot_rows(table[...], weight(1)))
    here_high, here_low = split(dot_rows(latent, weight(2)))
    chosen = jnp.concatenate([pick[...], pick[...], take[...], take[...]], axis=0)
    value = pre[...] + dot_cols(chosen, jnp.concatenate([high, low, here_high, here_low], axis=0))
    edge_pre[...] = value
    act = (value * sigmoid(value)).astype(bf16)
    out = dot(act, jnp.concatenate([out_mine[...], out_other[...]], axis=0))
    part[...] = out
    sent[:half] = out.astype(bf16)
    nodes_pre = dot_rows(latent, jnp.concatenate([n_mine[:, :features], n_other[:, :features]], axis=0))
    lat[...] = nodes_pre
    high, low = split(nodes_pre)
    sent[half:] = jnp.zeros((nodes, features), bf16)
    sent[half:, :hidden] = high
    sent[half:, hidden : 2 * hidden] = low


def update_edges(groups, *refs):
    part, lat, came, packs = refs[0], refs[1], refs[2 : groups + 1], refs[groups + 1 : 2 * groups + 1]
    theirs, state, take, normed, inverse, kept, lent, aggregate, lat_all, extra, next_all = refs[2 * groups + 1 :]
    group, core = place()
    nodes, half = take.shape
    width = kept.shape[1]
    hidden = lat.shape[1]
    for step, pack in enumerate(packs):
        both = pair(half_rows(pack, core, half), theirs[:, step * width : (step + 1) * width], core)
        extra[:, lanes(group ^ step, width * cores)] = both
    value = part[...]
    lat_all[:, :hidden] = lat[...]
    for step, ref in enumerate(came, 1):
        value = value + ref[:half].astype(f32)
        high, low = ref[half:, :hidden], ref[half:, hidden : 2 * hidden]
        lat_all[:, step * hidden : (step + 1) * hidden] = high.astype(f32) + low.astype(f32)
    normed_rows, inverse_rows = normalize(value)
    normed[...] = normed_rows
    inverse[...] = inverse_rows
    gain = extra[half + nodes :].astype(f32)[0:1]
    rows = (state[...].astype(f32) + normed_rows * gain).astype(bf16)
    aggregate[...] = dot(take[...], rows)
    next_all[...] = rows
    mine = next_all[:, lanes(group, width * cores)]
    kept[...] = jnp.where(core == 0, mine[:, :width], mine[:, width:])
    lent[...] = jnp.where(core == 0, mine[:, width:], mine[:, :width])


def turn(groups, *refs):
    far, refs = refs[: 2 * (groups - 1)], refs[2 * (groups - 1) :]
    aggregate, aggregate2, own, lat_all, extra, take, normed, inverse, edge_pre = refs[:9]
    e_mine, e_other, out_mine, out_other, in_mine, in_other, n_mine, n_other = refs[9:17]
    node_next, kept, *sents, dpre_ref, node_dpre_ref, next_all, grads = refs[17:]
    group, core = place()
    nodes, half = take.shape
    features = extra.shape[1]
    hidden = edge_pre.shape[1]
    wide = kept.shape[1]
    width = node_next.shape[1]
    gain_rows = extra[half + nodes :].astype(f32)
    edge_gain, node_gain = gain_rows[0:1], gain_rows[1:2]

    from_agg = jnp.concatenate(
        [in_mine[:, features:], in_other[:, features:]] + [f[:, :features] for f in far], axis=0
    )
    to_out = jnp.concatenate([n_mine[...], n_other[...]] + [f[:, features:] for f in far], axis=0)
    together = (aggregate[...] + aggregate2[...]).astype(bf16)
    pre = lat_all[...] + dot_rows(together, from_agg)
    act = (pre * sigmoid(pre)).astype(bf16)
    node_normed, node_inverse = normalize(dot(act, to_out))
    next_all[...] = (own[...].astype(f32) + node_normed * node_gain).astype(bf16)
    mine = next_all[:, lanes(group, wide)]
    node_next[...] = jnp.where(core == 0, mine[:, :width], mine[:, width:])
    cot = extra[half : half + nodes].astype(f32)
    node_dy = norm_back(cot * node_gain, node_normed, node_inverse).astype(bf16)
    node_dpre = (dot_rows(node_dy, to_out) * swish_slope(pre)).astype(bf16)
    high, low = split(dot(node_dpre, from_agg))

    taken = take[...]
    edge_total = extra[:half].astype(f32) + dot_cols(
        jnp.concatenate([taken, taken], axis=0), jnp.concatenate([high, low], axis=0)
    )
    dy = norm_back(edge_total * edge_gain, normed[...], inverse[...]).astype(bf16)
    back = dot_rows(dy, jnp.concatenate([out_mine[...], out_other[...]], axis=0))
    dpre = (back * swish_slope(edge_pre[...])).astype(bf16)

    dpre_ref[...] = dpre
    node_dpre_ref[...] = node_dpre[:, :hidden]
    grads[...] = dot(dpre, jnp.concatenate([e_mine[:, :features], e_other[:, :features]], axis=0))
    for step, sent in enumerate(sents, 1):
        sent[...] = grads[:, lanes(group ^ step, wide)].astype(bf16)
    grads[...] += edge_total
    kept[...] = grads[:, lanes(group, wide)]


def spread_nodes(dpre, node_dpre, pick, take, e_mine, e_other, in_mine, in_other, spread, grads):
    block = lax.axis_index("nodes")
    count, nodes, width = spread.shape
    features = grads.shape[1]
    feats = features // width

    def weighted(values, index):
        columns = slice(index * features, (index + 1) * features)
        weight = jnp.concatenate([e_mine[:, columns], e_other[:, columns]], axis=0)
        both = dot(jnp.concatenate(split(values), axis=0), weight)
        return both[: values.shape[0]] + both[values.shape[0] :]

    grads[...] = weighted(dot(pick[...], dpre[...]), 1)
    home = weighted(dot(take[...], dpre[...]), 2)
    node_weight = jnp.concatenate([in_mine[:, :features], in_other[:, :features]], axis=0)
    home = home + 0.5 * dot(node_dpre[...], node_weight)
    grads[pl.ds(pl.multiple_of(block * nodes, nodes), nodes)] += home
    for target in range(count):
        first, column = target // feats * nodes, target % feats * width
        spread[target] = grads[first : first + nodes, column : column + width].astype(bf16)


def add_groups(groups, *refs):
    parts, (kept, sent) = refs[:groups], refs[groups:]
    _, core = place()
    width = kept.shape[1]
    value = total(parts)
    kept[...] = jnp.where(core == 0, value[:, :width], value[:, width:]).astype(bf16)
    sent[...] = jnp.where(core == 0, value[:, width:], value[:, :width]).astype(bf16)


def add_nodes(shares, node_cot, node_grad):
    value = node_cot[...].astype(f32)
    for source in range(shares.shape[0]):
        value = value + shares[source].astype(f32)
    node_grad[...] = value.astype(bf16)


def assemble(next_mine, next_came, grad_mine, grad_came, edge_next, edge_grad):
    _, core = place()
    half = next_mine.shape[0]
    mine = pl.ds(pl.multiple_of(core * half, half), half)
    theirs = pl.ds(pl.multiple_of((1 - core) * half, half), half)
    edge_next[mine] = next_mine[...]
    edge_next[theirs] = next_came[...]
    edge_grad[mine] = grad_mine[...]
    edge_grad[theirs] = grad_came[...]


def shards(
    latent,
    edge_state,
    send_rows,
    sender_slot,
    receiver_row,
    edge_in_weight,
    edge_out_weight,
    edge_gain,
    node_in_weight,
    node_out_weight,
    node_gain,
    edge_cot,
    node_cot,
):
    nodes, width = latent.shape
    edge_dev = edge_state.shape[0]
    half = edge_dev // cores
    blocks = send_rows.shape[0]
    feats = lax.axis_size("feat")
    groups = feats // cores
    features = width * feats
    wide = width * cores
    hidden = edge_in_weight.shape[0] * cores
    table = blocks * nodes
    everyone = ("nodes", "feat")

    def swapped(values, bits):
        return lax.ppermute(values, "feat", [(i, i ^ bits) for i in range(feats)])

    def over_cores(values):
        return swapped(values, 1)

    def over_groups(values):
        return [swapped(values, cores * step) for step in range(1, groups)]

    gain_e, gain_n = edge_gain.reshape(1, width), node_gain.reshape(1, width)
    slot_rows = sender_slot.reshape(cores, half)
    receiver_rows = receiver_row.reshape(cores, half)

    latents = lax.all_to_all(
        jnp.broadcast_to(latent[None], (blocks * feats, nodes, width)), everyone, 0, 0
    )
    states = [edge_state] + [swapped(edge_state, step) for step in range(1, feats)]
    e_in = (edge_in_weight, over_cores(edge_in_weight))
    state, pre, pick, take = stage(
        functools.partial(prepare_edges, feats),
        [((half, features), bf16), ((half, hidden), f32), ((table, half), bf16), ((nodes, half), bf16)],
        [*states, *e_in, slot_rows, receiver_rows, send_rows],
        scalars=1,
    )
    pre, node_in_weight, node_out_weight, edge_out_weight, edge_cot = lax.optimization_barrier(
        (pre, node_in_weight, node_out_weight, edge_out_weight, edge_cot)
    )
    e_out = (edge_out_weight, over_cores(edge_out_weight))
    far = []
    for weights in over_groups(jnp.concatenate([node_in_weight[:, features:], node_out_weight], axis=1)):
        far += [weights, over_cores(weights)]
    rows = edge_dev + 2 * nodes
    (pack,) = stage(pack_extra, [((rows, width), bf16)], [edge_cot, node_cot, gain_e, gain_n])
    packs = [pack] + over_groups(pack)
    (sent,) = stage(functools.partial(send_half, groups), [((rows - half, groups * width), bf16)], packs)
    extra_came = over_cores(sent)
    n_in = (node_in_weight, over_cores(node_in_weight))
    n_out = (node_out_weight, over_cores(node_out_weight))
    edge_pre, part, sent, own, lat, _ = stage(
        finish_edges,
        [
            ((half, hidden), f32),
            ((half, features), f32),
            ((half + nodes, features), bf16),
            ((nodes, features), bf16),
            ((nodes, hidden), f32),
            ((table, features), bf16),
        ],
        [latents, pre, pick, take, *e_in, *e_out, *n_in],
    )
    normed, inverse, next_mine, next_sent, aggregate, lat_all, extra, _ = stage(
        functools.partial(update_edges, groups),
        [
            ((half, features), f32),
            ((half, 1), f32),
            ((half, width), bf16),
            ((half, width), bf16),
            ((nodes, features), f32),
            ((nodes, features), f32),
            ((half + 2 * nodes, features), bf16),
            ((half, features), bf16),
        ],
        [part, lat, *over_groups(sent), *packs, extra_came, state, take],
    )
    aggregate2 = over_cores(aggregate)
    next_came = over_cores(next_sent)
    node_next, kept, *sents, dpre, node_dpre, _, _ = stage(
        functools.partial(turn, groups),
        [((nodes, width), bf16), ((half, wide), f32)]
        + [((half, wide), bf16)] * (groups - 1)
        + [
            ((half, hidden), bf16),
            ((nodes, hidden), bf16),
            ((nodes, features), bf16),
            ((half, features), f32),
        ],
        [*far, aggregate, aggregate2, own, lat_all, extra, take, normed, inverse, edge_pre]
        + [*e_in, *e_out, *n_in, *n_out],
    )
    sents = [swapped(s, cores * k) for k, s in enumerate(sents, 1)]
    spread, _ = stage(
        spread_nodes,
        [((blocks * feats, nodes, width), bf16), ((table, features), f32)],
        [dpre, node_dpre, pick, take, *e_in, *n_in],
    )
    shares = lax.all_to_all(spread, everyone, 0, 0)
    grad_mine, grad_sent = stage(
        functools.partial(add_groups, groups),
        [((half, width), bf16), ((half, width), bf16)],
        [kept, *sents],
    )
    edge_next, edge_grad = stage(
        assemble,
        [((edge_dev, width), bf16), ((edge_dev, width), bf16)],
        [next_mine, next_came, grad_mine, over_cores(grad_sent)],
    )
    (node_grad,) = stage(add_nodes, [((nodes, width), bf16)], [shares, node_cot])
    return (edge_next, node_next, edge_grad, node_grad)


def solution(mesh):
    rows = P(("groups", "nodes"), "feat")
    flat = P(("groups", "nodes"))
    matrix = P("feat", None)
    vector = P("feat")
    return jax.shard_map(
        shards,
        mesh=mesh,
        in_specs=(
            rows,
            rows,
            P("groups", None, None),
            flat,
            flat,
            matrix,
            matrix,
            vector,
            matrix,
            matrix,
            vector,
            rows,
            rows,
        ),
        out_specs=(rows, rows, rows, rows),
        check_vma=False,
    )
```

```python
import functools

import jax
import jax.numpy as jnp
from jax import lax
from jax.experimental import pallas as pl
from jax.experimental.pallas import tpu as pltpu
from jax.sharding import PartitionSpec as P

epsilon = 1e-05
f32 = jnp.float32
bf16 = jnp.bfloat16
cores = 2
kernel_vmem = 8 << 20


def dot(left, right):
    return jnp.dot(left, right, preferred_element_type=f32)


def dot_rows(left, right):
    return lax.dot_general(left, right, (((1,), (1,)), ((), ())), preferred_element_type=f32)


def dot_cols(left, right):
    return lax.dot_general(left, right, (((0,), (0,)), ((), ())), preferred_element_type=f32)


def split(values):
    high = values.astype(bf16)
    return high, (values - high.astype(f32)).astype(bf16)


def sigmoid(values):
    return 1.0 / (1.0 + jnp.exp(-values))


def swish_slope(pre_act):
    sigma = sigmoid(pre_act)
    return sigma * (1.0 + pre_act * (1.0 - sigma))


def normalize(values):
    mean = jnp.mean(values, axis=1, keepdims=True)
    square = jnp.mean(values * values, axis=1, keepdims=True)
    inverse = lax.rsqrt(square - mean * mean + epsilon)
    return (values - mean) * inverse, inverse


def norm_back(grad, normed, inverse):
    total = jnp.mean(grad, axis=1, keepdims=True)
    cross = jnp.mean(grad * normed, axis=1, keepdims=True)
    return inverse * (grad - total - normed * cross)


def place():
    feat = lax.axis_index("feat")
    return feat // cores, feat % cores


def pair(mine, other, core):
    return jnp.where(core == 0, jnp.concatenate([mine, other], 1), jnp.concatenate([other, mine], 1))


def lanes(group, width):
    return pl.ds(pl.multiple_of(group * width, width), width)


def stage(kernel, outs, operands, scalars=0, scratch=(), flops=1 << 24):
    specs = [pl.BlockSpec(memory_space=pltpu.VMEM)] * (len(operands) - scalars)
    specs += [pl.BlockSpec(memory_space=pltpu.SMEM)] * scalars
    moved = sum(o.size * o.dtype.itemsize for o in operands)
    return pl.pallas_call(
        kernel,
        out_shape=[jax.ShapeDtypeStruct(shape, kind) for shape, kind in outs],
        in_specs=specs,
        out_specs=[pl.BlockSpec(memory_space=pltpu.VMEM)] * len(outs),
        scratch_shapes=[pltpu.VMEM(shape, kind) for shape, kind in scratch],
        cost_estimate=pl.CostEstimate(flops=flops, bytes_accessed=moved, transcendentals=0),
        compiler_params=pltpu.CompilerParams(vmem_limit_bytes=kernel_vmem),
    )(*operands)


def gains(gain_e, gain_n, rows):
    shape = (rows, gain_e.shape[1])
    row = lax.broadcasted_iota(jnp.int32, shape, 0)
    e = jnp.broadcast_to(gain_e[...].astype(f32), shape)
    n = jnp.broadcast_to(gain_n[...].astype(f32), shape)
    return jnp.where(row == 0, e, n).astype(bf16)


def total(refs):
    value = refs[0][...]
    for ref in refs[1:]:
        value = value + ref[...].astype(f32)
    return value


def pack_extra(edge_cot, node_cot, pack):
    edge_dev = edge_cot.shape[0]
    nodes = node_cot.shape[0]
    pack[:edge_dev] = edge_cot[...]
    pack[edge_dev:] = node_cot[...]


def join_weights(edge_in, edge_out, node_in, node_out, wall, far):
    features = node_out.shape[1]
    wall[:, : 3 * features] = edge_in[...]
    wall[:, 3 * features : 4 * features] = edge_out[...]
    wall[:, 4 * features : 6 * features] = node_in[...]
    wall[:, 6 * features :] = node_out[...]
    far[:, :features] = node_in[:, features:]
    far[:, features:] = node_out[...]


def chip_weights(walls, index, features):
    return jnp.concatenate([wall[:, index * features : (index + 1) * features] for wall in walls], axis=0)


def half_rows(pack, core, half):
    rows = pack[pl.ds(pl.multiple_of(core * half, half), half)]
    if pack.shape[0] == cores * half:
        return rows
    return jnp.concatenate([rows, pack[cores * half :]], axis=0)


def stack_tables(*refs):
    *parts, gain_e, gain_n, table = refs
    nodes = parts[0].shape[0]
    table[...] = jnp.concatenate([part[...] for part in parts] + [gains(gain_e, gain_n, nodes)], axis=0)


def join_groups(*refs):
    *parts, joined = refs
    joined[...] = jnp.concatenate([part[...] for part in parts], axis=1)


def send_half(groups, *refs):
    packs, sent = refs[:groups], refs[groups]
    _, core = place()
    width = packs[0].shape[1]
    half = packs[0].shape[0] - sent.shape[0] if packs[0].shape[0] < cores * sent.shape[0] else sent.shape[0]
    for step, pack in enumerate(packs):
        sent[:, step * width : (step + 1) * width] = half_rows(pack, 1 - core, half)


def prepare_edges(groups, *refs):
    packs = refs[:groups]
    theirs, *walls, slot, receiver, send_rows, state, pre, pick, take = refs[groups:]
    group, core = place()
    block = lax.axis_index("nodes")
    features = state.shape[1]
    nodes, half = take.shape
    width = packs[0].shape[1]
    blocks, _, slots = send_rows.shape
    for step, pack in enumerate(packs):
        both = pair(half_rows(pack, core, half), theirs[:, step * width : (step + 1) * width], core)
        state[:, lanes(group ^ step, width * cores)] = both

    slot_row = slot[pl.ds(core, 1)]
    sender = slot_row
    for source in range(blocks):
        for k in range(slots):
            row = (source ^ block) * nodes + send_rows[source, block, k]
            sender = jnp.where(slot_row == nodes + source * slots + k, row, sender)
    pick[...] = (lax.broadcasted_iota(jnp.int32, pick.shape, 0) == sender).astype(f32).astype(bf16)
    here = receiver[pl.ds(core, 1)]
    take[...] = (lax.broadcasted_iota(jnp.int32, take.shape, 0) == here).astype(f32).astype(bf16)
    pre[...] = dot_rows(state[...], chip_weights(walls, 0, features))


def finish_edges(groups, *refs):
    tables = refs[:groups]
    theirs, pre, pick, take, *walls, edge_pre, part, sent, own, lat, gain, table = refs[groups:]
    group, core = place()
    features = table.shape[1]
    nodes = own.shape[0]
    half, hidden = pre.shape
    width = tables[0].shape[1]
    for step, ours in enumerate(tables):
        both = pair(ours[...], theirs[:, step * width : (step + 1) * width], core)
        table[:, lanes(group ^ step, cores * width)] = both
    latent = table[:nodes]
    own[...] = latent
    count = table.shape[0] - nodes
    gain[...] = table[count:]

    def weight(index):
        return chip_weights(walls, index, features)

    high, low = split(dot_rows(table[:count], weight(1)))
    here_high, here_low = split(dot_rows(latent, weight(2)))
    chosen = jnp.concatenate([pick[...], pick[...], take[...], take[...]], axis=0)
    value = pre[...] + dot_cols(chosen, jnp.concatenate([high, low, here_high, here_low], axis=0))
    edge_pre[...] = value
    act = (value * sigmoid(value)).astype(bf16)
    out = dot(act, weight(3))
    part[...] = out
    sent[:half] = out.astype(bf16)
    nodes_pre = dot_rows(latent, weight(4))
    lat[...] = nodes_pre
    high, low = split(nodes_pre)
    sent[half:] = jnp.zeros((nodes, features), bf16)
    sent[half:, :hidden] = high
    sent[half:, hidden : 2 * hidden] = low


def update_edges(groups, *refs):
    part, lat, came = refs[0], refs[1], refs[2 : groups + 1]
    gain, state, take, normed, inverse, kept, lent, aggregate, lat_all, next_all = refs[groups + 1 :]
    group, core = place()
    nodes, half = take.shape
    width = kept.shape[1]
    hidden = lat.shape[1]
    value = part[...]
    lat_all[:, :hidden] = lat[...]
    for step, ref in enumerate(came, 1):
        value = value + ref[:half].astype(f32)
        high, low = ref[half:, :hidden], ref[half:, hidden : 2 * hidden]
        lat_all[:, step * hidden : (step + 1) * hidden] = high.astype(f32) + low.astype(f32)
    normed_rows, inverse_rows = normalize(value)
    normed[...] = normed_rows
    inverse[...] = inverse_rows
    rows = (state[...].astype(f32) + normed_rows * gain[...].astype(f32)[0:1]).astype(bf16)
    aggregate[...] = dot(take[...], rows)
    next_all[...] = rows
    mine = next_all[:, lanes(group, width * cores)]
    kept[...] = jnp.where(core == 0, mine[:, :width], mine[:, width:])
    lent[...] = jnp.where(core == 0, mine[:, width:], mine[:, :width])


def turn(groups, *refs):
    far, refs = refs[: 2 * (groups - 1)], refs[2 * (groups - 1) :]
    packs, refs = refs[:groups], refs[groups:]
    theirs, aggregate, aggregate2, own, lat_all, gain, take, normed, inverse, edge_pre = refs[:10]
    walls = refs[10:12]
    node_next, kept, *sents, dpre_ref, node_dpre_ref, next_all, grads, extra = refs[12:]
    group, core = place()
    nodes, half = take.shape
    features = gain.shape[1]
    hidden = edge_pre.shape[1]
    wide = kept.shape[1]
    width = node_next.shape[1]
    gain_rows = gain[...].astype(f32)
    edge_gain, node_gain = gain_rows[0:1], gain_rows[1:2]
    for step, pack in enumerate(packs):
        both = pair(half_rows(pack, core, half), theirs[:, step * width : (step + 1) * width], core)
        extra[:, lanes(group ^ step, wide)] = both

    from_agg = jnp.concatenate([chip_weights(walls, 5, features)] + [f[:, :features] for f in far], axis=0)
    to_out = jnp.concatenate([chip_weights(walls, 6, features)] + [f[:, features:] for f in far], axis=0)
    together = (aggregate[...] + aggregate2[...]).astype(bf16)
    pre = lat_all[...] + dot_rows(together, from_agg)
    act = (pre * sigmoid(pre)).astype(bf16)
    node_normed, node_inverse = normalize(dot(act, to_out))
    next_all[...] = (own[...].astype(f32) + node_normed * node_gain).astype(bf16)
    mine = next_all[:, lanes(group, wide)]
    node_next[...] = jnp.where(core == 0, mine[:, :width], mine[:, width:])
    cot = extra[half:].astype(f32)
    node_dy = norm_back(cot * node_gain, node_normed, node_inverse).astype(bf16)
    node_dpre = (dot_rows(node_dy, to_out) * swish_slope(pre)).astype(bf16)
    high, low = split(dot(node_dpre, from_agg))

    taken = take[...]
    edge_total = extra[:half].astype(f32) + dot_cols(
        jnp.concatenate([taken, taken], axis=0), jnp.concatenate([high, low], axis=0)
    )
    dy = norm_back(edge_total * edge_gain, normed[...], inverse[...]).astype(bf16)
    back = dot_rows(dy, chip_weights(walls, 3, features))
    dpre = (back * swish_slope(edge_pre[...])).astype(bf16)

    dpre_ref[...] = dpre
    node_dpre_ref[...] = node_dpre[:, :hidden]
    grads[...] = dot(dpre, chip_weights(walls, 0, features))
    for step, sent in enumerate(sents, 1):
        sent[...] = grads[:, lanes(group ^ step, wide)].astype(bf16)
    grads[...] += edge_total
    kept[...] = grads[:, lanes(group, wide)]


def spread_nodes(dpre, node_dpre, pick, take, *refs):
    *walls, spread, grads = refs
    block = lax.axis_index("nodes")
    count, nodes, width = spread.shape
    features = grads.shape[1]
    feats = features // width

    def weighted(values, index):
        both = dot(jnp.concatenate(split(values), axis=0), chip_weights(walls, index, features))
        return both[: values.shape[0]] + both[values.shape[0] :]

    grads[...] = weighted(dot(pick[...], dpre[...]), 1)
    home = weighted(dot(take[...], dpre[...]), 2)
    home = home + 0.5 * dot(node_dpre[...], chip_weights(walls, 4, features))
    grads[:nodes] += home
    for target in range(count):
        first = pl.multiple_of((target // feats ^ block) * nodes, nodes)
        column = target % feats * width
        spread[target] = grads[pl.ds(first, nodes), column : column + width].astype(bf16)


def add_groups(groups, *refs):
    parts, (kept, sent) = refs[:groups], refs[groups:]
    _, core = place()
    width = kept.shape[1]
    value = total(parts)
    kept[...] = jnp.where(core == 0, value[:, :width], value[:, width:]).astype(bf16)
    sent[...] = jnp.where(core == 0, value[:, width:], value[:, :width]).astype(bf16)


def add_nodes(shares, node_cot, node_grad):
    value = node_cot[...].astype(f32)
    for source in range(shares.shape[0]):
        value = value + shares[source].astype(f32)
    node_grad[...] = value.astype(bf16)


def assemble(next_mine, next_came, grad_mine, grad_came, edge_next, edge_grad):
    _, core = place()
    half = next_mine.shape[0]
    mine = pl.ds(pl.multiple_of(core * half, half), half)
    theirs = pl.ds(pl.multiple_of((1 - core) * half, half), half)
    edge_next[mine] = next_mine[...]
    edge_next[theirs] = next_came[...]
    edge_grad[mine] = grad_mine[...]
    edge_grad[theirs] = grad_came[...]


def shards(
    latent,
    edge_state,
    send_rows,
    sender_slot,
    receiver_row,
    edge_in_weight,
    edge_out_weight,
    edge_gain,
    node_in_weight,
    node_out_weight,
    node_gain,
    edge_cot,
    node_cot,
):
    nodes, width = latent.shape
    edge_dev = edge_state.shape[0]
    half = edge_dev // cores
    blocks = send_rows.shape[0]
    feats = lax.axis_size("feat")
    groups = feats // cores
    features = width * feats
    wide = width * cores
    hidden = edge_in_weight.shape[0] * cores
    table = blocks * nodes
    everyone = ("nodes", "feat")

    def swapped(values, bits):
        return lax.ppermute(values, "feat", [(i, i ^ bits) for i in range(feats)])

    def over_cores(values):
        return swapped(values, 1)

    def over_groups(values):
        return [swapped(values, cores * step) for step in range(1, groups)]

    gain_e, gain_n = edge_gain.reshape(1, width), node_gain.reshape(1, width)
    slot_rows = sender_slot.reshape(cores, half)
    receiver_rows = receiver_row.reshape(cores, half)

    def over_nodes(values, step):
        return lax.ppermute(values, "nodes", [(i, i ^ step) for i in range(blocks)])

    hid = edge_in_weight.shape[0]
    tables = [over_nodes(latent, step) for step in range(1, blocks)]
    states = over_groups(edge_state)
    wall, far = stage(
        join_weights,
        [((hid, 7 * features), bf16), ((hid, 2 * features), bf16)],
        [edge_in_weight, edge_out_weight, node_in_weight, node_out_weight],
    )
    far = over_groups(far)
    walls = [wall, over_cores(wall)]
    tables, states = lax.optimization_barrier((tables, states))
    (mine,) = stage(stack_tables, [((table + nodes, width), bf16)], [latent, *tables, gain_e, gain_n])
    tables = [mine] + over_groups(mine)
    states = [edge_state] + states
    (sent,) = stage(functools.partial(send_half, groups), [((half, groups * width), bf16)], states)
    state, pre, pick, take = stage(
        functools.partial(prepare_edges, groups),
        [((half, features), bf16), ((half, hidden), f32), ((table, half), bf16), ((nodes, half), bf16)],
        [*states, over_cores(sent), *walls, slot_rows, receiver_rows, send_rows],
        scalars=1,
    )
    (joined,) = stage(join_groups, [((table + nodes, groups * width), bf16)], tables)
    edge_pre, part, sent, own, lat, gain = stage(
        functools.partial(finish_edges, groups),
        [
            ((half, hidden), f32),
            ((half, features), f32),
            ((half + nodes, features), bf16),
            ((nodes, features), bf16),
            ((nodes, hidden), f32),
            ((nodes, features), bf16),
        ],
        [*tables, over_cores(joined), pre, pick, take, *walls],
        scratch=[((table + nodes, features), bf16)],
    )
    sent, edge_cot, far = lax.optimization_barrier((sent, edge_cot, far))
    far = [weights for came in far for weights in (came, over_cores(came))]
    (pack,) = stage(pack_extra, [((edge_dev + nodes, width), bf16)], [edge_cot, node_cot])
    packs = [pack] + over_groups(pack)
    (extra_sent,) = stage(
        functools.partial(send_half, groups), [((half + nodes, groups * width), bf16)], packs
    )
    extra_came = over_cores(extra_sent)
    normed, inverse, next_mine, next_sent, aggregate, lat_all = stage(
        functools.partial(update_edges, groups),
        [
            ((half, features), f32),
            ((half, 1), f32),
            ((half, width), bf16),
            ((half, width), bf16),
            ((nodes, features), f32),
            ((nodes, features), f32),
        ],
        [part, lat, *over_groups(sent), gain, state, take],
        scratch=[((half, features), bf16)],
    )
    aggregate2 = over_cores(aggregate)
    next_came = over_cores(next_sent)
    node_next, kept, *sents, dpre, node_dpre = stage(
        functools.partial(turn, groups),
        [((nodes, width), bf16), ((half, wide), f32)]
        + [((half, wide), bf16)] * (groups - 1)
        + [((half, hidden), bf16), ((nodes, hidden), bf16)],
        [*far, *packs, extra_came, aggregate, aggregate2, own, lat_all, gain, take, normed, inverse, edge_pre]
        + walls,
        scratch=[((nodes, features), bf16), ((half, features), f32), ((half + nodes, features), bf16)],
    )
    sents = [swapped(s, cores * k) for k, s in enumerate(sents, 1)]
    (spread,) = stage(
        spread_nodes,
        [((blocks * feats, nodes, width), bf16)],
        [dpre, node_dpre, pick, take, *walls],
        scratch=[((table, features), f32)],
    )
    shares = lax.all_to_all(spread, everyone, 0, 0)
    grad_mine, grad_sent = stage(
        functools.partial(add_groups, groups),
        [((half, width), bf16), ((half, width), bf16)],
        [kept, *sents],
    )
    edge_next, edge_grad = stage(
        assemble,
        [((edge_dev, width), bf16), ((edge_dev, width), bf16)],
        [next_mine, next_came, grad_mine, over_cores(grad_sent)],
    )
    (node_grad,) = stage(add_nodes, [((nodes, width), bf16)], [shares, node_cot])
    return (edge_next, node_next, edge_grad, node_grad)


def solution(mesh):
    rows = P(("groups", "nodes"), "feat")
    flat = P(("groups", "nodes"))
    matrix = P("feat", None)
    vector = P("feat")
    return jax.shard_map(
        shards,
        mesh=mesh,
        in_specs=(
            rows,
            rows,
            P("groups", None, None),
            flat,
            flat,
            matrix,
            matrix,
            vector,
            matrix,
            matrix,
            vector,
            rows,
            rows,
        ),
        out_specs=(rows, rows, rows, rows),
        check_vma=False,
    )
```

```python
import functools

import jax
import jax.numpy as jnp
from jax import lax
from jax.experimental import pallas as pl
from jax.experimental.pallas import tpu as pltpu
from jax.sharding import PartitionSpec as P

epsilon = 1e-05
f32 = jnp.float32
bf16 = jnp.bfloat16
cores = 2
kernel_vmem = 8 << 20


def dot(left, right):
    return jnp.dot(left, right, preferred_element_type=f32)


def dot_rows(left, right):
    return lax.dot_general(left, right, (((1,), (1,)), ((), ())), preferred_element_type=f32)


def dot_cols(left, right):
    return lax.dot_general(left, right, (((0,), (0,)), ((), ())), preferred_element_type=f32)


def split(values):
    high = values.astype(bf16)
    return high, (values - high.astype(f32)).astype(bf16)


def sigmoid(values):
    return 1.0 / (1.0 + jnp.exp(-values))


def swish_slope(pre_act):
    sigma = sigmoid(pre_act)
    return sigma * (1.0 + pre_act * (1.0 - sigma))


def normalize(values):
    mean = jnp.mean(values, axis=1, keepdims=True)
    square = jnp.mean(values * values, axis=1, keepdims=True)
    inverse = lax.rsqrt(square - mean * mean + epsilon)
    return (values - mean) * inverse, inverse


def norm_back(grad, normed, inverse):
    total = jnp.mean(grad, axis=1, keepdims=True)
    cross = jnp.mean(grad * normed, axis=1, keepdims=True)
    return inverse * (grad - total - normed * cross)


def place():
    feat = lax.axis_index("feat")
    return feat // cores, feat % cores


def pair(mine, other, core):
    return jnp.where(core == 0, jnp.concatenate([mine, other], 1), jnp.concatenate([other, mine], 1))


def lanes(group, width):
    return pl.ds(pl.multiple_of(group * width, width), width)


def stage(kernel, outs, operands, scalars=0, scratch=(), flops=1 << 24):
    specs = [pl.BlockSpec(memory_space=pltpu.VMEM)] * (len(operands) - scalars)
    specs += [pl.BlockSpec(memory_space=pltpu.SMEM)] * scalars
    moved = sum(o.size * o.dtype.itemsize for o in operands)
    return pl.pallas_call(
        kernel,
        out_shape=[jax.ShapeDtypeStruct(shape, kind) for shape, kind in outs],
        in_specs=specs,
        out_specs=[pl.BlockSpec(memory_space=pltpu.VMEM)] * len(outs),
        scratch_shapes=[pltpu.VMEM(shape, kind) for shape, kind in scratch],
        cost_estimate=pl.CostEstimate(flops=flops, bytes_accessed=moved, transcendentals=0),
        compiler_params=pltpu.CompilerParams(vmem_limit_bytes=kernel_vmem),
    )(*operands)


def gains(gain_e, gain_n, rows):
    shape = (rows, gain_e.shape[1])
    row = lax.broadcasted_iota(jnp.int32, shape, 0)
    e = jnp.broadcast_to(gain_e[...].astype(f32), shape)
    n = jnp.broadcast_to(gain_n[...].astype(f32), shape)
    return jnp.where(row == 0, e, n).astype(bf16)


def total(refs):
    value = refs[0][...]
    for ref in refs[1:]:
        value = value + ref[...].astype(f32)
    return value


def spread_inputs(latent, node_cot, gain_e, gain_n, spread):
    nodes = latent.shape[0]
    rows = jnp.concatenate([latent[...], node_cot[...], gains(gain_e, gain_n, nodes)], axis=0)
    spread[...] = jnp.broadcast_to(rows[None], spread.shape)


def half_rows(pack, core, half):
    first = pl.multiple_of(core * half, half)
    return pack[pl.ds(first, half)], pack[pl.ds(cores * half + first, half)]


def send_half(groups, *refs):
    packs, sent = refs[:groups], refs[groups]
    _, core = place()
    width = packs[0].shape[1]
    half = sent.shape[0] // 2
    for step, pack in enumerate(packs):
        columns = slice(step * width, (step + 1) * width)
        sent[:half, columns], sent[half:, columns] = half_rows(pack, 1 - core, half)


def prepare_edges(groups, *refs):
    packs = refs[:groups]
    theirs, mine, other, slot, receiver, send_rows, state, cot, pre, pick, take = refs[groups:]
    group, core = place()
    block = lax.axis_index("nodes")
    features = state.shape[1]
    nodes, half = take.shape
    width = packs[0].shape[1]
    blocks, _, slots = send_rows.shape
    for step, pack in enumerate(packs):
        columns = slice(step * width, (step + 1) * width)
        wide = lanes(group ^ step, width * cores)
        my_state, my_cot = half_rows(pack, core, half)
        state[:, wide] = pair(my_state, theirs[:half, columns], core)
        cot[:, wide] = pair(my_cot, theirs[half:, columns], core)

    slot_row = slot[pl.ds(core, 1)]
    sender = block * nodes + slot_row
    for source in range(blocks):
        for k in range(slots):
            row = source * nodes + send_rows[source, block, k]
            sender = jnp.where(slot_row == nodes + source * slots + k, row, sender)
    pick[...] = (lax.broadcasted_iota(jnp.int32, pick.shape, 0) == sender).astype(f32).astype(bf16)
    here = receiver[pl.ds(core, 1)]
    take[...] = (lax.broadcasted_iota(jnp.int32, take.shape, 0) == here).astype(f32).astype(bf16)
    weight = jnp.concatenate([mine[:, :features], other[:, :features]], axis=0)
    pre[...] = dot_rows(state[...], weight)


def finish_edges(came, pre, pick, take, *refs):
    mine, other, out_mine, out_other, n_mine, n_other, edge_pre, part, sent, own, node_cot, gain, lat, table = refs
    block = lax.axis_index("nodes")
    count, _, width = came.shape
    features = table.shape[1]
    nodes = own.shape[0]
    half, hidden = pre.shape
    feats = features // width
    for source in range(count):
        first, column = source // feats * nodes, source % feats * width
        table[first : first + nodes, column : column + width] = came[source, :nodes]
    for feat in range(feats):
        columns = slice(feat * width, (feat + 1) * width)
        here = came[block * feats + feat]
        own[:, columns] = here[:nodes]
        node_cot[:, columns] = here[nodes : 2 * nodes]
        gain[:, columns] = here[2 * nodes :]
    latent = own[...]

    def weight(index):
        columns = slice(index * features, (index + 1) * features)
        return jnp.concatenate([mine[:, columns], other[:, columns]], axis=0)

    high, low = split(dot_rows(table[...], weight(1)))
    here_high, here_low = split(dot_rows(latent, weight(2)))
    chosen = jnp.concatenate([pick[...], pick[...], take[...], take[...]], axis=0)
    value = pre[...] + dot_cols(chosen, jnp.concatenate([high, low, here_high, here_low], axis=0))
    edge_pre[...] = value
    act = (value * sigmoid(value)).astype(bf16)
    out = dot(act, jnp.concatenate([out_mine[...], out_other[...]], axis=0))
    part[...] = out
    sent[:half] = out.astype(bf16)
    nodes_pre = dot_rows(latent, jnp.concatenate([n_mine[:, :features], n_other[:, :features]], axis=0))
    lat[...] = nodes_pre
    high, low = split(nodes_pre)
    sent[half:] = jnp.zeros((nodes, features), bf16)
    sent[half:, :hidden] = high
    sent[half:, hidden : 2 * hidden] = low


def update_edges(groups, *refs):
    part, lat, came = refs[0], refs[1], refs[2 : groups + 1]
    gain, state, take, normed, inverse, kept, lent, aggregate, lat_all, next_all = refs[groups + 1 :]
    group, core = place()
    nodes, half = take.shape
    width = kept.shape[1]
    hidden = lat.shape[1]
    value = part[...]
    lat_all[:, :hidden] = lat[...]
    for step, ref in enumerate(came, 1):
        value = value + ref[:half].astype(f32)
        high, low = ref[half:, :hidden], ref[half:, hidden : 2 * hidden]
        lat_all[:, step * hidden : (step + 1) * hidden] = high.astype(f32) + low.astype(f32)
    normed_rows, inverse_rows = normalize(value)
    normed[...] = normed_rows
    inverse[...] = inverse_rows
    rows = (state[...].astype(f32) + normed_rows * gain[...].astype(f32)[0:1]).astype(bf16)
    aggregate[...] = dot(take[...], rows)
    next_all[...] = rows
    mine = next_all[:, lanes(group, width * cores)]
    kept[...] = jnp.where(core == 0, mine[:, :width], mine[:, width:])
    lent[...] = jnp.where(core == 0, mine[:, width:], mine[:, :width])


def turn(groups, *refs):
    far, refs = refs[: 2 * (groups - 1)], refs[2 * (groups - 1) :]
    aggregate, aggregate2, own, lat_all, gain, node_cot, edge_cot, take, normed, inverse, edge_pre = refs[:11]
    e_mine, e_other, out_mine, out_other, in_mine, in_other, n_mine, n_other = refs[11:19]
    node_next, kept, *sents, dpre_ref, node_dpre_ref, next_all, grads = refs[19:]
    group, core = place()
    nodes, half = take.shape
    features = gain.shape[1]
    hidden = edge_pre.shape[1]
    wide = kept.shape[1]
    width = node_next.shape[1]
    gain_rows = gain[...].astype(f32)
    edge_gain, node_gain = gain_rows[0:1], gain_rows[1:2]

    from_agg = jnp.concatenate(
        [in_mine[:, features:], in_other[:, features:]] + [f[:, :features] for f in far], axis=0
    )
    to_out = jnp.concatenate([n_mine[...], n_other[...]] + [f[:, features:] for f in far], axis=0)
    together = (aggregate[...] + aggregate2[...]).astype(bf16)
    pre = lat_all[...] + dot_rows(together, from_agg)
    act = (pre * sigmoid(pre)).astype(bf16)
    node_normed, node_inverse = normalize(dot(act, to_out))
    next_all[...] = (own[...].astype(f32) + node_normed * node_gain).astype(bf16)
    mine = next_all[:, lanes(group, wide)]
    node_next[...] = jnp.where(core == 0, mine[:, :width], mine[:, width:])
    node_dy = norm_back(node_cot[...].astype(f32) * node_gain, node_normed, node_inverse).astype(bf16)
    node_dpre = (dot_rows(node_dy, to_out) * swish_slope(pre)).astype(bf16)
    high, low = split(dot(node_dpre, from_agg))

    taken = take[...]
    edge_total = edge_cot[...].astype(f32) + dot_cols(
        jnp.concatenate([taken, taken], axis=0), jnp.concatenate([high, low], axis=0)
    )
    dy = norm_back(edge_total * edge_gain, normed[...], inverse[...]).astype(bf16)
    back = dot_rows(dy, jnp.concatenate([out_mine[...], out_other[...]], axis=0))
    dpre = (back * swish_slope(edge_pre[...])).astype(bf16)

    dpre_ref[...] = dpre
    node_dpre_ref[...] = node_dpre[:, :hidden]
    grads[...] = dot(dpre, jnp.concatenate([e_mine[:, :features], e_other[:, :features]], axis=0))
    for step, sent in enumerate(sents, 1):
        sent[...] = grads[:, lanes(group ^ step, wide)].astype(bf16)
    grads[...] += edge_total
    kept[...] = grads[:, lanes(group, wide)]


def spread_nodes(dpre, node_dpre, pick, take, e_mine, e_other, in_mine, in_other, spread, grads):
    block = lax.axis_index("nodes")
    count, nodes, width = spread.shape
    features = grads.shape[1]
    feats = features // width

    def weighted(values, index):
        columns = slice(index * features, (index + 1) * features)
        weight = jnp.concatenate([e_mine[:, columns], e_other[:, columns]], axis=0)
        both = dot(jnp.concatenate(split(values), axis=0), weight)
        return both[: values.shape[0]] + both[values.shape[0] :]

    grads[...] = weighted(dot(pick[...], dpre[...]), 1)
    home = weighted(dot(take[...], dpre[...]), 2)
    node_weight = jnp.concatenate([in_mine[:, :features], in_other[:, :features]], axis=0)
    home = home + 0.5 * dot(node_dpre[...], node_weight)
    grads[pl.ds(pl.multiple_of(block * nodes, nodes), nodes)] += home
    for target in range(count):
        first, column = target // feats * nodes, target % feats * width
        spread[target] = grads[first : first + nodes, column : column + width].astype(bf16)


def add_groups(groups, *refs):
    parts, (kept, sent) = refs[:groups], refs[groups:]
    _, core = place()
    width = kept.shape[1]
    value = total(parts)
    kept[...] = jnp.where(core == 0, value[:, :width], value[:, width:]).astype(bf16)
    sent[...] = jnp.where(core == 0, value[:, width:], value[:, :width]).astype(bf16)


def add_nodes(shares, node_cot, node_grad):
    value = node_cot[...].astype(f32)
    for source in range(shares.shape[0]):
        value = value + shares[source].astype(f32)
    node_grad[...] = value.astype(bf16)


def assemble(next_mine, next_came, grad_mine, grad_came, edge_next, edge_grad):
    _, core = place()
    half = next_mine.shape[0]
    mine = pl.ds(pl.multiple_of(core * half, half), half)
    theirs = pl.ds(pl.multiple_of((1 - core) * half, half), half)
    edge_next[mine] = next_mine[...]
    edge_next[theirs] = next_came[...]
    edge_grad[mine] = grad_mine[...]
    edge_grad[theirs] = grad_came[...]


def shards(
    latent,
    edge_state,
    send_rows,
    sender_slot,
    receiver_row,
    edge_in_weight,
    edge_out_weight,
    edge_gain,
    node_in_weight,
    node_out_weight,
    node_gain,
    edge_cot,
    node_cot,
):
    nodes, width = latent.shape
    edge_dev = edge_state.shape[0]
    half = edge_dev // cores
    blocks = send_rows.shape[0]
    feats = lax.axis_size("feat")
    groups = feats // cores
    features = width * feats
    wide = width * cores
    hidden = edge_in_weight.shape[0] * cores
    table = blocks * nodes
    everyone = ("nodes", "feat")

    def swapped(values, bits):
        return lax.ppermute(values, "feat", [(i, i ^ bits) for i in range(feats)])

    def over_cores(values):
        return swapped(values, 1)

    def over_groups(values):
        return [swapped(values, cores * step) for step in range(1, groups)]

    gain_e, gain_n = edge_gain.reshape(1, width), node_gain.reshape(1, width)
    slot_rows = sender_slot.reshape(cores, half)
    receiver_rows = receiver_row.reshape(cores, half)

    far = []
    for weights in over_groups(jnp.concatenate([node_in_weight[:, features:], node_out_weight], axis=1)):
        far += [weights, over_cores(weights)]
    e_in = (edge_in_weight, over_cores(edge_in_weight))
    e_out = (edge_out_weight, over_cores(edge_out_weight))
    n_in = (node_in_weight, over_cores(node_in_weight))
    n_out = (node_out_weight, over_cores(node_out_weight))
    pack = jnp.concatenate([edge_state, edge_cot])
    packs = [pack] + over_groups(pack)
    (spread,) = stage(
        spread_inputs, [((blocks * feats, 3 * nodes, width), bf16)], [latent, node_cot, gain_e, gain_n]
    )
    came = lax.all_to_all(spread, everyone, 0, 0)
    (sent,) = stage(functools.partial(send_half, groups), [((edge_dev, groups * width), bf16)], packs)
    state, cot, pre, pick, take = stage(
        functools.partial(prepare_edges, groups),
        [
            ((half, features), bf16),
            ((half, features), bf16),
            ((half, hidden), f32),
            ((table, half), bf16),
            ((nodes, half), bf16),
        ],
        [*packs, over_cores(sent), *e_in, slot_rows, receiver_rows, send_rows],
        scalars=1,
    )
    edge_pre, part, sent, own, full_node_cot, gain, lat = stage(
        finish_edges,
        [
            ((half, hidden), f32),
            ((half, features), f32),
            ((half + nodes, features), bf16),
            ((nodes, features), bf16),
            ((nodes, features), bf16),
            ((nodes, features), bf16),
            ((nodes, hidden), f32),
        ],
        [came, pre, pick, take, *e_in, *e_out, *n_in],
        scratch=[((table, features), bf16)],
    )
    normed, inverse, next_mine, next_sent, aggregate, lat_all = stage(
        functools.partial(update_edges, groups),
        [
            ((half, features), f32),
            ((half, 1), f32),
            ((half, width), bf16),
            ((half, width), bf16),
            ((nodes, features), f32),
            ((nodes, features), f32),
        ],
        [part, lat, *over_groups(sent), gain, state, take],
        scratch=[((half, features), bf16)],
    )
    aggregate2 = over_cores(aggregate)
    next_came = over_cores(next_sent)
    node_next, kept, *sents, dpre, node_dpre = stage(
        functools.partial(turn, groups),
        [((nodes, width), bf16), ((half, wide), f32)]
        + [((half, wide), bf16)] * (groups - 1)
        + [((half, hidden), bf16), ((nodes, hidden), bf16)],
        [*far, aggregate, aggregate2, own, lat_all, gain, full_node_cot, cot, take, normed, inverse, edge_pre]
        + [*e_in, *e_out, *n_in, *n_out],
        scratch=[((nodes, features), bf16), ((half, features), f32)],
    )
    sents = [swapped(s, cores * k) for k, s in enumerate(sents, 1)]
    (spread,) = stage(
        spread_nodes,
        [((blocks * feats, nodes, width), bf16)],
        [dpre, node_dpre, pick, take, *e_in, *n_in],
        scratch=[((table, features), f32)],
    )
    shares = lax.all_to_all(spread, everyone, 0, 0)
    grad_mine, grad_sent = stage(
        functools.partial(add_groups, groups),
        [((half, width), bf16), ((half, width), bf16)],
        [kept, *sents],
    )
    edge_next, edge_grad = stage(
        assemble,
        [((edge_dev, width), bf16), ((edge_dev, width), bf16)],
        [next_mine, next_came, grad_mine, over_cores(grad_sent)],
    )
    (node_grad,) = stage(add_nodes, [((nodes, width), bf16)], [shares, node_cot])
    return (edge_next, node_next, edge_grad, node_grad)


def solution(mesh):
    rows = P(("groups", "nodes"), "feat")
    flat = P(("groups", "nodes"))
    matrix = P("feat", None)
    vector = P("feat")
    return jax.shard_map(
        shards,
        mesh=mesh,
        in_specs=(
            rows,
            rows,
            P("groups", None, None),
            flat,
            flat,
            matrix,
            matrix,
            vector,
            matrix,
            matrix,
            vector,
            rows,
            rows,
        ),
        out_specs=(rows, rows, rows, rows),
        check_vma=False,
    )
```

```python
import functools

import jax
import jax.numpy as jnp
from jax import lax
from jax.experimental import pallas as pl
from jax.experimental.pallas import tpu as pltpu
from jax.sharding import PartitionSpec as P

epsilon = 1e-05
f32 = jnp.float32
bf16 = jnp.bfloat16
cores = 2
kernel_vmem = 8 << 20


def dot(left, right):
    return jnp.dot(left, right, preferred_element_type=f32)


def dot_rows(left, right):
    return lax.dot_general(left, right, (((1,), (1,)), ((), ())), preferred_element_type=f32)


def dot_cols(left, right):
    return lax.dot_general(left, right, (((0,), (0,)), ((), ())), preferred_element_type=f32)


def split(values):
    high = values.astype(bf16)
    return high, (values - high.astype(f32)).astype(bf16)


def sigmoid(values):
    return 1.0 / (1.0 + jnp.exp(-values))


def swish_slope(pre_act):
    sigma = sigmoid(pre_act)
    return sigma * (1.0 + pre_act * (1.0 - sigma))


def normalize(values):
    mean = jnp.mean(values, axis=1, keepdims=True)
    square = jnp.mean(values * values, axis=1, keepdims=True)
    inverse = lax.rsqrt(square - mean * mean + epsilon)
    return (values - mean) * inverse, inverse


def norm_back(grad, normed, inverse):
    total = jnp.mean(grad, axis=1, keepdims=True)
    cross = jnp.mean(grad * normed, axis=1, keepdims=True)
    return inverse * (grad - total - normed * cross)


def place():
    feat = lax.axis_index("feat")
    return feat // cores, feat % cores


def pair(mine, other, core):
    return jnp.where(core == 0, jnp.concatenate([mine, other], 1), jnp.concatenate([other, mine], 1))


def lanes(group, width):
    return pl.ds(pl.multiple_of(group * width, width), width)


def stage(kernel, outs, operands, scalars=0, scratch=(), flops=1 << 24):
    specs = [pl.BlockSpec(memory_space=pltpu.VMEM)] * (len(operands) - scalars)
    specs += [pl.BlockSpec(memory_space=pltpu.SMEM)] * scalars
    moved = sum(o.size * o.dtype.itemsize for o in operands)
    return pl.pallas_call(
        kernel,
        out_shape=[jax.ShapeDtypeStruct(shape, kind) for shape, kind in outs],
        in_specs=specs,
        out_specs=[pl.BlockSpec(memory_space=pltpu.VMEM)] * len(outs),
        scratch_shapes=[pltpu.VMEM(shape, kind) for shape, kind in scratch],
        cost_estimate=pl.CostEstimate(flops=flops, bytes_accessed=moved, transcendentals=0),
        compiler_params=pltpu.CompilerParams(vmem_limit_bytes=kernel_vmem),
    )(*operands)


def gains(gain_e, gain_n, rows):
    shape = (rows, gain_e.shape[1])
    row = lax.broadcasted_iota(jnp.int32, shape, 0)
    e = jnp.broadcast_to(gain_e[...].astype(f32), shape)
    n = jnp.broadcast_to(gain_n[...].astype(f32), shape)
    return jnp.where(row == 0, e, n).astype(bf16)


def total(refs):
    value = refs[0][...]
    for ref in refs[1:]:
        value = value + ref[...].astype(f32)
    return value


def pack_extra(edge_cot, node_cot, gain_e, gain_n, pack):
    edge_dev = edge_cot.shape[0]
    nodes = node_cot.shape[0]
    pack[:edge_dev] = edge_cot[...]
    pack[edge_dev : edge_dev + nodes] = node_cot[...]
    pack[edge_dev + nodes :] = gains(gain_e, gain_n, nodes)


def half_rows(pack, core, half):
    rows = pack[pl.ds(pl.multiple_of(core * half, half), half)]
    if pack.shape[0] == cores * half:
        return rows
    return jnp.concatenate([rows, pack[cores * half :]], axis=0)


def send_half(groups, *refs):
    packs, sent = refs[:groups], refs[groups]
    _, core = place()
    width = packs[0].shape[1]
    half = packs[0].shape[0] - sent.shape[0]
    for step, pack in enumerate(packs):
        sent[:, step * width : (step + 1) * width] = half_rows(pack, 1 - core, half)


def prepare_edges(groups, *refs):
    packs = refs[:groups]
    theirs, mine, other, slot, receiver, send_rows, state, pre, pick, take = refs[groups:]
    group, core = place()
    block = lax.axis_index("nodes")
    features = state.shape[1]
    nodes, half = take.shape
    width = packs[0].shape[1]
    blocks, _, slots = send_rows.shape
    for step, pack in enumerate(packs):
        both = pair(half_rows(pack, core, half), theirs[:, step * width : (step + 1) * width], core)
        state[:, lanes(group ^ step, width * cores)] = both

    slot_row = slot[pl.ds(core, 1)]
    sender = block * nodes + slot_row
    for source in range(blocks):
        for k in range(slots):
            row = source * nodes + send_rows[source, block, k]
            sender = jnp.where(slot_row == nodes + source * slots + k, row, sender)
    pick[...] = (lax.broadcasted_iota(jnp.int32, pick.shape, 0) == sender).astype(f32).astype(bf16)
    here = receiver[pl.ds(core, 1)]
    take[...] = (lax.broadcasted_iota(jnp.int32, take.shape, 0) == here).astype(f32).astype(bf16)
    weight = jnp.concatenate([mine[:, :features], other[:, :features]], axis=0)
    pre[...] = dot_rows(state[...], weight)


def finish_edges(came, pre, pick, take, mine, other, out_mine, out_other, n_mine, n_other, edge_pre, part, sent, own, lat, table):
    block = lax.axis_index("nodes")
    count, nodes, width = came.shape
    rows, features = table.shape
    half, hidden = pre.shape
    feats = features // width
    for source in range(count):
        first, column = source // feats * nodes, source % feats * width
        table[first : first + nodes, column : column + width] = came[source]
    latent = table[pl.ds(pl.multiple_of(block * nodes, nodes), nodes)]
    own[...] = latent

    def weight(index):
        columns = slice(index * features, (index + 1) * features)
        return jnp.concatenate([mine[:, columns], other[:, columns]], axis=0)

    high, low = split(dot_rows(table[...], weight(1)))
    here_high, here_low = split(dot_rows(latent, weight(2)))
    chosen = jnp.concatenate([pick[...], pick[...], take[...], take[...]], axis=0)
    value = pre[...] + dot_cols(chosen, jnp.concatenate([high, low, here_high, here_low], axis=0))
    edge_pre[...] = value
    act = (value * sigmoid(value)).astype(bf16)
    out = dot(act, jnp.concatenate([out_mine[...], out_other[...]], axis=0))
    part[...] = out
    sent[:half] = out.astype(bf16)
    nodes_pre = dot_rows(latent, jnp.concatenate([n_mine[:, :features], n_other[:, :features]], axis=0))
    lat[...] = nodes_pre
    high, low = split(nodes_pre)
    sent[half:] = jnp.zeros((nodes, features), bf16)
    sent[half:, :hidden] = high
    sent[half:, hidden : 2 * hidden] = low


def update_edges(groups, *refs):
    part, lat, came, packs = refs[0], refs[1], refs[2 : groups + 1], refs[groups + 1 : 2 * groups + 1]
    theirs, state, take, normed, inverse, kept, lent, aggregate, lat_all, extra, next_all = refs[2 * groups + 1 :]
    group, core = place()
    nodes, half = take.shape
    width = kept.shape[1]
    hidden = lat.shape[1]
    for step, pack in enumerate(packs):
        both = pair(half_rows(pack, core, half), theirs[:, step * width : (step + 1) * width], core)
        extra[:, lanes(group ^ step, width * cores)] = both
    value = part[...]
    lat_all[:, :hidden] = lat[...]
    for step, ref in enumerate(came, 1):
        value = value + ref[:half].astype(f32)
        high, low = ref[half:, :hidden], ref[half:, hidden : 2 * hidden]
        lat_all[:, step * hidden : (step + 1) * hidden] = high.astype(f32) + low.astype(f32)
    normed_rows, inverse_rows = normalize(value)
    normed[...] = normed_rows
    inverse[...] = inverse_rows
    gain = extra[half + nodes :].astype(f32)[0:1]
    rows = (state[...].astype(f32) + normed_rows * gain).astype(bf16)
    aggregate[...] = dot(take[...], rows)
    next_all[...] = rows
    mine = next_all[:, lanes(group, width * cores)]
    kept[...] = jnp.where(core == 0, mine[:, :width], mine[:, width:])
    lent[...] = jnp.where(core == 0, mine[:, width:], mine[:, :width])


def turn(groups, *refs):
    far, refs = refs[: 2 * (groups - 1)], refs[2 * (groups - 1) :]
    aggregate, aggregate2, own, lat_all, extra, take, normed, inverse, edge_pre = refs[:9]
    e_mine, e_other, out_mine, out_other, in_mine, in_other, n_mine, n_other = refs[9:17]
    node_next, kept, *sents, dpre_ref, node_dpre_ref, next_all, grads = refs[17:]
    group, core = place()
    nodes, half = take.shape
    features = extra.shape[1]
    hidden = edge_pre.shape[1]
    wide = kept.shape[1]
    width = node_next.shape[1]
    gain_rows = extra[half + nodes :].astype(f32)
    edge_gain, node_gain = gain_rows[0:1], gain_rows[1:2]

    from_agg = jnp.concatenate(
        [in_mine[:, features:], in_other[:, features:]] + [f[:, :features] for f in far], axis=0
    )
    to_out = jnp.concatenate([n_mine[...], n_other[...]] + [f[:, features:] for f in far], axis=0)
    together = (aggregate[...] + aggregate2[...]).astype(bf16)
    pre = lat_all[...] + dot_rows(together, from_agg)
    act = (pre * sigmoid(pre)).astype(bf16)
    node_normed, node_inverse = normalize(dot(act, to_out))
    next_all[...] = (own[...].astype(f32) + node_normed * node_gain).astype(bf16)
    mine = next_all[:, lanes(group, wide)]
    node_next[...] = jnp.where(core == 0, mine[:, :width], mine[:, width:])
    cot = extra[half : half + nodes].astype(f32)
    node_dy = norm_back(cot * node_gain, node_normed, node_inverse).astype(bf16)
    node_dpre = (dot_rows(node_dy, to_out) * swish_slope(pre)).astype(bf16)
    high, low = split(dot(node_dpre, from_agg))

    taken = take[...]
    edge_total = extra[:half].astype(f32) + dot_cols(
        jnp.concatenate([taken, taken], axis=0), jnp.concatenate([high, low], axis=0)
    )
    dy = norm_back(edge_total * edge_gain, normed[...], inverse[...]).astype(bf16)
    back = dot_rows(dy, jnp.concatenate([out_mine[...], out_other[...]], axis=0))
    dpre = (back * swish_slope(edge_pre[...])).astype(bf16)

    dpre_ref[...] = dpre
    node_dpre_ref[...] = node_dpre[:, :hidden]
    grads[...] = dot(dpre, jnp.concatenate([e_mine[:, :features], e_other[:, :features]], axis=0))
    for step, sent in enumerate(sents, 1):
        sent[...] = grads[:, lanes(group ^ step, wide)].astype(bf16)
    grads[...] += edge_total
    kept[...] = grads[:, lanes(group, wide)]


def spread_nodes(dpre, node_dpre, pick, take, e_mine, e_other, in_mine, in_other, spread, grads):
    block = lax.axis_index("nodes")
    count, nodes, width = spread.shape
    features = grads.shape[1]
    feats = features // width

    def weighted(values, index):
        columns = slice(index * features, (index + 1) * features)
        weight = jnp.concatenate([e_mine[:, columns], e_other[:, columns]], axis=0)
        both = dot(jnp.concatenate(split(values), axis=0), weight)
        return both[: values.shape[0]] + both[values.shape[0] :]

    grads[...] = weighted(dot(pick[...], dpre[...]), 1)
    home = weighted(dot(take[...], dpre[...]), 2)
    node_weight = jnp.concatenate([in_mine[:, :features], in_other[:, :features]], axis=0)
    home = home + 0.5 * dot(node_dpre[...], node_weight)
    grads[pl.ds(pl.multiple_of(block * nodes, nodes), nodes)] += home
    for target in range(count):
        first, column = target // feats * nodes, target % feats * width
        spread[target] = grads[first : first + nodes, column : column + width].astype(bf16)


def add_groups(groups, *refs):
    parts, (kept, sent) = refs[:groups], refs[groups:]
    _, core = place()
    width = kept.shape[1]
    value = total(parts)
    kept[...] = jnp.where(core == 0, value[:, :width], value[:, width:]).astype(bf16)
    sent[...] = jnp.where(core == 0, value[:, width:], value[:, :width]).astype(bf16)


def add_nodes(shares, node_cot, node_grad):
    value = node_cot[...].astype(f32)
    for source in range(shares.shape[0]):
        value = value + shares[source].astype(f32)
    node_grad[...] = value.astype(bf16)


def assemble(next_mine, next_came, grad_mine, grad_came, edge_next, edge_grad):
    _, core = place()
    half = next_mine.shape[0]
    mine = pl.ds(pl.multiple_of(core * half, half), half)
    theirs = pl.ds(pl.multiple_of((1 - core) * half, half), half)
    edge_next[mine] = next_mine[...]
    edge_next[theirs] = next_came[...]
    edge_grad[mine] = grad_mine[...]
    edge_grad[theirs] = grad_came[...]


def shards(
    latent,
    edge_state,
    send_rows,
    sender_slot,
    receiver_row,
    edge_in_weight,
    edge_out_weight,
    edge_gain,
    node_in_weight,
    node_out_weight,
    node_gain,
    edge_cot,
    node_cot,
):
    nodes, width = latent.shape
    edge_dev = edge_state.shape[0]
    half = edge_dev // cores
    blocks = send_rows.shape[0]
    feats = lax.axis_size("feat")
    groups = feats // cores
    features = width * feats
    wide = width * cores
    hidden = edge_in_weight.shape[0] * cores
    table = blocks * nodes
    everyone = ("nodes", "feat")

    def swapped(values, bits):
        return lax.ppermute(values, "feat", [(i, i ^ bits) for i in range(feats)])

    def over_cores(values):
        return swapped(values, 1)

    def over_groups(values):
        return [swapped(values, cores * step) for step in range(1, groups)]

    gain_e, gain_n = edge_gain.reshape(1, width), node_gain.reshape(1, width)
    slot_rows = sender_slot.reshape(cores, half)
    receiver_rows = receiver_row.reshape(cores, half)

    latents = lax.all_to_all(
        jnp.broadcast_to(latent[None], (blocks * feats, nodes, width)), everyone, 0, 0
    )
    states = [edge_state] + over_groups(edge_state)
    e_in = (edge_in_weight, over_cores(edge_in_weight))
    e_out = (edge_out_weight, over_cores(edge_out_weight))
    n_in = (node_in_weight, over_cores(node_in_weight))
    n_out = (node_out_weight, over_cores(node_out_weight))
    far = []
    for weights in over_groups(jnp.concatenate([node_in_weight[:, features:], node_out_weight], axis=1)):
        far += [weights, over_cores(weights)]
    (sent,) = stage(functools.partial(send_half, groups), [((half, groups * width), bf16)], states)
    state, pre, pick, take = stage(
        functools.partial(prepare_edges, groups),
        [((half, features), bf16), ((half, hidden), f32), ((table, half), bf16), ((nodes, half), bf16)],
        [*states, over_cores(sent), *e_in, slot_rows, receiver_rows, send_rows],
        scalars=1,
    )
    rows = edge_dev + 2 * nodes
    (pack,) = stage(pack_extra, [((rows, width), bf16)], [edge_cot, node_cot, gain_e, gain_n])
    packs = [pack] + over_groups(pack)
    (sent,) = stage(functools.partial(send_half, groups), [((rows - half, groups * width), bf16)], packs)
    extra_came = over_cores(sent)
    edge_pre, part, sent, own, lat = stage(
        finish_edges,
        [
            ((half, hidden), f32),
            ((half, features), f32),
            ((half + nodes, features), bf16),
            ((nodes, features), bf16),
            ((nodes, hidden), f32),
        ],
        [latents, pre, pick, take, *e_in, *e_out, *n_in],
        scratch=[((table, features), bf16)],
    )
    normed, inverse, next_mine, next_sent, aggregate, lat_all, extra = stage(
        functools.partial(update_edges, groups),
        [
            ((half, features), f32),
            ((half, 1), f32),
            ((half, width), bf16),
            ((half, width), bf16),
            ((nodes, features), f32),
            ((nodes, features), f32),
            ((half + 2 * nodes, features), bf16),
        ],
        [part, lat, *over_groups(sent), *packs, extra_came, state, take],
        scratch=[((half, features), bf16)],
    )
    aggregate2 = over_cores(aggregate)
    next_came = over_cores(next_sent)
    node_next, kept, *sents, dpre, node_dpre = stage(
        functools.partial(turn, groups),
        [((nodes, width), bf16), ((half, wide), f32)]
        + [((half, wide), bf16)] * (groups - 1)
        + [((half, hidden), bf16), ((nodes, hidden), bf16)],
        [*far, aggregate, aggregate2, own, lat_all, extra, take, normed, inverse, edge_pre]
        + [*e_in, *e_out, *n_in, *n_out],
        scratch=[((nodes, features), bf16), ((half, features), f32)],
    )
    sents = [swapped(s, cores * k) for k, s in enumerate(sents, 1)]
    (spread,) = stage(
        spread_nodes,
        [((blocks * feats, nodes, width), bf16)],
        [dpre, node_dpre, pick, take, *e_in, *n_in],
        scratch=[((table, features), f32)],
    )
    shares = lax.all_to_all(spread, everyone, 0, 0)
    grad_mine, grad_sent = stage(
        functools.partial(add_groups, groups),
        [((half, width), bf16), ((half, width), bf16)],
        [kept, *sents],
    )
    edge_next, edge_grad = stage(
        assemble,
        [((edge_dev, width), bf16), ((edge_dev, width), bf16)],
        [next_mine, next_came, grad_mine, over_cores(grad_sent)],
    )
    (node_grad,) = stage(add_nodes, [((nodes, width), bf16)], [shares, node_cot])
    return (edge_next, node_next, edge_grad, node_grad)


def solution(mesh):
    rows = P(("groups", "nodes"), "feat")
    flat = P(("groups", "nodes"))
    matrix = P("feat", None)
    vector = P("feat")
    return jax.shard_map(
        shards,
        mesh=mesh,
        in_specs=(
            rows,
            rows,
            P("groups", None, None),
            flat,
            flat,
            matrix,
            matrix,
            vector,
            matrix,
            matrix,
            vector,
            rows,
            rows,
        ),
        out_specs=(rows, rows, rows, rows),
        check_vma=False,
    )
```

```python
import functools

import jax
import jax.numpy as jnp
from jax import lax
from jax.experimental import pallas as pl
from jax.experimental.pallas import tpu as pltpu
from jax.sharding import PartitionSpec as P

epsilon = 1e-05
f32 = jnp.float32
bf16 = jnp.bfloat16
cores = 2
kernel_vmem = 8 << 20


def dot(left, right):
    return jnp.dot(left, right, preferred_element_type=f32)


def dot_rows(left, right):
    return lax.dot_general(left, right, (((1,), (1,)), ((), ())), preferred_element_type=f32)


def dot_cols(left, right):
    return lax.dot_general(left, right, (((0,), (0,)), ((), ())), preferred_element_type=f32)


def split(values):
    high = values.astype(bf16)
    return high, (values - high.astype(f32)).astype(bf16)


def sigmoid(values):
    return 1.0 / (1.0 + jnp.exp(-values))


def swish_slope(pre_act):
    sigma = sigmoid(pre_act)
    return sigma * (1.0 + pre_act * (1.0 - sigma))


def normalize(values):
    mean = jnp.mean(values, axis=1, keepdims=True)
    square = jnp.mean(values * values, axis=1, keepdims=True)
    inverse = lax.rsqrt(square - mean * mean + epsilon)
    return (values - mean) * inverse, inverse


def norm_back(grad, normed, inverse):
    total = jnp.mean(grad, axis=1, keepdims=True)
    cross = jnp.mean(grad * normed, axis=1, keepdims=True)
    return inverse * (grad - total - normed * cross)


def place():
    feat = lax.axis_index("feat")
    return feat // cores, feat % cores


def pair(mine, other, core):
    return jnp.where(core == 0, jnp.concatenate([mine, other], 1), jnp.concatenate([other, mine], 1))


def lanes(group, width):
    return pl.ds(pl.multiple_of(group * width, width), width)


def stage(kernel, outs, operands, scalars=0, scratch=(), flops=1 << 24):
    specs = [pl.BlockSpec(memory_space=pltpu.VMEM)] * (len(operands) - scalars)
    specs += [pl.BlockSpec(memory_space=pltpu.SMEM)] * scalars
    moved = sum(o.size * o.dtype.itemsize for o in operands)
    return pl.pallas_call(
        kernel,
        out_shape=[jax.ShapeDtypeStruct(shape, kind) for shape, kind in outs],
        in_specs=specs,
        out_specs=[pl.BlockSpec(memory_space=pltpu.VMEM)] * len(outs),
        scratch_shapes=[pltpu.VMEM(shape, kind) for shape, kind in scratch],
        cost_estimate=pl.CostEstimate(flops=flops, bytes_accessed=moved, transcendentals=0),
        compiler_params=pltpu.CompilerParams(vmem_limit_bytes=kernel_vmem),
    )(*operands)


def gains(gain_e, gain_n, rows):
    shape = (rows, gain_e.shape[1])
    row = lax.broadcasted_iota(jnp.int32, shape, 0)
    e = jnp.broadcast_to(gain_e[...].astype(f32), shape)
    n = jnp.broadcast_to(gain_n[...].astype(f32), shape)
    return jnp.where(row == 0, e, n).astype(bf16)


def total(refs):
    value = refs[0][...]
    for ref in refs[1:]:
        value = value + ref[...].astype(f32)
    return value


def spread_latent(latent, spread):
    spread[...] = jnp.broadcast_to(latent[...][None], spread.shape)


def merge_state(state, state2, pack):
    _, core = place()
    half = pack.shape[0]
    mine = pl.ds(pl.multiple_of(core * half, half), half)
    pack[...] = pair(state[mine], state2[mine], core)


def pack_extra(edge_cot, node_cot, gain_e, gain_n, pack):
    edge_dev = edge_cot.shape[0]
    nodes = node_cot.shape[0]
    pack[:edge_dev] = edge_cot[...]
    pack[edge_dev : edge_dev + nodes] = node_cot[...]
    pack[edge_dev + nodes :] = gains(gain_e, gain_n, nodes)


def half_rows(pack, core, half):
    rows = pack[pl.ds(pl.multiple_of(core * half, half), half)]
    if pack.shape[0] == cores * half:
        return rows
    return jnp.concatenate([rows, pack[cores * half :]], axis=0)


def send_half(groups, *refs):
    packs, sent = refs[:groups], refs[groups]
    _, core = place()
    width = packs[0].shape[1]
    half = packs[0].shape[0] - sent.shape[0]
    for step, pack in enumerate(packs):
        sent[:, step * width : (step + 1) * width] = half_rows(pack, 1 - core, half)


def prepare_edges(groups, *refs):
    packs = refs[:groups]
    mine, other, slot, receiver, send_rows, state, pre, pick, take = refs[groups:]
    group, core = place()
    block = lax.axis_index("nodes")
    features = state.shape[1]
    nodes, half = take.shape
    blocks, _, slots = send_rows.shape
    for step, pack in enumerate(packs):
        state[:, lanes(group ^ step, pack.shape[1])] = pack[...]

    slot_row = slot[pl.ds(core, 1)]
    sender = block * nodes + slot_row
    for source in range(blocks):
        for k in range(slots):
            row = source * nodes + send_rows[source, block, k]
            sender = jnp.where(slot_row == nodes + source * slots + k, row, sender)
    pick[...] = (lax.broadcasted_iota(jnp.int32, pick.shape, 0) == sender).astype(f32).astype(bf16)
    here = receiver[pl.ds(core, 1)]
    take[...] = (lax.broadcasted_iota(jnp.int32, take.shape, 0) == here).astype(f32).astype(bf16)
    weight = jnp.concatenate([mine[:, :features], other[:, :features]], axis=0)
    pre[...] = dot_rows(state[...], weight)


def finish_edges(came, pre, pick, take, mine, other, n_mine, n_other, edge_pre, sent, own, lat, table):
    block = lax.axis_index("nodes")
    count, nodes, width = came.shape
    rows, features = table.shape
    half = pre.shape[0]
    feats = features // width
    for source in range(count):
        first, column = source // feats * nodes, source % feats * width
        table[first : first + nodes, column : column + width] = came[source]
    latent = table[pl.ds(pl.multiple_of(block * nodes, nodes), nodes)]
    own[...] = latent

    def weight(index):
        columns = slice(index * features, (index + 1) * features)
        return jnp.concatenate([mine[:, columns], other[:, columns]], axis=0)

    high, low = split(dot_rows(table[...], weight(1)))
    here_high, here_low = split(dot_rows(latent, weight(2)))
    chosen = jnp.concatenate([pick[...], pick[...], take[...], take[...]], axis=0)
    value = pre[...] + dot_cols(chosen, jnp.concatenate([high, low, here_high, here_low], axis=0))
    edge_pre[...] = value
    sent[:half] = (value * sigmoid(value)).astype(bf16)
    nodes_pre = dot_rows(latent, jnp.concatenate([n_mine[:, :features], n_other[:, :features]], axis=0))
    lat[...] = nodes_pre
    sent[half:] = jnp.concatenate(split(nodes_pre), axis=0)


def update_edges(groups, *refs):
    lat, acts, packs, refs = refs[0], refs[1 : groups + 1], refs[groups + 1 : 2 * groups + 1], refs[2 * groups + 1 :]
    far, refs = refs[: 2 * (groups - 1)], refs[2 * (groups - 1) :]
    out_mine, out_other, theirs, state, take, normed, inverse, kept, lent, aggregate, lat_all, extra, next_all = refs
    group, core = place()
    nodes, half = take.shape
    width = kept.shape[1]
    hidden = lat.shape[1]
    for step, pack in enumerate(packs):
        both = pair(half_rows(pack, core, half), theirs[:, step * width : (step + 1) * width], core)
        extra[:, lanes(group ^ step, width * cores)] = both
    lat_all[:, :hidden] = lat[...]
    for step, act in enumerate(acts[1:], 1):
        high, low = act[half : half + nodes], act[half + nodes :]
        lat_all[:, step * hidden : (step + 1) * hidden] = high.astype(f32) + low.astype(f32)
    features = state.shape[1]
    weight = jnp.concatenate([out_mine[...], out_other[...]] + [f[:, 2 * features :] for f in far], axis=0)
    value = dot(jnp.concatenate([act[:half] for act in acts], axis=1), weight)
    normed_rows, inverse_rows = normalize(value)
    normed[...] = normed_rows
    inverse[...] = inverse_rows
    gain = extra[half + nodes :].astype(f32)[0:1]
    rows = (state[...].astype(f32) + normed_rows * gain).astype(bf16)
    aggregate[...] = dot(take[...], rows)
    next_all[...] = rows
    mine = next_all[:, lanes(group, width * cores)]
    kept[...] = jnp.where(core == 0, mine[:, :width], mine[:, width:])
    lent[...] = jnp.where(core == 0, mine[:, width:], mine[:, :width])


def turn(groups, *refs):
    far, refs = refs[: 2 * (groups - 1)], refs[2 * (groups - 1) :]
    aggregate, aggregate2, own, lat_all, extra, take, normed, inverse, edge_pre = refs[:9]
    e_mine, e_other, out_mine, out_other, in_mine, in_other, n_mine, n_other = refs[9:17]
    node_next, kept, *sents, dpre_ref, node_dpre_ref, next_all, grads = refs[17:]
    group, core = place()
    nodes, half = take.shape
    features = extra.shape[1]
    hidden = edge_pre.shape[1]
    wide = kept.shape[1]
    width = node_next.shape[1]
    gain_rows = extra[half + nodes :].astype(f32)
    edge_gain, node_gain = gain_rows[0:1], gain_rows[1:2]

    from_agg = jnp.concatenate(
        [in_mine[:, features:], in_other[:, features:]] + [f[:, :features] for f in far], axis=0
    )
    to_out = jnp.concatenate([n_mine[...], n_other[...]] + [f[:, features : 2 * features] for f in far], axis=0)
    together = (aggregate[...] + aggregate2[...]).astype(bf16)
    pre = lat_all[...] + dot_rows(together, from_agg)
    act = (pre * sigmoid(pre)).astype(bf16)
    node_normed, node_inverse = normalize(dot(act, to_out))
    next_all[...] = (own[...].astype(f32) + node_normed * node_gain).astype(bf16)
    mine = next_all[:, lanes(group, wide)]
    node_next[...] = jnp.where(core == 0, mine[:, :width], mine[:, width:])
    cot = extra[half : half + nodes].astype(f32)
    node_dy = norm_back(cot * node_gain, node_normed, node_inverse).astype(bf16)
    node_dpre = (dot_rows(node_dy, to_out) * swish_slope(pre)).astype(bf16)
    high, low = split(dot(node_dpre, from_agg))

    taken = take[...]
    edge_total = extra[:half].astype(f32) + dot_cols(
        jnp.concatenate([taken, taken], axis=0), jnp.concatenate([high, low], axis=0)
    )
    dy = norm_back(edge_total * edge_gain, normed[...], inverse[...]).astype(bf16)
    back = dot_rows(dy, jnp.concatenate([out_mine[...], out_other[...]], axis=0))
    dpre = (back * swish_slope(edge_pre[...])).astype(bf16)

    dpre_ref[...] = dpre
    node_dpre_ref[...] = node_dpre[:, :hidden]
    grads[...] = dot(dpre, jnp.concatenate([e_mine[:, :features], e_other[:, :features]], axis=0))
    for step, sent in enumerate(sents, 1):
        sent[...] = grads[:, lanes(group ^ step, wide)].astype(bf16)
    grads[...] += edge_total
    kept[...] = grads[:, lanes(group, wide)]


def spread_nodes(dpre, node_dpre, pick, take, e_mine, e_other, in_mine, in_other, spread, grads):
    block = lax.axis_index("nodes")
    count, nodes, width = spread.shape
    features = grads.shape[1]
    feats = features // width

    def weighted(values, index):
        columns = slice(index * features, (index + 1) * features)
        weight = jnp.concatenate([e_mine[:, columns], e_other[:, columns]], axis=0)
        both = dot(jnp.concatenate(split(values), axis=0), weight)
        return both[: values.shape[0]] + both[values.shape[0] :]

    grads[...] = weighted(dot(pick[...], dpre[...]), 1)
    home = weighted(dot(take[...], dpre[...]), 2)
    node_weight = jnp.concatenate([in_mine[:, :features], in_other[:, :features]], axis=0)
    home = home + 0.5 * dot(node_dpre[...], node_weight)
    grads[pl.ds(pl.multiple_of(block * nodes, nodes), nodes)] += home
    for target in range(count):
        first, column = target // feats * nodes, target % feats * width
        spread[target] = grads[first : first + nodes, column : column + width].astype(bf16)


def add_groups(groups, *refs):
    parts, (kept, sent) = refs[:groups], refs[groups:]
    _, core = place()
    width = kept.shape[1]
    value = total(parts)
    kept[...] = jnp.where(core == 0, value[:, :width], value[:, width:]).astype(bf16)
    sent[...] = jnp.where(core == 0, value[:, width:], value[:, :width]).astype(bf16)


def add_nodes(shares, node_cot, node_grad):
    value = node_cot[...].astype(f32)
    for source in range(shares.shape[0]):
        value = value + shares[source].astype(f32)
    node_grad[...] = value.astype(bf16)


def assemble(next_mine, next_came, grad_mine, grad_came, edge_next, edge_grad):
    _, core = place()
    half = next_mine.shape[0]
    mine = pl.ds(pl.multiple_of(core * half, half), half)
    theirs = pl.ds(pl.multiple_of((1 - core) * half, half), half)
    edge_next[mine] = next_mine[...]
    edge_next[theirs] = next_came[...]
    edge_grad[mine] = grad_mine[...]
    edge_grad[theirs] = grad_came[...]


def shards(
    latent,
    edge_state,
    send_rows,
    sender_slot,
    receiver_row,
    edge_in_weight,
    edge_out_weight,
    edge_gain,
    node_in_weight,
    node_out_weight,
    node_gain,
    edge_cot,
    node_cot,
):
    nodes, width = latent.shape
    edge_dev = edge_state.shape[0]
    half = edge_dev // cores
    blocks = send_rows.shape[0]
    feats = lax.axis_size("feat")
    groups = feats // cores
    features = width * feats
    wide = width * cores
    hidden = edge_in_weight.shape[0] * cores
    table = blocks * nodes
    everyone = ("nodes", "feat")

    def swapped(values, bits):
        return lax.ppermute(values, "feat", [(i, i ^ bits) for i in range(feats)])

    def over_cores(values):
        return swapped(values, 1)

    def over_groups(values):
        return [swapped(values, cores * step) for step in range(1, groups)]

    gain_e, gain_n = edge_gain.reshape(1, width), node_gain.reshape(1, width)
    slot_rows = sender_slot.reshape(cores, half)
    receiver_rows = receiver_row.reshape(cores, half)

    (spread,) = stage(spread_latent, [((blocks * feats, nodes, width), bf16)], [latent])
    latents = lax.all_to_all(spread, everyone, 0, 0)
    (pack,) = stage(merge_state, [((half, wide), bf16)], [edge_state, over_cores(edge_state)])
    pack, edge_cot = lax.optimization_barrier((pack, edge_cot))
    states = [pack] + over_groups(pack)
    e_in = (edge_in_weight, over_cores(edge_in_weight))
    e_out = (edge_out_weight, over_cores(edge_out_weight))
    n_in = (node_in_weight, over_cores(node_in_weight))
    n_out = (node_out_weight, over_cores(node_out_weight))
    far = []
    for weights in over_groups(jnp.concatenate([node_in_weight[:, features:], node_out_weight, edge_out_weight], axis=1)):
        far += [weights, over_cores(weights)]
    state, pre, pick, take = stage(
        functools.partial(prepare_edges, groups),
        [((half, features), bf16), ((half, hidden), f32), ((table, half), bf16), ((nodes, half), bf16)],
        [*states, *e_in, slot_rows, receiver_rows, send_rows],
        scalars=1,
    )
    rows = edge_dev + 2 * nodes
    (pack,) = stage(pack_extra, [((rows, width), bf16)], [edge_cot, node_cot, gain_e, gain_n])
    packs = [pack] + over_groups(pack)
    (sent,) = stage(functools.partial(send_half, groups), [((rows - half, groups * width), bf16)], packs)
    extra_came = over_cores(sent)
    edge_pre, sent, own, lat = stage(
        finish_edges,
        [
            ((half, hidden), f32),
            ((half + 2 * nodes, hidden), bf16),
            ((nodes, features), bf16),
            ((nodes, hidden), f32),
        ],
        [latents, pre, pick, take, *e_in, *n_in],
        scratch=[((table, features), bf16)],
    )
    normed, inverse, next_mine, next_sent, aggregate, lat_all, extra = stage(
        functools.partial(update_edges, groups),
        [
            ((half, features), f32),
            ((half, 1), f32),
            ((half, width), bf16),
            ((half, width), bf16),
            ((nodes, features), f32),
            ((nodes, features), f32),
            ((half + 2 * nodes, features), bf16),
        ],
        [lat, sent, *over_groups(sent), *packs, *far, *e_out, extra_came, state, take],
        scratch=[((half, features), bf16)],
    )
    aggregate2 = over_cores(aggregate)
    next_came = over_cores(next_sent)
    node_next, kept, *sents, dpre, node_dpre = stage(
        functools.partial(turn, groups),
        [((nodes, width), bf16), ((half, wide), f32)]
        + [((half, wide), bf16)] * (groups - 1)
        + [((half, hidden), bf16), ((nodes, hidden), bf16)],
        [*far, aggregate, aggregate2, own, lat_all, extra, take, normed, inverse, edge_pre]
        + [*e_in, *e_out, *n_in, *n_out],
        scratch=[((nodes, features), bf16), ((half, features), f32)],
    )
    sents = [swapped(s, cores * k) for k, s in enumerate(sents, 1)]
    (spread,) = stage(
        spread_nodes,
        [((blocks * feats, nodes, width), bf16)],
        [dpre, node_dpre, pick, take, *e_in, *n_in],
        scratch=[((table, features), f32)],
    )
    shares = lax.all_to_all(spread, everyone, 0, 0)
    grad_mine, grad_sent = stage(
        functools.partial(add_groups, groups),
        [((half, width), bf16), ((half, width), bf16)],
        [kept, *sents],
    )
    edge_next, edge_grad = stage(
        assemble,
        [((edge_dev, width), bf16), ((edge_dev, width), bf16)],
        [next_mine, next_came, grad_mine, over_cores(grad_sent)],
    )
    (node_grad,) = stage(add_nodes, [((nodes, width), bf16)], [shares, node_cot])
    return (edge_next, node_next, edge_grad, node_grad)


def solution(mesh):
    rows = P(("groups", "nodes"), "feat")
    flat = P(("groups", "nodes"))
    matrix = P("feat", None)
    vector = P("feat")
    return jax.shard_map(
        shards,
        mesh=mesh,
        in_specs=(
            rows,
            rows,
            P("groups", None, None),
            flat,
            flat,
            matrix,
            matrix,
            vector,
            matrix,
            matrix,
            vector,
            rows,
            rows,
        ),
        out_specs=(rows, rows, rows, rows),
        check_vma=False,
    )
```

```python
import functools

import jax
import jax.numpy as jnp
from jax import lax
from jax.experimental import pallas as pl
from jax.experimental.pallas import tpu as pltpu
from jax.sharding import PartitionSpec as P

epsilon = 1e-05
f32 = jnp.float32
bf16 = jnp.bfloat16
cores = 2
kernel_vmem = 8 << 20


def dot(left, right):
    return jnp.dot(left, right, preferred_element_type=f32)


def dot_rows(left, right):
    return lax.dot_general(left, right, (((1,), (1,)), ((), ())), preferred_element_type=f32)


def dot_cols(left, right):
    return lax.dot_general(left, right, (((0,), (0,)), ((), ())), preferred_element_type=f32)


def split(values):
    high = values.astype(bf16)
    return high, (values - high.astype(f32)).astype(bf16)


def sigmoid(values):
    return 1.0 / (1.0 + jnp.exp(-values))


def swish_slope(pre_act):
    sigma = sigmoid(pre_act)
    return sigma * (1.0 + pre_act * (1.0 - sigma))


def normalize(values):
    mean = jnp.mean(values, axis=1, keepdims=True)
    square = jnp.mean(values * values, axis=1, keepdims=True)
    inverse = lax.rsqrt(square - mean * mean + epsilon)
    return (values - mean) * inverse, inverse


def norm_back(grad, normed, inverse):
    total = jnp.mean(grad, axis=1, keepdims=True)
    cross = jnp.mean(grad * normed, axis=1, keepdims=True)
    return inverse * (grad - total - normed * cross)


def place():
    feat = lax.axis_index("feat")
    return feat // cores, feat % cores


def pair(mine, other, core):
    return jnp.where(core == 0, jnp.concatenate([mine, other], 1), jnp.concatenate([other, mine], 1))


def lanes(group, width):
    return pl.ds(pl.multiple_of(group * width, width), width)


def stage(kernel, outs, operands, scalars=0, scratch=(), flops=1 << 24):
    specs = [pl.BlockSpec(memory_space=pltpu.VMEM)] * (len(operands) - scalars)
    specs += [pl.BlockSpec(memory_space=pltpu.SMEM)] * scalars
    moved = sum(o.size * o.dtype.itemsize for o in operands)
    return pl.pallas_call(
        kernel,
        out_shape=[jax.ShapeDtypeStruct(shape, kind) for shape, kind in outs],
        in_specs=specs,
        out_specs=[pl.BlockSpec(memory_space=pltpu.VMEM)] * len(outs),
        scratch_shapes=[pltpu.VMEM(shape, kind) for shape, kind in scratch],
        cost_estimate=pl.CostEstimate(flops=flops, bytes_accessed=moved, transcendentals=0),
        compiler_params=pltpu.CompilerParams(vmem_limit_bytes=kernel_vmem),
    )(*operands)


def gains(gain_e, gain_n, rows):
    shape = (rows, gain_e.shape[1])
    row = lax.broadcasted_iota(jnp.int32, shape, 0)
    e = jnp.broadcast_to(gain_e[...].astype(f32), shape)
    n = jnp.broadcast_to(gain_n[...].astype(f32), shape)
    return jnp.where(row == 0, e, n).astype(bf16)


def total(refs):
    value = refs[0][...]
    for ref in refs[1:]:
        value = value + ref[...].astype(f32)
    return value


def spread_latent(latent, spread):
    spread[...] = jnp.broadcast_to(latent[...][None], spread.shape)


def merge_state(state, state2, pack):
    _, core = place()
    half = pack.shape[0]
    mine = pl.ds(pl.multiple_of(core * half, half), half)
    pack[...] = pair(state[mine], state2[mine], core)


def pack_extra(edge_cot, node_cot, gain_e, gain_n, pack):
    edge_dev = edge_cot.shape[0]
    nodes = node_cot.shape[0]
    pack[:edge_dev] = edge_cot[...]
    pack[edge_dev : edge_dev + nodes] = node_cot[...]
    pack[edge_dev + nodes :] = gains(gain_e, gain_n, nodes)


def half_rows(pack, core, half):
    rows = pack[pl.ds(pl.multiple_of(core * half, half), half)]
    if pack.shape[0] == cores * half:
        return rows
    return jnp.concatenate([rows, pack[cores * half :]], axis=0)


def send_half(groups, *refs):
    packs, sent = refs[:groups], refs[groups]
    _, core = place()
    width = packs[0].shape[1]
    half = packs[0].shape[0] - sent.shape[0]
    for step, pack in enumerate(packs):
        sent[:, step * width : (step + 1) * width] = half_rows(pack, 1 - core, half)


def prepare_edges(groups, *refs):
    packs = refs[:groups]
    mine, other, slot, receiver, send_rows, state, pre, pick, take = refs[groups:]
    group, core = place()
    block = lax.axis_index("nodes")
    features = state.shape[1]
    nodes, half = take.shape
    blocks, _, slots = send_rows.shape
    for step, pack in enumerate(packs):
        state[:, lanes(group ^ step, pack.shape[1])] = pack[...]

    slot_row = slot[pl.ds(core, 1)]
    sender = block * nodes + slot_row
    for source in range(blocks):
        for k in range(slots):
            row = source * nodes + send_rows[source, block, k]
            sender = jnp.where(slot_row == nodes + source * slots + k, row, sender)
    pick[...] = (lax.broadcasted_iota(jnp.int32, pick.shape, 0) == sender).astype(f32).astype(bf16)
    here = receiver[pl.ds(core, 1)]
    take[...] = (lax.broadcasted_iota(jnp.int32, take.shape, 0) == here).astype(f32).astype(bf16)
    weight = jnp.concatenate([mine[:, :features], other[:, :features]], axis=0)
    pre[...] = dot_rows(state[...], weight)


def finish_edges(came, pre, pick, take, mine, other, out_mine, out_other, n_mine, n_other, edge_pre, part, sent, own, lat, table):
    block = lax.axis_index("nodes")
    count, nodes, width = came.shape
    rows, features = table.shape
    half, hidden = pre.shape
    feats = features // width
    for source in range(count):
        first, column = source // feats * nodes, source % feats * width
        table[first : first + nodes, column : column + width] = came[source]
    latent = table[pl.ds(pl.multiple_of(block * nodes, nodes), nodes)]
    own[...] = latent

    def weight(index):
        columns = slice(index * features, (index + 1) * features)
        return jnp.concatenate([mine[:, columns], other[:, columns]], axis=0)

    high, low = split(dot_rows(table[...], weight(1)))
    here_high, here_low = split(dot_rows(latent, weight(2)))
    chosen = jnp.concatenate([pick[...], pick[...], take[...], take[...]], axis=0)
    value = pre[...] + dot_cols(chosen, jnp.concatenate([high, low, here_high, here_low], axis=0))
    edge_pre[...] = value
    act = (value * sigmoid(value)).astype(bf16)
    out = dot(act, jnp.concatenate([out_mine[...], out_other[...]], axis=0))
    part[...] = out
    sent[:half] = out.astype(bf16)
    nodes_pre = dot_rows(latent, jnp.concatenate([n_mine[:, :features], n_other[:, :features]], axis=0))
    lat[...] = nodes_pre
    high, low = split(nodes_pre)
    sent[half:] = jnp.zeros((nodes, features), bf16)
    sent[half:, :hidden] = high
    sent[half:, hidden : 2 * hidden] = low


def update_edges(groups, *refs):
    part, lat, came, packs = refs[0], refs[1], refs[2 : groups + 1], refs[groups + 1 : 2 * groups + 1]
    theirs, state, take, normed, inverse, kept, lent, aggregate, lat_all, extra, next_all = refs[2 * groups + 1 :]
    group, core = place()
    nodes, half = take.shape
    width = kept.shape[1]
    hidden = lat.shape[1]
    for step, pack in enumerate(packs):
        both = pair(half_rows(pack, core, half), theirs[:, step * width : (step + 1) * width], core)
        extra[:, lanes(group ^ step, width * cores)] = both
    value = part[...]
    lat_all[:, :hidden] = lat[...]
    for step, ref in enumerate(came, 1):
        value = value + ref[:half].astype(f32)
        high, low = ref[half:, :hidden], ref[half:, hidden : 2 * hidden]
        lat_all[:, step * hidden : (step + 1) * hidden] = high.astype(f32) + low.astype(f32)
    normed_rows, inverse_rows = normalize(value)
    normed[...] = normed_rows
    inverse[...] = inverse_rows
    gain = extra[half + nodes :].astype(f32)[0:1]
    rows = (state[...].astype(f32) + normed_rows * gain).astype(bf16)
    aggregate[...] = dot(take[...], rows)
    next_all[...] = rows
    mine = next_all[:, lanes(group, width * cores)]
    kept[...] = jnp.where(core == 0, mine[:, :width], mine[:, width:])
    lent[...] = jnp.where(core == 0, mine[:, width:], mine[:, :width])


def turn(groups, *refs):
    far, refs = refs[: 2 * (groups - 1)], refs[2 * (groups - 1) :]
    aggregate, aggregate2, own, lat_all, extra, take, normed, inverse, edge_pre = refs[:9]
    e_mine, e_other, out_mine, out_other, in_mine, in_other, n_mine, n_other = refs[9:17]
    node_next, kept, *sents, dpre_ref, node_dpre_ref, next_all, grads = refs[17:]
    group, core = place()
    nodes, half = take.shape
    features = extra.shape[1]
    hidden = edge_pre.shape[1]
    wide = kept.shape[1]
    width = node_next.shape[1]
    gain_rows = extra[half + nodes :].astype(f32)
    edge_gain, node_gain = gain_rows[0:1], gain_rows[1:2]

    from_agg = jnp.concatenate(
        [in_mine[:, features:], in_other[:, features:]] + [f[:, :features] for f in far], axis=0
    )
    to_out = jnp.concatenate([n_mine[...], n_other[...]] + [f[:, features:] for f in far], axis=0)
    together = (aggregate[...] + aggregate2[...]).astype(bf16)
    pre = lat_all[...] + dot_rows(together, from_agg)
    act = (pre * sigmoid(pre)).astype(bf16)
    node_normed, node_inverse = normalize(dot(act, to_out))
    next_all[...] = (own[...].astype(f32) + node_normed * node_gain).astype(bf16)
    mine = next_all[:, lanes(group, wide)]
    node_next[...] = jnp.where(core == 0, mine[:, :width], mine[:, width:])
    cot = extra[half : half + nodes].astype(f32)
    node_dy = norm_back(cot * node_gain, node_normed, node_inverse).astype(bf16)
    node_dpre = (dot_rows(node_dy, to_out) * swish_slope(pre)).astype(bf16)
    high, low = split(dot(node_dpre, from_agg))

    taken = take[...]
    edge_total = extra[:half].astype(f32) + dot_cols(
        jnp.concatenate([taken, taken], axis=0), jnp.concatenate([high, low], axis=0)
    )
    dy = norm_back(edge_total * edge_gain, normed[...], inverse[...]).astype(bf16)
    back = dot_rows(dy, jnp.concatenate([out_mine[...], out_other[...]], axis=0))
    dpre = (back * swish_slope(edge_pre[...])).astype(bf16)

    dpre_ref[...] = dpre
    node_dpre_ref[...] = node_dpre[:, :hidden]
    grads[...] = dot(dpre, jnp.concatenate([e_mine[:, :features], e_other[:, :features]], axis=0))
    for step, sent in enumerate(sents, 1):
        sent[...] = grads[:, lanes(group ^ step, wide)].astype(bf16)
    grads[...] += edge_total
    kept[...] = grads[:, lanes(group, wide)]


def spread_nodes(dpre, node_dpre, pick, take, e_mine, e_other, in_mine, in_other, spread, grads):
    block = lax.axis_index("nodes")
    count, nodes, width = spread.shape
    features = grads.shape[1]
    feats = features // width

    def weighted(values, index):
        columns = slice(index * features, (index + 1) * features)
        weight = jnp.concatenate([e_mine[:, columns], e_other[:, columns]], axis=0)
        both = dot(jnp.concatenate(split(values), axis=0), weight)
        return both[: values.shape[0]] + both[values.shape[0] :]

    grads[...] = weighted(dot(pick[...], dpre[...]), 1)
    home = weighted(dot(take[...], dpre[...]), 2)
    node_weight = jnp.concatenate([in_mine[:, :features], in_other[:, :features]], axis=0)
    home = home + 0.5 * dot(node_dpre[...], node_weight)
    grads[pl.ds(pl.multiple_of(block * nodes, nodes), nodes)] += home
    for target in range(count):
        first, column = target // feats * nodes, target % feats * width
        spread[target] = grads[first : first + nodes, column : column + width].astype(bf16)


def add_groups(groups, *refs):
    parts, (kept, sent) = refs[:groups], refs[groups:]
    _, core = place()
    width = kept.shape[1]
    value = total(parts)
    kept[...] = jnp.where(core == 0, value[:, :width], value[:, width:]).astype(bf16)
    sent[...] = jnp.where(core == 0, value[:, width:], value[:, :width]).astype(bf16)


def add_nodes(shares, node_cot, node_grad):
    value = node_cot[...].astype(f32)
    for source in range(shares.shape[0]):
        value = value + shares[source].astype(f32)
    node_grad[...] = value.astype(bf16)


def assemble(next_mine, next_came, grad_mine, grad_came, edge_next, edge_grad):
    _, core = place()
    half = next_mine.shape[0]
    mine = pl.ds(pl.multiple_of(core * half, half), half)
    theirs = pl.ds(pl.multiple_of((1 - core) * half, half), half)
    edge_next[mine] = next_mine[...]
    edge_next[theirs] = next_came[...]
    edge_grad[mine] = grad_mine[...]
    edge_grad[theirs] = grad_came[...]


def shards(
    latent,
    edge_state,
    send_rows,
    sender_slot,
    receiver_row,
    edge_in_weight,
    edge_out_weight,
    edge_gain,
    node_in_weight,
    node_out_weight,
    node_gain,
    edge_cot,
    node_cot,
):
    nodes, width = latent.shape
    edge_dev = edge_state.shape[0]
    half = edge_dev // cores
    blocks = send_rows.shape[0]
    feats = lax.axis_size("feat")
    groups = feats // cores
    features = width * feats
    wide = width * cores
    hidden = edge_in_weight.shape[0] * cores
    table = blocks * nodes
    everyone = ("nodes", "feat")

    def swapped(values, bits):
        return lax.ppermute(values, "feat", [(i, i ^ bits) for i in range(feats)])

    def over_cores(values):
        return swapped(values, 1)

    def over_groups(values):
        return [swapped(values, cores * step) for step in range(1, groups)]

    gain_e, gain_n = edge_gain.reshape(1, width), node_gain.reshape(1, width)
    slot_rows = sender_slot.reshape(cores, half)
    receiver_rows = receiver_row.reshape(cores, half)

    (spread,) = stage(spread_latent, [((blocks * feats, nodes, width), bf16)], [latent])
    latents = lax.all_to_all(spread, everyone, 0, 0)
    (pack,) = stage(merge_state, [((half, wide), bf16)], [edge_state, over_cores(edge_state)])
    pack, edge_cot = lax.optimization_barrier((pack, edge_cot))
    states = [pack] + over_groups(pack)
    e_in = (edge_in_weight, over_cores(edge_in_weight))
    e_out = (edge_out_weight, over_cores(edge_out_weight))
    n_in = (node_in_weight, over_cores(node_in_weight))
    n_out = (node_out_weight, over_cores(node_out_weight))
    far = over_groups(jnp.concatenate([node_in_weight[:, features:], node_out_weight], axis=1))
    state, pre, pick, take = stage(
        functools.partial(prepare_edges, groups),
        [((half, features), bf16), ((half, hidden), f32), ((table, half), bf16), ((nodes, half), bf16)],
        [*states, *e_in, slot_rows, receiver_rows, send_rows],
        scalars=1,
    )
    rows = edge_dev + 2 * nodes
    (pack,) = stage(pack_extra, [((rows, width), bf16)], [edge_cot, node_cot, gain_e, gain_n])
    packs = over_groups(pack)
    far, packs, _ = lax.optimization_barrier((far, packs, pre))
    far = [weights for came in far for weights in (came, over_cores(came))]
    packs = [pack] + packs
    (sent,) = stage(functools.partial(send_half, groups), [((rows - half, groups * width), bf16)], packs)
    extra_came = over_cores(sent)
    edge_pre, part, sent, own, lat = stage(
        finish_edges,
        [
            ((half, hidden), f32),
            ((half, features), f32),
            ((half + nodes, features), bf16),
            ((nodes, features), bf16),
            ((nodes, hidden), f32),
        ],
        [latents, pre, pick, take, *e_in, *e_out, *n_in],
        scratch=[((table, features), bf16)],
    )
    normed, inverse, next_mine, next_sent, aggregate, lat_all, extra = stage(
        functools.partial(update_edges, groups),
        [
            ((half, features), f32),
            ((half, 1), f32),
            ((half, width), bf16),
            ((half, width), bf16),
            ((nodes, features), f32),
            ((nodes, features), f32),
            ((half + 2 * nodes, features), bf16),
        ],
        [part, lat, *over_groups(sent), *packs, extra_came, state, take],
        scratch=[((half, features), bf16)],
    )
    aggregate2 = over_cores(aggregate)
    next_came = over_cores(next_sent)
    node_next, kept, *sents, dpre, node_dpre = stage(
        functools.partial(turn, groups),
        [((nodes, width), bf16), ((half, wide), f32)]
        + [((half, wide), bf16)] * (groups - 1)
        + [((half, hidden), bf16), ((nodes, hidden), bf16)],
        [*far, aggregate, aggregate2, own, lat_all, extra, take, normed, inverse, edge_pre]
        + [*e_in, *e_out, *n_in, *n_out],
        scratch=[((nodes, features), bf16), ((half, features), f32)],
    )
    sents = [swapped(s, cores * k) for k, s in enumerate(sents, 1)]
    (spread,) = stage(
        spread_nodes,
        [((blocks * feats, nodes, width), bf16)],
        [dpre, node_dpre, pick, take, *e_in, *n_in],
        scratch=[((table, features), f32)],
    )
    shares = lax.all_to_all(spread, everyone, 0, 0)
    grad_mine, grad_sent = stage(
        functools.partial(add_groups, groups),
        [((half, width), bf16), ((half, width), bf16)],
        [kept, *sents],
    )
    edge_next, edge_grad = stage(
        assemble,
        [((edge_dev, width), bf16), ((edge_dev, width), bf16)],
        [next_mine, next_came, grad_mine, over_cores(grad_sent)],
    )
    (node_grad,) = stage(add_nodes, [((nodes, width), bf16)], [shares, node_cot])
    return (edge_next, node_next, edge_grad, node_grad)


def solution(mesh):
    rows = P(("groups", "nodes"), "feat")
    flat = P(("groups", "nodes"))
    matrix = P("feat", None)
    vector = P("feat")
    return jax.shard_map(
        shards,
        mesh=mesh,
        in_specs=(
            rows,
            rows,
            P("groups", None, None),
            flat,
            flat,
            matrix,
            matrix,
            vector,
            matrix,
            matrix,
            vector,
            rows,
            rows,
        ),
        out_specs=(rows, rows, rows, rows),
        check_vma=False,
    )
```

```python
import functools

import jax
import jax.numpy as jnp
from jax import lax
from jax.experimental import pallas as pl
from jax.experimental.pallas import tpu as pltpu
from jax.sharding import PartitionSpec as P

epsilon = 1e-05
f32 = jnp.float32
bf16 = jnp.bfloat16
cores = 2
kernel_vmem = 8 << 20


def dot(left, right):
    return jnp.dot(left, right, preferred_element_type=f32)


def dot_rows(left, right):
    return lax.dot_general(left, right, (((1,), (1,)), ((), ())), preferred_element_type=f32)


def dot_cols(left, right):
    return lax.dot_general(left, right, (((0,), (0,)), ((), ())), preferred_element_type=f32)


def split(values):
    high = values.astype(bf16)
    return high, (values - high.astype(f32)).astype(bf16)


def sigmoid(values):
    return 1.0 / (1.0 + jnp.exp(-values))


def swish_slope(pre_act):
    sigma = sigmoid(pre_act)
    return sigma * (1.0 + pre_act * (1.0 - sigma))


def normalize(values):
    mean = jnp.mean(values, axis=1, keepdims=True)
    square = jnp.mean(values * values, axis=1, keepdims=True)
    inverse = lax.rsqrt(square - mean * mean + epsilon)
    return (values - mean) * inverse, inverse


def norm_back(grad, normed, inverse):
    total = jnp.mean(grad, axis=1, keepdims=True)
    cross = jnp.mean(grad * normed, axis=1, keepdims=True)
    return inverse * (grad - total - normed * cross)


def place():
    feat = lax.axis_index("feat")
    return feat // cores, feat % cores


def pair(mine, other, core):
    return jnp.where(core == 0, jnp.concatenate([mine, other], 1), jnp.concatenate([other, mine], 1))


def lanes(group, width):
    return pl.ds(pl.multiple_of(group * width, width), width)


def stage(kernel, outs, operands, scalars=0, scratch=(), flops=1 << 24):
    specs = [pl.BlockSpec(memory_space=pltpu.VMEM)] * (len(operands) - scalars)
    specs += [pl.BlockSpec(memory_space=pltpu.SMEM)] * scalars
    moved = sum(o.size * o.dtype.itemsize for o in operands)
    return pl.pallas_call(
        kernel,
        out_shape=[jax.ShapeDtypeStruct(shape, kind) for shape, kind in outs],
        in_specs=specs,
        out_specs=[pl.BlockSpec(memory_space=pltpu.VMEM)] * len(outs),
        scratch_shapes=[pltpu.VMEM(shape, kind) for shape, kind in scratch],
        cost_estimate=pl.CostEstimate(flops=flops, bytes_accessed=moved, transcendentals=0),
        compiler_params=pltpu.CompilerParams(vmem_limit_bytes=kernel_vmem),
    )(*operands)


def gains(gain_e, gain_n, rows):
    shape = (rows, gain_e.shape[1])
    row = lax.broadcasted_iota(jnp.int32, shape, 0)
    e = jnp.broadcast_to(gain_e[...].astype(f32), shape)
    n = jnp.broadcast_to(gain_n[...].astype(f32), shape)
    return jnp.where(row == 0, e, n).astype(bf16)


def total(refs):
    value = refs[0][...]
    for ref in refs[1:]:
        value = value + ref[...].astype(f32)
    return value


def spread_latent(latent, spread):
    spread[...] = jnp.broadcast_to(latent[...][None], spread.shape)


def pack_extra(edge_cot, node_cot, gain_e, gain_n, pack):
    edge_dev = edge_cot.shape[0]
    nodes = node_cot.shape[0]
    pack[:edge_dev] = edge_cot[...]
    pack[edge_dev : edge_dev + nodes] = node_cot[...]
    pack[edge_dev + nodes :] = gains(gain_e, gain_n, nodes)


def half_rows(pack, core, half):
    rows = pack[pl.ds(pl.multiple_of(core * half, half), half)]
    if pack.shape[0] == cores * half:
        return rows
    return jnp.concatenate([rows, pack[cores * half :]], axis=0)


def send_half(groups, *refs):
    packs, sent = refs[:groups], refs[groups]
    _, core = place()
    width = packs[0].shape[1]
    half = packs[0].shape[0] - sent.shape[0]
    for step, pack in enumerate(packs):
        sent[:, step * width : (step + 1) * width] = half_rows(pack, 1 - core, half)


def prepare_edges(groups, *refs):
    packs = refs[:groups]
    theirs, mine, other, slot, receiver, send_rows, state, pre, pick, take = refs[groups:]
    group, core = place()
    block = lax.axis_index("nodes")
    features = state.shape[1]
    nodes, half = take.shape
    width = packs[0].shape[1]
    blocks, _, slots = send_rows.shape
    for step, pack in enumerate(packs):
        both = pair(half_rows(pack, core, half), theirs[:, step * width : (step + 1) * width], core)
        state[:, lanes(group ^ step, width * cores)] = both

    slot_row = slot[pl.ds(core, 1)]
    sender = block * nodes + slot_row
    for source in range(blocks):
        for k in range(slots):
            row = source * nodes + send_rows[source, block, k]
            sender = jnp.where(slot_row == nodes + source * slots + k, row, sender)
    pick[...] = (lax.broadcasted_iota(jnp.int32, pick.shape, 0) == sender).astype(f32).astype(bf16)
    here = receiver[pl.ds(core, 1)]
    take[...] = (lax.broadcasted_iota(jnp.int32, take.shape, 0) == here).astype(f32).astype(bf16)
    weight = jnp.concatenate([mine[:, :features], other[:, :features]], axis=0)
    pre[...] = dot_rows(state[...], weight)


def finish_edges(came, pre, pick, take, mine, other, out_mine, out_other, n_mine, n_other, edge_pre, part, sent, own, lat, table):
    block = lax.axis_index("nodes")
    count, nodes, width = came.shape
    rows, features = table.shape
    half, hidden = pre.shape
    feats = features // width
    for source in range(count):
        first, column = source // feats * nodes, source % feats * width
        table[first : first + nodes, column : column + width] = came[source]
    latent = table[pl.ds(pl.multiple_of(block * nodes, nodes), nodes)]
    own[...] = latent

    def weight(index):
        columns = slice(index * features, (index + 1) * features)
        return jnp.concatenate([mine[:, columns], other[:, columns]], axis=0)

    high, low = split(dot_rows(table[...], weight(1)))
    here_high, here_low = split(dot_rows(latent, weight(2)))
    chosen = jnp.concatenate([pick[...], pick[...], take[...], take[...]], axis=0)
    value = pre[...] + dot_cols(chosen, jnp.concatenate([high, low, here_high, here_low], axis=0))
    edge_pre[...] = value
    act = (value * sigmoid(value)).astype(bf16)
    out = dot(act, jnp.concatenate([out_mine[...], out_other[...]], axis=0))
    part[...] = out
    sent[:half] = out.astype(bf16)
    nodes_pre = dot_rows(latent, jnp.concatenate([n_mine[:, :features], n_other[:, :features]], axis=0))
    lat[...] = nodes_pre
    high, low = split(nodes_pre)
    sent[half:] = jnp.zeros((nodes, features), bf16)
    sent[half:, :hidden] = high
    sent[half:, hidden : 2 * hidden] = low


def update_edges(groups, *refs):
    part, lat, came, packs = refs[0], refs[1], refs[2 : groups + 1], refs[groups + 1 : 2 * groups + 1]
    theirs, state, take, normed, inverse, kept, lent, aggregate, lat_all, extra, next_all = refs[2 * groups + 1 :]
    group, core = place()
    nodes, half = take.shape
    width = kept.shape[1]
    hidden = lat.shape[1]
    for step, pack in enumerate(packs):
        both = pair(half_rows(pack, core, half), theirs[:, step * width : (step + 1) * width], core)
        extra[:, lanes(group ^ step, width * cores)] = both
    value = part[...]
    lat_all[:, :hidden] = lat[...]
    for step, ref in enumerate(came, 1):
        value = value + ref[:half].astype(f32)
        high, low = ref[half:, :hidden], ref[half:, hidden : 2 * hidden]
        lat_all[:, step * hidden : (step + 1) * hidden] = high.astype(f32) + low.astype(f32)
    normed_rows, inverse_rows = normalize(value)
    normed[...] = normed_rows
    inverse[...] = inverse_rows
    gain = extra[half + nodes :].astype(f32)[0:1]
    rows = (state[...].astype(f32) + normed_rows * gain).astype(bf16)
    aggregate[...] = dot(take[...], rows)
    next_all[...] = rows
    mine = next_all[:, lanes(group, width * cores)]
    kept[...] = jnp.where(core == 0, mine[:, :width], mine[:, width:])
    lent[...] = jnp.where(core == 0, mine[:, width:], mine[:, :width])


def turn(groups, *refs):
    far, refs = refs[: 2 * (groups - 1)], refs[2 * (groups - 1) :]
    aggregate, aggregate2, own, lat_all, extra, take, pick, normed, inverse, edge_pre = refs[:10]
    e_mine, e_other, out_mine, out_other, in_mine, in_other, n_mine, n_other = refs[10:18]
    node_next, dpre_ref, total_ref, spread, next_all, grads = refs[18:]
    group, core = place()
    block = lax.axis_index("nodes")
    nodes, half = take.shape
    features = extra.shape[1]
    hidden = edge_pre.shape[1]
    width = node_next.shape[1]
    wide = width * cores
    gain_rows = extra[half + nodes :].astype(f32)
    edge_gain, node_gain = gain_rows[0:1], gain_rows[1:2]

    from_agg = jnp.concatenate(
        [in_mine[:, features:], in_other[:, features:]] + [f[:, :features] for f in far], axis=0
    )
    to_out = jnp.concatenate([n_mine[...], n_other[...]] + [f[:, features:] for f in far], axis=0)
    together = (aggregate[...] + aggregate2[...]).astype(bf16)
    pre = lat_all[...] + dot_rows(together, from_agg)
    act = (pre * sigmoid(pre)).astype(bf16)
    node_normed, node_inverse = normalize(dot(act, to_out))
    next_all[...] = (own[...].astype(f32) + node_normed * node_gain).astype(bf16)
    mine = next_all[:, lanes(group, wide)]
    node_next[...] = jnp.where(core == 0, mine[:, :width], mine[:, width:])
    cot = extra[half : half + nodes].astype(f32)
    node_dy = norm_back(cot * node_gain, node_normed, node_inverse).astype(bf16)
    node_dpre = (dot_rows(node_dy, to_out) * swish_slope(pre)).astype(bf16)
    high, low = split(dot(node_dpre, from_agg))

    taken = take[...]
    edge_total = extra[:half].astype(f32) + dot_cols(
        jnp.concatenate([taken, taken], axis=0), jnp.concatenate([high, low], axis=0)
    )
    dy = norm_back(edge_total * edge_gain, normed[...], inverse[...]).astype(bf16)
    back = dot_rows(dy, jnp.concatenate([out_mine[...], out_other[...]], axis=0))
    dpre = (back * swish_slope(edge_pre[...])).astype(bf16)

    dpre_ref[...] = dpre
    total_ref[...] = edge_total

    def weighted(values, index):
        columns = slice(index * features, (index + 1) * features)
        weight = jnp.concatenate([e_mine[:, columns], e_other[:, columns]], axis=0)
        both = dot(jnp.concatenate(split(values), axis=0), weight)
        return both[: values.shape[0]] + both[values.shape[0] :]

    grads[...] = weighted(dot(pick[...], dpre), 1)
    home = weighted(dot(taken, dpre), 2)
    node_weight = jnp.concatenate([in_mine[:, :features], in_other[:, :features]], axis=0)
    home = home + 0.5 * dot(node_dpre[:, :hidden], node_weight)
    grads[pl.ds(pl.multiple_of(block * nodes, nodes), nodes)] += home
    feats = features // width
    for target in range(spread.shape[0]):
        first, column = target // feats * nodes, target % feats * width
        spread[target] = grads[first : first + nodes, column : column + width].astype(bf16)


def turn_edges(dpre, edge_total, e_mine, e_other, kept, *refs):
    *sents, grads = refs
    group, _ = place()
    features = edge_total.shape[1]
    wide = kept.shape[1]
    grads[...] = dot(dpre[...], jnp.concatenate([e_mine[:, :features], e_other[:, :features]], axis=0))
    for step, sent in enumerate(sents, 1):
        sent[...] = grads[:, lanes(group ^ step, wide)].astype(bf16)
    kept[...] = grads[:, lanes(group, wide)] + edge_total[:, lanes(group, wide)]


def add_groups(groups, *refs):
    parts, (kept, sent) = refs[:groups], refs[groups:]
    _, core = place()
    width = kept.shape[1]
    value = total(parts)
    kept[...] = jnp.where(core == 0, value[:, :width], value[:, width:]).astype(bf16)
    sent[...] = jnp.where(core == 0, value[:, width:], value[:, :width]).astype(bf16)


def add_nodes(shares, node_cot, node_grad):
    value = node_cot[...].astype(f32)
    for source in range(shares.shape[0]):
        value = value + shares[source].astype(f32)
    node_grad[...] = value.astype(bf16)


def assemble(next_mine, next_came, grad_mine, grad_came, edge_next, edge_grad):
    _, core = place()
    half = next_mine.shape[0]
    mine = pl.ds(pl.multiple_of(core * half, half), half)
    theirs = pl.ds(pl.multiple_of((1 - core) * half, half), half)
    edge_next[mine] = next_mine[...]
    edge_next[theirs] = next_came[...]
    edge_grad[mine] = grad_mine[...]
    edge_grad[theirs] = grad_came[...]


def shards(
    latent,
    edge_state,
    send_rows,
    sender_slot,
    receiver_row,
    edge_in_weight,
    edge_out_weight,
    edge_gain,
    node_in_weight,
    node_out_weight,
    node_gain,
    edge_cot,
    node_cot,
):
    nodes, width = latent.shape
    edge_dev = edge_state.shape[0]
    half = edge_dev // cores
    blocks = send_rows.shape[0]
    feats = lax.axis_size("feat")
    groups = feats // cores
    features = width * feats
    wide = width * cores
    hidden = edge_in_weight.shape[0] * cores
    table = blocks * nodes
    everyone = ("nodes", "feat")

    def swapped(values, bits):
        return lax.ppermute(values, "feat", [(i, i ^ bits) for i in range(feats)])

    def over_cores(values):
        return swapped(values, 1)

    def over_groups(values):
        return [swapped(values, cores * step) for step in range(1, groups)]

    gain_e, gain_n = edge_gain.reshape(1, width), node_gain.reshape(1, width)
    slot_rows = sender_slot.reshape(cores, half)
    receiver_rows = receiver_row.reshape(cores, half)

    (spread,) = stage(spread_latent, [((blocks * feats, nodes, width), bf16)], [latent])
    latents = lax.all_to_all(spread, everyone, 0, 0)
    states = [edge_state] + over_groups(edge_state)
    e_in = (edge_in_weight, over_cores(edge_in_weight))
    e_out = (edge_out_weight, over_cores(edge_out_weight))
    n_in = (node_in_weight, over_cores(node_in_weight))
    n_out = (node_out_weight, over_cores(node_out_weight))
    far = []
    for weights in over_groups(jnp.concatenate([node_in_weight[:, features:], node_out_weight], axis=1)):
        far += [weights, over_cores(weights)]
    (sent,) = stage(functools.partial(send_half, groups), [((half, groups * width), bf16)], states)
    state, pre, pick, take = stage(
        functools.partial(prepare_edges, groups),
        [((half, features), bf16), ((half, hidden), f32), ((table, half), bf16), ((nodes, half), bf16)],
        [*states, over_cores(sent), *e_in, slot_rows, receiver_rows, send_rows],
        scalars=1,
    )
    rows = edge_dev + 2 * nodes
    (pack,) = stage(pack_extra, [((rows, width), bf16)], [edge_cot, node_cot, gain_e, gain_n])
    packs = [pack] + over_groups(pack)
    (sent,) = stage(functools.partial(send_half, groups), [((rows - half, groups * width), bf16)], packs)
    extra_came = over_cores(sent)
    edge_pre, part, sent, own, lat = stage(
        finish_edges,
        [
            ((half, hidden), f32),
            ((half, features), f32),
            ((half + nodes, features), bf16),
            ((nodes, features), bf16),
            ((nodes, hidden), f32),
        ],
        [latents, pre, pick, take, *e_in, *e_out, *n_in],
        scratch=[((table, features), bf16)],
    )
    normed, inverse, next_mine, next_sent, aggregate, lat_all, extra = stage(
        functools.partial(update_edges, groups),
        [
            ((half, features), f32),
            ((half, 1), f32),
            ((half, width), bf16),
            ((half, width), bf16),
            ((nodes, features), f32),
            ((nodes, features), f32),
            ((half + 2 * nodes, features), bf16),
        ],
        [part, lat, *over_groups(sent), *packs, extra_came, state, take],
        scratch=[((half, features), bf16)],
    )
    aggregate2 = over_cores(aggregate)
    next_came = over_cores(next_sent)
    node_next, dpre, edge_total, spread = stage(
        functools.partial(turn, groups),
        [
            ((nodes, width), bf16),
            ((half, hidden), bf16),
            ((half, features), f32),
            ((blocks * feats, nodes, width), bf16),
        ],
        [*far, aggregate, aggregate2, own, lat_all, extra, take, pick, normed, inverse, edge_pre]
        + [*e_in, *e_out, *n_in, *n_out],
        scratch=[((nodes, features), bf16), ((table, features), f32)],
    )
    kept, *sents = stage(
        turn_edges,
        [((half, wide), f32)] + [((half, wide), bf16)] * (groups - 1),
        [dpre, edge_total, *e_in],
        scratch=[((half, features), f32)],
    )
    sents = [swapped(s, cores * k) for k, s in enumerate(sents, 1)]
    shares = lax.all_to_all(spread, everyone, 0, 0)
    grad_mine, grad_sent = stage(
        functools.partial(add_groups, groups),
        [((half, width), bf16), ((half, width), bf16)],
        [kept, *sents],
    )
    edge_next, edge_grad = stage(
        assemble,
        [((edge_dev, width), bf16), ((edge_dev, width), bf16)],
        [next_mine, next_came, grad_mine, over_cores(grad_sent)],
    )
    (node_grad,) = stage(add_nodes, [((nodes, width), bf16)], [shares, node_cot])
    return (edge_next, node_next, edge_grad, node_grad)


def solution(mesh):
    rows = P(("groups", "nodes"), "feat")
    flat = P(("groups", "nodes"))
    matrix = P("feat", None)
    vector = P("feat")
    return jax.shard_map(
        shards,
        mesh=mesh,
        in_specs=(
            rows,
            rows,
            P("groups", None, None),
            flat,
            flat,
            matrix,
            matrix,
            vector,
            matrix,
            matrix,
            vector,
            rows,
            rows,
        ),
        out_specs=(rows, rows, rows, rows),
        check_vma=False,
    )
```

```python
import functools

import jax
import jax.numpy as jnp
from jax import lax
from jax.experimental import pallas as pl
from jax.experimental.pallas import tpu as pltpu
from jax.sharding import PartitionSpec as P

epsilon = 1e-05
f32 = jnp.float32
bf16 = jnp.bfloat16
cores = 2
kernel_vmem = 8 << 20


def dot(left, right):
    return jnp.dot(left, right, preferred_element_type=f32)


def dot_rows(left, right):
    return lax.dot_general(left, right, (((1,), (1,)), ((), ())), preferred_element_type=f32)


def dot_cols(left, right):
    return lax.dot_general(left, right, (((0,), (0,)), ((), ())), preferred_element_type=f32)


def split(values):
    high = values.astype(bf16)
    return high, (values - high.astype(f32)).astype(bf16)


def sigmoid(values):
    return 1.0 / (1.0 + jnp.exp(-values))


def swish_slope(pre_act):
    sigma = sigmoid(pre_act)
    return sigma * (1.0 + pre_act * (1.0 - sigma))


def normalize(values):
    mean = jnp.mean(values, axis=1, keepdims=True)
    square = jnp.mean(values * values, axis=1, keepdims=True)
    inverse = lax.rsqrt(square - mean * mean + epsilon)
    return (values - mean) * inverse, inverse


def norm_back(grad, normed, inverse):
    total = jnp.mean(grad, axis=1, keepdims=True)
    cross = jnp.mean(grad * normed, axis=1, keepdims=True)
    return inverse * (grad - total - normed * cross)


def place():
    feat = lax.axis_index("feat")
    return feat // cores, feat % cores


def pair(mine, other, core):
    return jnp.where(core == 0, jnp.concatenate([mine, other], 1), jnp.concatenate([other, mine], 1))


def lanes(group, width):
    return pl.ds(pl.multiple_of(group * width, width), width)


def stage(kernel, outs, operands, scalars=0, scratch=(), flops=1 << 24):
    specs = [pl.BlockSpec(memory_space=pltpu.VMEM)] * (len(operands) - scalars)
    specs += [pl.BlockSpec(memory_space=pltpu.SMEM)] * scalars
    moved = sum(o.size * o.dtype.itemsize for o in operands)
    return pl.pallas_call(
        kernel,
        out_shape=[jax.ShapeDtypeStruct(shape, kind) for shape, kind in outs],
        in_specs=specs,
        out_specs=[pl.BlockSpec(memory_space=pltpu.VMEM)] * len(outs),
        scratch_shapes=[pltpu.VMEM(shape, kind) for shape, kind in scratch],
        cost_estimate=pl.CostEstimate(flops=flops, bytes_accessed=moved, transcendentals=0),
        compiler_params=pltpu.CompilerParams(vmem_limit_bytes=kernel_vmem),
    )(*operands)


def gains(gain_e, gain_n, rows):
    shape = (rows, gain_e.shape[1])
    row = lax.broadcasted_iota(jnp.int32, shape, 0)
    e = jnp.broadcast_to(gain_e[...].astype(f32), shape)
    n = jnp.broadcast_to(gain_n[...].astype(f32), shape)
    return jnp.where(row == 0, e, n).astype(bf16)


def total(refs):
    value = refs[0][...]
    for ref in refs[1:]:
        value = value + ref[...].astype(f32)
    return value


def spread_latent(block, spread):
    _, nodes, width = spread.shape
    spread[...] = jnp.broadcast_to(block[:nodes, block.shape[1] - width :][None], spread.shape)


def pack_extra(edge_cot, node_cot, gain_e, gain_n, pack):
    edge_dev = edge_cot.shape[0]
    nodes = node_cot.shape[0]
    pack[:edge_dev] = edge_cot[...]
    pack[edge_dev : edge_dev + nodes] = node_cot[...]
    pack[edge_dev + nodes :] = gains(gain_e, gain_n, nodes)


def half_rows(pack, core, half):
    rows = pack[pl.ds(pl.multiple_of(core * half, half), half)]
    if pack.shape[0] == cores * half:
        return rows
    return jnp.concatenate([rows, pack[cores * half :]], axis=0)


def send_half(groups, *refs):
    packs, sent = refs[:groups], refs[groups]
    _, core = place()
    width = packs[0].shape[1]
    half = packs[0].shape[0] - sent.shape[0]
    for step, pack in enumerate(packs):
        sent[:, step * width : (step + 1) * width] = half_rows(pack, 1 - core, half)


def prepare_edges(groups, *refs):
    packs = refs[:groups]
    theirs, mine, other, slot, receiver, send_rows, state, pre, pick, take = refs[groups:]
    group, core = place()
    block = lax.axis_index("nodes")
    features = state.shape[1]
    nodes, half = take.shape
    width = packs[0].shape[1]
    blocks, _, slots = send_rows.shape
    for step, pack in enumerate(packs):
        both = pair(half_rows(pack, core, half), theirs[:, step * width : (step + 1) * width], core)
        state[:, lanes(group ^ step, width * cores)] = both

    slot_row = slot[pl.ds(core, 1)]
    sender = block * nodes + slot_row
    for source in range(blocks):
        for k in range(slots):
            row = source * nodes + send_rows[source, block, k]
            sender = jnp.where(slot_row == nodes + source * slots + k, row, sender)
    pick[...] = (lax.broadcasted_iota(jnp.int32, pick.shape, 0) == sender).astype(f32).astype(bf16)
    here = receiver[pl.ds(core, 1)]
    take[...] = (lax.broadcasted_iota(jnp.int32, take.shape, 0) == here).astype(f32).astype(bf16)
    weight = jnp.concatenate([mine[:, :features], other[:, :features]], axis=0)
    pre[...] = dot_rows(state[...], weight)


def finish_edges(came, pre, pick, take, mine, other, out_mine, out_other, n_mine, n_other, edge_pre, part, sent, own, lat, table):
    block = lax.axis_index("nodes")
    count, nodes, width = came.shape
    rows, features = table.shape
    half, hidden = pre.shape
    feats = features // width
    for source in range(count):
        first, column = source // feats * nodes, source % feats * width
        table[first : first + nodes, column : column + width] = came[source]
    latent = table[pl.ds(pl.multiple_of(block * nodes, nodes), nodes)]
    own[...] = latent

    def weight(index):
        columns = slice(index * features, (index + 1) * features)
        return jnp.concatenate([mine[:, columns], other[:, columns]], axis=0)

    high, low = split(dot_rows(table[...], weight(1)))
    here_high, here_low = split(dot_rows(latent, weight(2)))
    chosen = jnp.concatenate([pick[...], pick[...], take[...], take[...]], axis=0)
    value = pre[...] + dot_cols(chosen, jnp.concatenate([high, low, here_high, here_low], axis=0))
    edge_pre[...] = value
    act = (value * sigmoid(value)).astype(bf16)
    out = dot(act, jnp.concatenate([out_mine[...], out_other[...]], axis=0))
    part[...] = out
    sent[:half] = out.astype(bf16)
    nodes_pre = dot_rows(latent, jnp.concatenate([n_mine[:, :features], n_other[:, :features]], axis=0))
    lat[...] = nodes_pre
    high, low = split(nodes_pre)
    sent[half:] = jnp.zeros((nodes, features), bf16)
    sent[half:, :hidden] = high
    sent[half:, hidden : 2 * hidden] = low


def update_edges(groups, *refs):
    part, lat, came, packs = refs[0], refs[1], refs[2 : groups + 1], refs[groups + 1 : 2 * groups + 1]
    theirs, state, take, normed, inverse, kept, lent, aggregate, lat_all, extra, next_all = refs[2 * groups + 1 :]
    group, core = place()
    nodes, half = take.shape
    width = kept.shape[1]
    hidden = lat.shape[1]
    for step, pack in enumerate(packs):
        both = pair(half_rows(pack, core, half), theirs[:, step * width : (step + 1) * width], core)
        extra[:, lanes(group ^ step, width * cores)] = both
    value = part[...]
    lat_all[:, :hidden] = lat[...]
    for step, ref in enumerate(came, 1):
        value = value + ref[:half].astype(f32)
        high, low = ref[half:, :hidden], ref[half:, hidden : 2 * hidden]
        lat_all[:, step * hidden : (step + 1) * hidden] = high.astype(f32) + low.astype(f32)
    normed_rows, inverse_rows = normalize(value)
    normed[...] = normed_rows
    inverse[...] = inverse_rows
    gain = extra[half + nodes :].astype(f32)[0:1]
    rows = (state[...].astype(f32) + normed_rows * gain).astype(bf16)
    aggregate[...] = dot(take[...], rows)
    next_all[...] = rows
    mine = next_all[:, lanes(group, width * cores)]
    kept[...] = jnp.where(core == 0, mine[:, :width], mine[:, width:])
    lent[...] = jnp.where(core == 0, mine[:, width:], mine[:, :width])


def turn(groups, *refs):
    far, refs = refs[: 2 * (groups - 1)], refs[2 * (groups - 1) :]
    aggregate, aggregate2, own, lat_all, extra, take, pick, normed, inverse, edge_pre = refs[:10]
    e_mine, e_other, out_mine, out_other, in_mine, in_other, n_mine, n_other = refs[10:18]
    node_next, dpre_ref, total_ref, spread, next_all, grads = refs[18:]
    group, core = place()
    block = lax.axis_index("nodes")
    nodes, half = take.shape
    features = extra.shape[1]
    hidden = edge_pre.shape[1]
    width = node_next.shape[1]
    wide = width * cores
    gain_rows = extra[half + nodes :].astype(f32)
    edge_gain, node_gain = gain_rows[0:1], gain_rows[1:2]

    from_agg = jnp.concatenate(
        [in_mine[:, features:], in_other[:, features:]] + [f[:, :features] for f in far], axis=0
    )
    to_out = jnp.concatenate([n_mine[...], n_other[...]] + [f[:, features : 2 * features] for f in far], axis=0)
    together = (aggregate[...] + aggregate2[...]).astype(bf16)
    pre = lat_all[...] + dot_rows(together, from_agg)
    act = (pre * sigmoid(pre)).astype(bf16)
    node_normed, node_inverse = normalize(dot(act, to_out))
    next_all[...] = (own[...].astype(f32) + node_normed * node_gain).astype(bf16)
    mine = next_all[:, lanes(group, wide)]
    node_next[...] = jnp.where(core == 0, mine[:, :width], mine[:, width:])
    cot = extra[half : half + nodes].astype(f32)
    node_dy = norm_back(cot * node_gain, node_normed, node_inverse).astype(bf16)
    node_dpre = (dot_rows(node_dy, to_out) * swish_slope(pre)).astype(bf16)
    high, low = split(dot(node_dpre, from_agg))

    taken = take[...]
    edge_total = extra[:half].astype(f32) + dot_cols(
        jnp.concatenate([taken, taken], axis=0), jnp.concatenate([high, low], axis=0)
    )
    dy = norm_back(edge_total * edge_gain, normed[...], inverse[...]).astype(bf16)
    back = dot_rows(dy, jnp.concatenate([out_mine[...], out_other[...]], axis=0))
    dpre = (back * swish_slope(edge_pre[...])).astype(bf16)

    dpre_ref[...] = dpre
    total_ref[...] = edge_total

    def weighted(values, index):
        columns = slice(index * features, (index + 1) * features)
        weight = jnp.concatenate([e_mine[:, columns], e_other[:, columns]], axis=0)
        both = dot(jnp.concatenate(split(values), axis=0), weight)
        return both[: values.shape[0]] + both[values.shape[0] :]

    grads[...] = weighted(dot(pick[...], dpre), 1)
    home = weighted(dot(taken, dpre), 2)
    node_weight = jnp.concatenate([in_mine[:, :features], in_other[:, :features]], axis=0)
    home = home + 0.5 * dot(node_dpre[:, :hidden], node_weight)
    grads[pl.ds(pl.multiple_of(block * nodes, nodes), nodes)] += home
    feats = features // width
    for target in range(spread.shape[0]):
        first, column = target // feats * nodes, target % feats * width
        spread[target] = grads[first : first + nodes, column : column + width].astype(bf16)


def turn_edges(dpre, edge_total, e_mine, e_other, kept, *refs):
    *sents, grads = refs
    group, _ = place()
    features = edge_total.shape[1]
    wide = kept.shape[1]
    grads[...] = dot(dpre[...], jnp.concatenate([e_mine[:, :features], e_other[:, :features]], axis=0))
    for step, sent in enumerate(sents, 1):
        sent[...] = grads[:, lanes(group ^ step, wide)].astype(bf16)
    kept[...] = grads[:, lanes(group, wide)] + edge_total[:, lanes(group, wide)]


def add_groups(groups, *refs):
    parts, (kept, sent) = refs[:groups], refs[groups:]
    _, core = place()
    width = kept.shape[1]
    value = total(parts)
    kept[...] = jnp.where(core == 0, value[:, :width], value[:, width:]).astype(bf16)
    sent[...] = jnp.where(core == 0, value[:, width:], value[:, :width]).astype(bf16)


def add_nodes(shares, node_cot, node_grad):
    value = node_cot[...].astype(f32)
    for source in range(shares.shape[0]):
        value = value + shares[source].astype(f32)
    node_grad[...] = value.astype(bf16)


def assemble(next_mine, next_came, grad_mine, grad_came, edge_next, edge_grad):
    _, core = place()
    half = next_mine.shape[0]
    mine = pl.ds(pl.multiple_of(core * half, half), half)
    theirs = pl.ds(pl.multiple_of((1 - core) * half, half), half)
    edge_next[mine] = next_mine[...]
    edge_next[theirs] = next_came[...]
    edge_grad[mine] = grad_mine[...]
    edge_grad[theirs] = grad_came[...]


def shards(
    latent,
    edge_state,
    send_rows,
    sender_slot,
    receiver_row,
    edge_in_weight,
    edge_out_weight,
    edge_gain,
    node_in_weight,
    node_out_weight,
    node_gain,
    edge_cot,
    node_cot,
):
    nodes, width = latent.shape
    edge_dev = edge_state.shape[0]
    half = edge_dev // cores
    blocks = send_rows.shape[0]
    feats = lax.axis_size("feat")
    groups = feats // cores
    features = width * feats
    wide = width * cores
    hidden = edge_in_weight.shape[0] * cores
    table = blocks * nodes
    everyone = ("nodes", "feat")

    def swapped(values, bits):
        return lax.ppermute(values, "feat", [(i, i ^ bits) for i in range(feats)])

    def over_cores(values):
        return swapped(values, 1)

    def over_groups(values):
        return [swapped(values, cores * step) for step in range(1, groups)]

    gain_e, gain_n = edge_gain.reshape(1, width), node_gain.reshape(1, width)
    slot_rows = sender_slot.reshape(cores, half)
    receiver_rows = receiver_row.reshape(cores, half)

    hid = edge_in_weight.shape[0]
    block = jnp.concatenate(
        [node_in_weight[:, features:], node_out_weight, jnp.pad(latent, ((0, hid - nodes), (0, 0)))], axis=1
    )
    (spread,) = stage(spread_latent, [((blocks * feats, nodes, width), bf16)], [block])
    latents = lax.all_to_all(spread, everyone, 0, 0)
    states = [edge_state] + over_groups(edge_state)
    e_in = (edge_in_weight, over_cores(edge_in_weight))
    e_out = (edge_out_weight, over_cores(edge_out_weight))
    n_in = (node_in_weight, over_cores(node_in_weight))
    n_out = (node_out_weight, over_cores(node_out_weight))
    far = []
    for weights in over_groups(block):
        far += [weights, over_cores(weights)]
    (sent,) = stage(functools.partial(send_half, groups), [((half, groups * width), bf16)], states)
    state, pre, pick, take = stage(
        functools.partial(prepare_edges, groups),
        [((half, features), bf16), ((half, hidden), f32), ((table, half), bf16), ((nodes, half), bf16)],
        [*states, over_cores(sent), *e_in, slot_rows, receiver_rows, send_rows],
        scalars=1,
    )
    rows = edge_dev + 2 * nodes
    (pack,) = stage(pack_extra, [((rows, width), bf16)], [edge_cot, node_cot, gain_e, gain_n])
    packs = [pack] + over_groups(pack)
    (sent,) = stage(functools.partial(send_half, groups), [((rows - half, groups * width), bf16)], packs)
    extra_came = over_cores(sent)
    edge_pre, part, sent, own, lat = stage(
        finish_edges,
        [
            ((half, hidden), f32),
            ((half, features), f32),
            ((half + nodes, features), bf16),
            ((nodes, features), bf16),
            ((nodes, hidden), f32),
        ],
        [latents, pre, pick, take, *e_in, *e_out, *n_in],
        scratch=[((table, features), bf16)],
    )
    normed, inverse, next_mine, next_sent, aggregate, lat_all, extra = stage(
        functools.partial(update_edges, groups),
        [
            ((half, features), f32),
            ((half, 1), f32),
            ((half, width), bf16),
            ((half, width), bf16),
            ((nodes, features), f32),
            ((nodes, features), f32),
            ((half + 2 * nodes, features), bf16),
        ],
        [part, lat, *over_groups(sent), *packs, extra_came, state, take],
        scratch=[((half, features), bf16)],
    )
    aggregate2 = over_cores(aggregate)
    next_came = over_cores(next_sent)
    node_next, dpre, edge_total, spread = stage(
        functools.partial(turn, groups),
        [
            ((nodes, width), bf16),
            ((half, hidden), bf16),
            ((half, features), f32),
            ((blocks * feats, nodes, width), bf16),
        ],
        [*far, aggregate, aggregate2, own, lat_all, extra, take, pick, normed, inverse, edge_pre]
        + [*e_in, *e_out, *n_in, *n_out],
        scratch=[((nodes, features), bf16), ((table, features), f32)],
    )
    kept, *sents = stage(
        turn_edges,
        [((half, wide), f32)] + [((half, wide), bf16)] * (groups - 1),
        [dpre, edge_total, *e_in],
        scratch=[((half, features), f32)],
    )
    sents = [swapped(s, cores * k) for k, s in enumerate(sents, 1)]
    shares = lax.all_to_all(spread, everyone, 0, 0)
    grad_mine, grad_sent = stage(
        functools.partial(add_groups, groups),
        [((half, width), bf16), ((half, width), bf16)],
        [kept, *sents],
    )
    edge_next, edge_grad = stage(
        assemble,
        [((edge_dev, width), bf16), ((edge_dev, width), bf16)],
        [next_mine, next_came, grad_mine, over_cores(grad_sent)],
    )
    (node_grad,) = stage(add_nodes, [((nodes, width), bf16)], [shares, node_cot])
    return (edge_next, node_next, edge_grad, node_grad)


def solution(mesh):
    rows = P(("groups", "nodes"), "feat")
    flat = P(("groups", "nodes"))
    matrix = P("feat", None)
    vector = P("feat")
    return jax.shard_map(
        shards,
        mesh=mesh,
        in_specs=(
            rows,
            rows,
            P("groups", None, None),
            flat,
            flat,
            matrix,
            matrix,
            vector,
            matrix,
            matrix,
            vector,
            rows,
            rows,
        ),
        out_specs=(rows, rows, rows, rows),
        check_vma=False,
    )
```

```python
import functools

import jax
import jax.numpy as jnp
from jax import lax
from jax.experimental import pallas as pl
from jax.experimental.pallas import tpu as pltpu
from jax.sharding import PartitionSpec as P

epsilon = 1e-05
f32 = jnp.float32
bf16 = jnp.bfloat16
cores = 2
kernel_vmem = 8 << 20


def dot(left, right):
    return jnp.dot(left, right, preferred_element_type=f32)


def dot_rows(left, right):
    return lax.dot_general(left, right, (((1,), (1,)), ((), ())), preferred_element_type=f32)


def dot_cols(left, right):
    return lax.dot_general(left, right, (((0,), (0,)), ((), ())), preferred_element_type=f32)


def split(values):
    high = values.astype(bf16)
    return high, (values - high.astype(f32)).astype(bf16)


def sigmoid(values):
    return 1.0 / (1.0 + jnp.exp(-values))


def swish_slope(pre_act):
    sigma = sigmoid(pre_act)
    return sigma * (1.0 + pre_act * (1.0 - sigma))


def normalize(values):
    mean = jnp.mean(values, axis=1, keepdims=True)
    square = jnp.mean(values * values, axis=1, keepdims=True)
    inverse = lax.rsqrt(square - mean * mean + epsilon)
    return (values - mean) * inverse, inverse


def norm_back(grad, normed, inverse):
    total = jnp.mean(grad, axis=1, keepdims=True)
    cross = jnp.mean(grad * normed, axis=1, keepdims=True)
    return inverse * (grad - total - normed * cross)


def place():
    feat = lax.axis_index("feat")
    return feat // cores, feat % cores


def pair(mine, other, core):
    return jnp.where(core == 0, jnp.concatenate([mine, other], 1), jnp.concatenate([other, mine], 1))


def lanes(group, width):
    return pl.ds(pl.multiple_of(group * width, width), width)


def stage(kernel, outs, operands, scalars=0, scratch=(), flops=1 << 24):
    specs = [pl.BlockSpec(memory_space=pltpu.VMEM)] * (len(operands) - scalars)
    specs += [pl.BlockSpec(memory_space=pltpu.SMEM)] * scalars
    moved = sum(o.size * o.dtype.itemsize for o in operands)
    return pl.pallas_call(
        kernel,
        out_shape=[jax.ShapeDtypeStruct(shape, kind) for shape, kind in outs],
        in_specs=specs,
        out_specs=[pl.BlockSpec(memory_space=pltpu.VMEM)] * len(outs),
        scratch_shapes=[pltpu.VMEM(shape, kind) for shape, kind in scratch],
        cost_estimate=pl.CostEstimate(flops=flops, bytes_accessed=moved, transcendentals=0),
        compiler_params=pltpu.CompilerParams(vmem_limit_bytes=kernel_vmem),
    )(*operands)


def gains(gain_e, gain_n, rows):
    shape = (rows, gain_e.shape[1])
    row = lax.broadcasted_iota(jnp.int32, shape, 0)
    e = jnp.broadcast_to(gain_e[...].astype(f32), shape)
    n = jnp.broadcast_to(gain_n[...].astype(f32), shape)
    return jnp.where(row == 0, e, n).astype(bf16)


def total(refs):
    value = refs[0][...]
    for ref in refs[1:]:
        value = value + ref[...].astype(f32)
    return value


def spread_latent(latent, spread):
    spread[...] = jnp.broadcast_to(latent[...][None], spread.shape)


def pack_extra(edge_cot, node_cot, gain_e, gain_n, pack):
    edge_dev = edge_cot.shape[0]
    nodes = node_cot.shape[0]
    pack[:edge_dev] = edge_cot[...]
    pack[edge_dev : edge_dev + nodes] = node_cot[...]
    pack[edge_dev + nodes :] = gains(gain_e, gain_n, nodes)


def half_rows(pack, core, half):
    rows = pack[pl.ds(pl.multiple_of(core * half, half), half)]
    if pack.shape[0] == cores * half:
        return rows
    return jnp.concatenate([rows, pack[cores * half :]], axis=0)


def send_half(groups, *refs):
    packs, sent = refs[:groups], refs[groups]
    _, core = place()
    width = packs[0].shape[1]
    half = packs[0].shape[0] - sent.shape[0]
    for step, pack in enumerate(packs):
        sent[:, step * width : (step + 1) * width] = half_rows(pack, 1 - core, half)


def prepare_edges(groups, *refs):
    packs = refs[:groups]
    theirs, mine, other, slot, receiver, send_rows, state, pre, pick, take = refs[groups:]
    group, core = place()
    block = lax.axis_index("nodes")
    features = state.shape[1]
    nodes, half = take.shape
    width = packs[0].shape[1]
    blocks, _, slots = send_rows.shape
    for step, pack in enumerate(packs):
        both = pair(half_rows(pack, core, half), theirs[:, step * width : (step + 1) * width], core)
        state[:, lanes(group ^ step, width * cores)] = both

    slot_row = slot[pl.ds(core, 1)]
    sender = block * nodes + slot_row
    for source in range(blocks):
        for k in range(slots):
            row = source * nodes + send_rows[source, block, k]
            sender = jnp.where(slot_row == nodes + source * slots + k, row, sender)
    pick[...] = (lax.broadcasted_iota(jnp.int32, pick.shape, 0) == sender).astype(f32).astype(bf16)
    here = receiver[pl.ds(core, 1)]
    take[...] = (lax.broadcasted_iota(jnp.int32, take.shape, 0) == here).astype(f32).astype(bf16)
    weight = jnp.concatenate([mine[:, :features], other[:, :features]], axis=0)
    pre[...] = dot_rows(state[...], weight)


def finish_edges(came, pre, pick, take, mine, other, out_mine, out_other, n_mine, n_other, edge_pre, part, sent, own, lat, table):
    block = lax.axis_index("nodes")
    count, nodes, width = came.shape
    rows, features = table.shape
    half, hidden = pre.shape
    feats = features // width
    for source in range(count):
        first, column = source // feats * nodes, source % feats * width
        table[first : first + nodes, column : column + width] = came[source]
    latent = table[pl.ds(pl.multiple_of(block * nodes, nodes), nodes)]
    own[...] = latent

    def weight(index):
        columns = slice(index * features, (index + 1) * features)
        return jnp.concatenate([mine[:, columns], other[:, columns]], axis=0)

    high, low = split(dot_rows(table[...], weight(1)))
    here_high, here_low = split(dot_rows(latent, weight(2)))
    chosen = jnp.concatenate([pick[...], pick[...], take[...], take[...]], axis=0)
    value = pre[...] + dot_cols(chosen, jnp.concatenate([high, low, here_high, here_low], axis=0))
    edge_pre[...] = value
    act = (value * sigmoid(value)).astype(bf16)
    out = dot(act, jnp.concatenate([out_mine[...], out_other[...]], axis=0))
    part[...] = out
    sent[:half] = out.astype(bf16)
    nodes_pre = dot_rows(latent, jnp.concatenate([n_mine[:, :features], n_other[:, :features]], axis=0))
    lat[...] = nodes_pre
    high, low = split(nodes_pre)
    sent[half:] = jnp.zeros((nodes, features), bf16)
    sent[half:, :hidden] = high
    sent[half:, hidden : 2 * hidden] = low


def update_edges(groups, *refs):
    part, lat, came, packs = refs[0], refs[1], refs[2 : groups + 1], refs[groups + 1 : 2 * groups + 1]
    theirs, state, take, normed, inverse, kept, lent, aggregate, lat_all, extra, next_all = refs[2 * groups + 1 :]
    group, core = place()
    nodes, half = take.shape
    width = kept.shape[1]
    hidden = lat.shape[1]
    for step, pack in enumerate(packs):
        both = pair(half_rows(pack, core, half), theirs[:, step * width : (step + 1) * width], core)
        extra[:, lanes(group ^ step, width * cores)] = both
    value = part[...]
    lat_all[:, :hidden] = lat[...]
    for step, ref in enumerate(came, 1):
        value = value + ref[:half].astype(f32)
        high, low = ref[half:, :hidden], ref[half:, hidden : 2 * hidden]
        lat_all[:, step * hidden : (step + 1) * hidden] = high.astype(f32) + low.astype(f32)
    normed_rows, inverse_rows = normalize(value)
    normed[...] = normed_rows
    inverse[...] = inverse_rows
    gain = extra[half + nodes :].astype(f32)[0:1]
    rows = (state[...].astype(f32) + normed_rows * gain).astype(bf16)
    aggregate[...] = dot(take[...], rows)
    next_all[...] = rows
    mine = next_all[:, lanes(group, width * cores)]
    kept[...] = jnp.where(core == 0, mine[:, :width], mine[:, width:])
    lent[...] = jnp.where(core == 0, mine[:, width:], mine[:, :width])


def turn(groups, *refs):
    far, refs = refs[: 2 * (groups - 1)], refs[2 * (groups - 1) :]
    aggregate, aggregate2, own, lat_all, extra, take, pick, normed, inverse, edge_pre = refs[:10]
    e_mine, e_other, out_mine, out_other, in_mine, in_other, n_mine, n_other = refs[10:18]
    node_next, dpre_ref, total_ref, spread, next_all, grads = refs[18:]
    group, core = place()
    block = lax.axis_index("nodes")
    nodes, half = take.shape
    features = extra.shape[1]
    hidden = edge_pre.shape[1]
    width = node_next.shape[1]
    wide = width * cores
    gain_rows = extra[half + nodes :].astype(f32)
    edge_gain, node_gain = gain_rows[0:1], gain_rows[1:2]

    from_agg = jnp.concatenate(
        [in_mine[:, features:], in_other[:, features:]] + [f[:, :features] for f in far], axis=0
    )
    to_out = jnp.concatenate([n_mine[...], n_other[...]] + [f[:, features:] for f in far], axis=0)
    together = (aggregate[...] + aggregate2[...]).astype(bf16)
    pre = lat_all[...] + dot_rows(together, from_agg)
    act = (pre * sigmoid(pre)).astype(bf16)
    node_normed, node_inverse = normalize(dot(act, to_out))
    next_all[...] = (own[...].astype(f32) + node_normed * node_gain).astype(bf16)
    mine = next_all[:, lanes(group, wide)]
    node_next[...] = jnp.where(core == 0, mine[:, :width], mine[:, width:])
    cot = extra[half : half + nodes].astype(f32)
    node_dy = norm_back(cot * node_gain, node_normed, node_inverse).astype(bf16)
    node_dpre = (dot_rows(node_dy, to_out) * swish_slope(pre)).astype(bf16)
    high, low = split(dot(node_dpre, from_agg))

    taken = take[...]
    edge_total = extra[:half].astype(f32) + dot_cols(
        jnp.concatenate([taken, taken], axis=0), jnp.concatenate([high, low], axis=0)
    )
    dy = norm_back(edge_total * edge_gain, normed[...], inverse[...]).astype(bf16)
    back = dot_rows(dy, jnp.concatenate([out_mine[...], out_other[...]], axis=0))
    dpre = (back * swish_slope(edge_pre[...])).astype(bf16)

    dpre_ref[...] = dpre
    total_ref[...] = edge_total

    def weighted(values, index):
        columns = slice(index * features, (index + 1) * features)
        weight = jnp.concatenate([e_mine[:, columns], e_other[:, columns]], axis=0)
        both = dot(jnp.concatenate(split(values), axis=0), weight)
        return both[: values.shape[0]] + both[values.shape[0] :]

    grads[...] = weighted(dot(pick[...], dpre), 1)
    home = weighted(dot(taken, dpre), 2)
    node_weight = jnp.concatenate([in_mine[:, :features], in_other[:, :features]], axis=0)
    home = home + 0.5 * dot(node_dpre[:, :hidden], node_weight)
    grads[pl.ds(pl.multiple_of(block * nodes, nodes), nodes)] += home
    feats = features // width
    for target in range(spread.shape[0]):
        first, column = target // feats * nodes, target % feats * width
        spread[target] = grads[first : first + nodes, column : column + width].astype(bf16)


def turn_edges(dpre, edge_total, e_mine, e_other, kept, *refs):
    *sents, grads = refs
    group, _ = place()
    features = edge_total.shape[1]
    wide = kept.shape[1]
    grads[...] = dot(dpre[...], jnp.concatenate([e_mine[:, :features], e_other[:, :features]], axis=0))
    for step, sent in enumerate(sents, 1):
        sent[...] = grads[:, lanes(group ^ step, wide)].astype(bf16)
    kept[...] = grads[:, lanes(group, wide)] + edge_total[:, lanes(group, wide)]


def add_groups(groups, *refs):
    parts, (kept, sent) = refs[:groups], refs[groups:]
    _, core = place()
    width = kept.shape[1]
    value = total(parts)
    kept[...] = jnp.where(core == 0, value[:, :width], value[:, width:]).astype(bf16)
    sent[...] = jnp.where(core == 0, value[:, width:], value[:, :width]).astype(bf16)


def add_nodes(shares, node_cot, node_grad):
    value = node_cot[...].astype(f32)
    for source in range(shares.shape[0]):
        value = value + shares[source].astype(f32)
    node_grad[...] = value.astype(bf16)


def assemble(next_mine, next_came, grad_mine, grad_came, edge_next, edge_grad):
    _, core = place()
    half = next_mine.shape[0]
    mine = pl.ds(pl.multiple_of(core * half, half), half)
    theirs = pl.ds(pl.multiple_of((1 - core) * half, half), half)
    edge_next[mine] = next_mine[...]
    edge_next[theirs] = next_came[...]
    edge_grad[mine] = grad_mine[...]
    edge_grad[theirs] = grad_came[...]


def shards(
    latent,
    edge_state,
    send_rows,
    sender_slot,
    receiver_row,
    edge_in_weight,
    edge_out_weight,
    edge_gain,
    node_in_weight,
    node_out_weight,
    node_gain,
    edge_cot,
    node_cot,
):
    nodes, width = latent.shape
    edge_dev = edge_state.shape[0]
    half = edge_dev // cores
    blocks = send_rows.shape[0]
    feats = lax.axis_size("feat")
    groups = feats // cores
    features = width * feats
    wide = width * cores
    hidden = edge_in_weight.shape[0] * cores
    table = blocks * nodes
    everyone = ("nodes", "feat")

    def swapped(values, bits):
        return lax.ppermute(values, "feat", [(i, i ^ bits) for i in range(feats)])

    def over_cores(values):
        return swapped(values, 1)

    def over_groups(values):
        return [swapped(values, cores * step) for step in range(1, groups)]

    gain_e, gain_n = edge_gain.reshape(1, width), node_gain.reshape(1, width)
    slot_rows = sender_slot.reshape(cores, half)
    receiver_rows = receiver_row.reshape(cores, half)

    (spread,) = stage(spread_latent, [((blocks * feats, nodes, width), bf16)], [latent])
    latents = lax.all_to_all(spread, everyone, 0, 0)
    states = [edge_state] + over_groups(edge_state)
    e_in = (edge_in_weight, over_cores(edge_in_weight))
    e_out = (edge_out_weight, over_cores(edge_out_weight))
    n_in = (node_in_weight, over_cores(node_in_weight))
    n_out = (node_out_weight, over_cores(node_out_weight))
    far = []
    far_in, far_out, _ = lax.optimization_barrier((node_in_weight, node_out_weight, e_in[1]))
    for weights in over_groups(jnp.concatenate([far_in[:, features:], far_out], axis=1)):
        far += [weights, over_cores(weights)]
    (sent,) = stage(functools.partial(send_half, groups), [((half, groups * width), bf16)], states)
    state, pre, pick, take = stage(
        functools.partial(prepare_edges, groups),
        [((half, features), bf16), ((half, hidden), f32), ((table, half), bf16), ((nodes, half), bf16)],
        [*states, over_cores(sent), *e_in, slot_rows, receiver_rows, send_rows],
        scalars=1,
    )
    rows = edge_dev + 2 * nodes
    (pack,) = stage(pack_extra, [((rows, width), bf16)], [edge_cot, node_cot, gain_e, gain_n])
    packs = [pack] + over_groups(pack)
    (sent,) = stage(functools.partial(send_half, groups), [((rows - half, groups * width), bf16)], packs)
    extra_came = over_cores(sent)
    edge_pre, part, sent, own, lat = stage(
        finish_edges,
        [
            ((half, hidden), f32),
            ((half, features), f32),
            ((half + nodes, features), bf16),
            ((nodes, features), bf16),
            ((nodes, hidden), f32),
        ],
        [latents, pre, pick, take, *e_in, *e_out, *n_in],
        scratch=[((table, features), bf16)],
    )
    normed, inverse, next_mine, next_sent, aggregate, lat_all, extra = stage(
        functools.partial(update_edges, groups),
        [
            ((half, features), f32),
            ((half, 1), f32),
            ((half, width), bf16),
            ((half, width), bf16),
            ((nodes, features), f32),
            ((nodes, features), f32),
            ((half + 2 * nodes, features), bf16),
        ],
        [part, lat, *over_groups(sent), *packs, extra_came, state, take],
        scratch=[((half, features), bf16)],
    )
    aggregate2 = over_cores(aggregate)
    next_came = over_cores(next_sent)
    node_next, dpre, edge_total, spread = stage(
        functools.partial(turn, groups),
        [
            ((nodes, width), bf16),
            ((half, hidden), bf16),
            ((half, features), f32),
            ((blocks * feats, nodes, width), bf16),
        ],
        [*far, aggregate, aggregate2, own, lat_all, extra, take, pick, normed, inverse, edge_pre]
        + [*e_in, *e_out, *n_in, *n_out],
        scratch=[((nodes, features), bf16), ((table, features), f32)],
    )
    kept, *sents = stage(
        turn_edges,
        [((half, wide), f32)] + [((half, wide), bf16)] * (groups - 1),
        [dpre, edge_total, *e_in],
        scratch=[((half, features), f32)],
    )
    sents = [swapped(s, cores * k) for k, s in enumerate(sents, 1)]
    shares = lax.all_to_all(spread, everyone, 0, 0)
    grad_mine, grad_sent = stage(
        functools.partial(add_groups, groups),
        [((half, width), bf16), ((half, width), bf16)],
        [kept, *sents],
    )
    edge_next, edge_grad = stage(
        assemble,
        [((edge_dev, width), bf16), ((edge_dev, width), bf16)],
        [next_mine, next_came, grad_mine, over_cores(grad_sent)],
    )
    (node_grad,) = stage(add_nodes, [((nodes, width), bf16)], [shares, node_cot])
    return (edge_next, node_next, edge_grad, node_grad)


def solution(mesh):
    rows = P(("groups", "nodes"), "feat")
    flat = P(("groups", "nodes"))
    matrix = P("feat", None)
    vector = P("feat")
    return jax.shard_map(
        shards,
        mesh=mesh,
        in_specs=(
            rows,
            rows,
            P("groups", None, None),
            flat,
            flat,
            matrix,
            matrix,
            vector,
            matrix,
            matrix,
            vector,
            rows,
            rows,
        ),
        out_specs=(rows, rows, rows, rows),
        check_vma=False,
    )
```

```python
import functools

import jax
import jax.numpy as jnp
from jax import lax
from jax.experimental import pallas as pl
from jax.experimental.pallas import tpu as pltpu
from jax.sharding import PartitionSpec as P

epsilon = 1e-05
f32 = jnp.float32
bf16 = jnp.bfloat16
cores = 2
kernel_vmem = 8 << 20


def dot(left, right):
    return jnp.dot(left, right, preferred_element_type=f32)


def dot_rows(left, right):
    return lax.dot_general(left, right, (((1,), (1,)), ((), ())), preferred_element_type=f32)


def dot_cols(left, right):
    return lax.dot_general(left, right, (((0,), (0,)), ((), ())), preferred_element_type=f32)


def split(values):
    high = values.astype(bf16)
    return high, (values - high.astype(f32)).astype(bf16)


def sigmoid(values):
    return 1.0 / (1.0 + jnp.exp(-values))


def swish_slope(pre_act):
    sigma = sigmoid(pre_act)
    return sigma * (1.0 + pre_act * (1.0 - sigma))


def normalize(values):
    mean = jnp.mean(values, axis=1, keepdims=True)
    square = jnp.mean(values * values, axis=1, keepdims=True)
    inverse = lax.rsqrt(square - mean * mean + epsilon)
    return (values - mean) * inverse, inverse


def norm_back(grad, normed, inverse):
    total = jnp.mean(grad, axis=1, keepdims=True)
    cross = jnp.mean(grad * normed, axis=1, keepdims=True)
    return inverse * (grad - total - normed * cross)


def place():
    feat = lax.axis_index("feat")
    return feat // cores, feat % cores


def pair(mine, other, core):
    return jnp.where(core == 0, jnp.concatenate([mine, other], 1), jnp.concatenate([other, mine], 1))


def lanes(group, width):
    return pl.ds(pl.multiple_of(group * width, width), width)


def stage(kernel, outs, operands, scalars=0, scratch=(), flops=1 << 24):
    specs = [pl.BlockSpec(memory_space=pltpu.VMEM)] * (len(operands) - scalars)
    specs += [pl.BlockSpec(memory_space=pltpu.SMEM)] * scalars
    moved = sum(o.size * o.dtype.itemsize for o in operands)
    return pl.pallas_call(
        kernel,
        out_shape=[jax.ShapeDtypeStruct(shape, kind) for shape, kind in outs],
        in_specs=specs,
        out_specs=[pl.BlockSpec(memory_space=pltpu.VMEM)] * len(outs),
        scratch_shapes=[pltpu.VMEM(shape, kind) for shape, kind in scratch],
        cost_estimate=pl.CostEstimate(flops=flops, bytes_accessed=moved, transcendentals=0),
        compiler_params=pltpu.CompilerParams(vmem_limit_bytes=kernel_vmem),
    )(*operands)


def gains(gain_e, gain_n, rows):
    shape = (rows, gain_e.shape[1])
    row = lax.broadcasted_iota(jnp.int32, shape, 0)
    e = jnp.broadcast_to(gain_e[...].astype(f32), shape)
    n = jnp.broadcast_to(gain_n[...].astype(f32), shape)
    return jnp.where(row == 0, e, n).astype(bf16)


def total(refs):
    value = refs[0][...]
    for ref in refs[1:]:
        value = value + ref[...].astype(f32)
    return value


def spread_latent(latent, spread):
    spread[...] = jnp.broadcast_to(latent[...][None], spread.shape)


def pack_extra(edge_cot, node_cot, gain_e, gain_n, out_weight, pack):
    edge_dev = edge_cot.shape[0]
    nodes = node_cot.shape[0]
    pack[:edge_dev] = edge_cot[...]
    pack[edge_dev : edge_dev + nodes] = node_cot[...]
    first = edge_dev + 2 * nodes
    pack[edge_dev + nodes : first] = gains(gain_e, gain_n, nodes)
    hid, width = out_weight.shape[0], pack.shape[1]
    for index in range(out_weight.shape[1] // width):
        columns = slice(index * width, (index + 1) * width)
        pack[first + index * hid : first + (index + 1) * hid] = out_weight[:, columns]


def half_rows(pack, core, half, shared=0):
    rows = pack[pl.ds(pl.multiple_of(core * half, half), half)]
    if shared == 0:
        return rows
    return jnp.concatenate([rows, pack[cores * half : cores * half + shared]], axis=0)


def send_half(groups, *refs):
    packs, sent = refs[:groups], refs[groups]
    _, core = place()
    width = packs[0].shape[1]
    half = packs[0].shape[0] - sent.shape[0]
    for step, pack in enumerate(packs):
        sent[:, step * width : (step + 1) * width] = half_rows(pack, 1 - core, half)


def prepare_edges(groups, *refs):
    packs = refs[:groups]
    theirs, mine, other, slot, receiver, send_rows, state, pre, pick, take = refs[groups:]
    group, core = place()
    block = lax.axis_index("nodes")
    features = state.shape[1]
    nodes, half = take.shape
    width = packs[0].shape[1]
    blocks, _, slots = send_rows.shape
    for step, pack in enumerate(packs):
        both = pair(half_rows(pack, core, half), theirs[:, step * width : (step + 1) * width], core)
        state[:, lanes(group ^ step, width * cores)] = both

    slot_row = slot[pl.ds(core, 1)]
    sender = block * nodes + slot_row
    for source in range(blocks):
        for k in range(slots):
            row = source * nodes + send_rows[source, block, k]
            sender = jnp.where(slot_row == nodes + source * slots + k, row, sender)
    pick[...] = (lax.broadcasted_iota(jnp.int32, pick.shape, 0) == sender).astype(f32).astype(bf16)
    here = receiver[pl.ds(core, 1)]
    take[...] = (lax.broadcasted_iota(jnp.int32, take.shape, 0) == here).astype(f32).astype(bf16)
    weight = jnp.concatenate([mine[:, :features], other[:, :features]], axis=0)
    pre[...] = dot_rows(state[...], weight)


def finish_edges(came, pre, pick, take, mine, other, n_mine, n_other, edge_pre, sent, own, lat, table):
    block = lax.axis_index("nodes")
    count, nodes, width = came.shape
    rows, features = table.shape
    half = pre.shape[0]
    feats = features // width
    for source in range(count):
        first, column = source // feats * nodes, source % feats * width
        table[first : first + nodes, column : column + width] = came[source]
    latent = table[pl.ds(pl.multiple_of(block * nodes, nodes), nodes)]
    own[...] = latent

    def weight(index):
        columns = slice(index * features, (index + 1) * features)
        return jnp.concatenate([mine[:, columns], other[:, columns]], axis=0)

    high, low = split(dot_rows(table[...], weight(1)))
    here_high, here_low = split(dot_rows(latent, weight(2)))
    chosen = jnp.concatenate([pick[...], pick[...], take[...], take[...]], axis=0)
    value = pre[...] + dot_cols(chosen, jnp.concatenate([high, low, here_high, here_low], axis=0))
    edge_pre[...] = value
    sent[:half] = (value * sigmoid(value)).astype(bf16)
    nodes_pre = dot_rows(latent, jnp.concatenate([n_mine[:, :features], n_other[:, :features]], axis=0))
    lat[...] = nodes_pre
    sent[half:] = jnp.concatenate(split(nodes_pre), axis=0)


def update_edges(groups, *refs):
    feats = groups * cores
    lat, acts, packs, refs = refs[0], refs[1 : groups + 1], refs[groups + 1 : groups + 1 + feats], refs[groups + 1 + feats :]
    state, take, normed, inverse, kept, lent, aggregate, lat_all, extra, next_all = refs
    group, core = place()
    nodes, half = take.shape
    width = kept.shape[1]
    hidden = lat.shape[1]
    hid = hidden // cores
    weights = []
    for step in range(groups):
        ours, theirs = packs[cores * step], packs[cores * step + 1]
        both = pair(half_rows(ours, core, half, 2 * nodes), half_rows(theirs, core, half, 2 * nodes), core)
        extra[:, lanes(group ^ step, width * cores)] = both
        for pack in (ours, theirs):
            first = cores * half + 2 * nodes
            parts = [pack[first + index * hid : first + (index + 1) * hid] for index in range(feats)]
            weights.append(jnp.concatenate(parts, axis=1))
    lat_all[:, :hidden] = lat[...]
    for step, act in enumerate(acts[1:], 1):
        high, low = act[half : half + nodes], act[half + nodes :]
        lat_all[:, step * hidden : (step + 1) * hidden] = high.astype(f32) + low.astype(f32)
    value = dot(jnp.concatenate([act[:half] for act in acts], axis=1), jnp.concatenate(weights, axis=0))
    normed_rows, inverse_rows = normalize(value)
    normed[...] = normed_rows
    inverse[...] = inverse_rows
    gain = extra[half + nodes :].astype(f32)[0:1]
    rows = (state[...].astype(f32) + normed_rows * gain).astype(bf16)
    aggregate[...] = dot(take[...], rows)
    next_all[...] = rows
    mine = next_all[:, lanes(group, width * cores)]
    kept[...] = jnp.where(core == 0, mine[:, :width], mine[:, width:])
    lent[...] = jnp.where(core == 0, mine[:, width:], mine[:, :width])


def turn(groups, *refs):
    far, refs = refs[: 2 * (groups - 1)], refs[2 * (groups - 1) :]
    aggregate, aggregate2, own, lat_all, extra, take, pick, normed, inverse, edge_pre = refs[:10]
    e_mine, e_other, out_mine, out_other, in_mine, in_other, n_mine, n_other = refs[10:18]
    node_next, dpre_ref, total_ref, spread, next_all, grads = refs[18:]
    group, core = place()
    block = lax.axis_index("nodes")
    nodes, half = take.shape
    features = extra.shape[1]
    hidden = edge_pre.shape[1]
    width = node_next.shape[1]
    wide = width * cores
    gain_rows = extra[half + nodes :].astype(f32)
    edge_gain, node_gain = gain_rows[0:1], gain_rows[1:2]

    from_agg = jnp.concatenate(
        [in_mine[:, features:], in_other[:, features:]] + [f[:, :features] for f in far], axis=0
    )
    to_out = jnp.concatenate([n_mine[...], n_other[...]] + [f[:, features:] for f in far], axis=0)
    together = (aggregate[...] + aggregate2[...]).astype(bf16)
    pre = lat_all[...] + dot_rows(together, from_agg)
    act = (pre * sigmoid(pre)).astype(bf16)
    node_normed, node_inverse = normalize(dot(act, to_out))
    next_all[...] = (own[...].astype(f32) + node_normed * node_gain).astype(bf16)
    mine = next_all[:, lanes(group, wide)]
    node_next[...] = jnp.where(core == 0, mine[:, :width], mine[:, width:])
    cot = extra[half : half + nodes].astype(f32)
    node_dy = norm_back(cot * node_gain, node_normed, node_inverse).astype(bf16)
    node_dpre = (dot_rows(node_dy, to_out) * swish_slope(pre)).astype(bf16)
    high, low = split(dot(node_dpre, from_agg))

    taken = take[...]
    edge_total = extra[:half].astype(f32) + dot_cols(
        jnp.concatenate([taken, taken], axis=0), jnp.concatenate([high, low], axis=0)
    )
    dy = norm_back(edge_total * edge_gain, normed[...], inverse[...]).astype(bf16)
    back = dot_rows(dy, jnp.concatenate([out_mine[...], out_other[...]], axis=0))
    dpre = (back * swish_slope(edge_pre[...])).astype(bf16)

    dpre_ref[...] = dpre
    total_ref[...] = edge_total

    def weighted(values, index):
        columns = slice(index * features, (index + 1) * features)
        weight = jnp.concatenate([e_mine[:, columns], e_other[:, columns]], axis=0)
        both = dot(jnp.concatenate(split(values), axis=0), weight)
        return both[: values.shape[0]] + both[values.shape[0] :]

    grads[...] = weighted(dot(pick[...], dpre), 1)
    home = weighted(dot(taken, dpre), 2)
    node_weight = jnp.concatenate([in_mine[:, :features], in_other[:, :features]], axis=0)
    home = home + 0.5 * dot(node_dpre[:, :hidden], node_weight)
    grads[pl.ds(pl.multiple_of(block * nodes, nodes), nodes)] += home
    feats = features // width
    for target in range(spread.shape[0]):
        first, column = target // feats * nodes, target % feats * width
        spread[target] = grads[first : first + nodes, column : column + width].astype(bf16)


def turn_edges(dpre, edge_total, e_mine, e_other, kept, *refs):
    *sents, grads = refs
    group, _ = place()
    features = edge_total.shape[1]
    wide = kept.shape[1]
    grads[...] = dot(dpre[...], jnp.concatenate([e_mine[:, :features], e_other[:, :features]], axis=0))
    for step, sent in enumerate(sents, 1):
        sent[...] = grads[:, lanes(group ^ step, wide)].astype(bf16)
    kept[...] = grads[:, lanes(group, wide)] + edge_total[:, lanes(group, wide)]


def add_groups(groups, *refs):
    parts, (kept, sent) = refs[:groups], refs[groups:]
    _, core = place()
    width = kept.shape[1]
    value = total(parts)
    kept[...] = jnp.where(core == 0, value[:, :width], value[:, width:]).astype(bf16)
    sent[...] = jnp.where(core == 0, value[:, width:], value[:, :width]).astype(bf16)


def add_nodes(shares, node_cot, node_grad):
    value = node_cot[...].astype(f32)
    for source in range(shares.shape[0]):
        value = value + shares[source].astype(f32)
    node_grad[...] = value.astype(bf16)


def assemble(next_mine, next_came, grad_mine, grad_came, edge_next, edge_grad):
    _, core = place()
    half = next_mine.shape[0]
    mine = pl.ds(pl.multiple_of(core * half, half), half)
    theirs = pl.ds(pl.multiple_of((1 - core) * half, half), half)
    edge_next[mine] = next_mine[...]
    edge_next[theirs] = next_came[...]
    edge_grad[mine] = grad_mine[...]
    edge_grad[theirs] = grad_came[...]


def shards(
    latent,
    edge_state,
    send_rows,
    sender_slot,
    receiver_row,
    edge_in_weight,
    edge_out_weight,
    edge_gain,
    node_in_weight,
    node_out_weight,
    node_gain,
    edge_cot,
    node_cot,
):
    nodes, width = latent.shape
    edge_dev = edge_state.shape[0]
    half = edge_dev // cores
    blocks = send_rows.shape[0]
    feats = lax.axis_size("feat")
    groups = feats // cores
    features = width * feats
    wide = width * cores
    hidden = edge_in_weight.shape[0] * cores
    table = blocks * nodes
    everyone = ("nodes", "feat")

    def swapped(values, bits):
        return lax.ppermute(values, "feat", [(i, i ^ bits) for i in range(feats)])

    def over_cores(values):
        return swapped(values, 1)

    def over_groups(values):
        return [swapped(values, cores * step) for step in range(1, groups)]

    gain_e, gain_n = edge_gain.reshape(1, width), node_gain.reshape(1, width)
    slot_rows = sender_slot.reshape(cores, half)
    receiver_rows = receiver_row.reshape(cores, half)

    (spread,) = stage(spread_latent, [((blocks * feats, nodes, width), bf16)], [latent])
    latents = lax.all_to_all(spread, everyone, 0, 0)
    states = [edge_state] + over_groups(edge_state)
    e_in = (edge_in_weight, over_cores(edge_in_weight))
    e_out = (edge_out_weight, over_cores(edge_out_weight))
    n_in = (node_in_weight, over_cores(node_in_weight))
    n_out = (node_out_weight, over_cores(node_out_weight))
    far = []
    for weights in over_groups(jnp.concatenate([node_in_weight[:, features:], node_out_weight], axis=1)):
        far += [weights, over_cores(weights)]
    (sent,) = stage(functools.partial(send_half, groups), [((half, groups * width), bf16)], states)
    state, pre, pick, take = stage(
        functools.partial(prepare_edges, groups),
        [((half, features), bf16), ((half, hidden), f32), ((table, half), bf16), ((nodes, half), bf16)],
        [*states, over_cores(sent), *e_in, slot_rows, receiver_rows, send_rows],
        scalars=1,
    )
    rows = edge_dev + 2 * nodes + feats * edge_out_weight.shape[0]
    (pack,) = stage(
        pack_extra, [((rows, width), bf16)], [edge_cot, node_cot, gain_e, gain_n, edge_out_weight]
    )
    packs = [part for came in [pack] + over_groups(pack) for part in (came, over_cores(came))]
    edge_pre, sent, own, lat = stage(
        finish_edges,
        [
            ((half, hidden), f32),
            ((half + 2 * nodes, hidden), bf16),
            ((nodes, features), bf16),
            ((nodes, hidden), f32),
        ],
        [latents, pre, pick, take, *e_in, *n_in],
        scratch=[((table, features), bf16)],
    )
    normed, inverse, next_mine, next_sent, aggregate, lat_all, extra = stage(
        functools.partial(update_edges, groups),
        [
            ((half, features), f32),
            ((half, 1), f32),
            ((half, width), bf16),
            ((half, width), bf16),
            ((nodes, features), f32),
            ((nodes, features), f32),
            ((half + 2 * nodes, features), bf16),
        ],
        [lat, sent, *over_groups(sent), *packs, state, take],
        scratch=[((half, features), bf16)],
    )
    aggregate2 = over_cores(aggregate)
    next_came = over_cores(next_sent)
    node_next, dpre, edge_total, spread = stage(
        functools.partial(turn, groups),
        [
            ((nodes, width), bf16),
            ((half, hidden), bf16),
            ((half, features), f32),
            ((blocks * feats, nodes, width), bf16),
        ],
        [*far, aggregate, aggregate2, own, lat_all, extra, take, pick, normed, inverse, edge_pre]
        + [*e_in, *e_out, *n_in, *n_out],
        scratch=[((nodes, features), bf16), ((table, features), f32)],
    )
    kept, *sents = stage(
        turn_edges,
        [((half, wide), f32)] + [((half, wide), bf16)] * (groups - 1),
        [dpre, edge_total, *e_in],
        scratch=[((half, features), f32)],
    )
    sents = [swapped(s, cores * k) for k, s in enumerate(sents, 1)]
    shares = lax.all_to_all(spread, everyone, 0, 0)
    grad_mine, grad_sent = stage(
        functools.partial(add_groups, groups),
        [((half, width), bf16), ((half, width), bf16)],
        [kept, *sents],
    )
    edge_next, edge_grad = stage(
        assemble,
        [((edge_dev, width), bf16), ((edge_dev, width), bf16)],
        [next_mine, next_came, grad_mine, over_cores(grad_sent)],
    )
    (node_grad,) = stage(add_nodes, [((nodes, width), bf16)], [shares, node_cot])
    return (edge_next, node_next, edge_grad, node_grad)


def solution(mesh):
    rows = P(("groups", "nodes"), "feat")
    flat = P(("groups", "nodes"))
    matrix = P("feat", None)
    vector = P("feat")
    return jax.shard_map(
        shards,
        mesh=mesh,
        in_specs=(
            rows,
            rows,
            P("groups", None, None),
            flat,
            flat,
            matrix,
            matrix,
            vector,
            matrix,
            matrix,
            vector,
            rows,
            rows,
        ),
        out_specs=(rows, rows, rows, rows),
        check_vma=False,
    )
```

```python
import functools

import jax
import jax.numpy as jnp
from jax import lax
from jax.experimental import pallas as pl
from jax.experimental.pallas import tpu as pltpu
from jax.sharding import PartitionSpec as P

epsilon = 1e-05
f32 = jnp.float32
bf16 = jnp.bfloat16
cores = 2
kernel_vmem = 8 << 20


def dot(left, right):
    return jnp.dot(left, right, preferred_element_type=f32)


def dot_rows(left, right):
    return lax.dot_general(left, right, (((1,), (1,)), ((), ())), preferred_element_type=f32)


def dot_cols(left, right):
    return lax.dot_general(left, right, (((0,), (0,)), ((), ())), preferred_element_type=f32)


def split(values):
    high = values.astype(bf16)
    return high, (values - high.astype(f32)).astype(bf16)


def sigmoid(values):
    return 1.0 / (1.0 + jnp.exp(-values))


def swish_slope(pre_act):
    sigma = sigmoid(pre_act)
    return sigma * (1.0 + pre_act * (1.0 - sigma))


def normalize(values):
    mean = jnp.mean(values, axis=1, keepdims=True)
    square = jnp.mean(values * values, axis=1, keepdims=True)
    inverse = lax.rsqrt(square - mean * mean + epsilon)
    return (values - mean) * inverse, inverse


def norm_back(grad, normed, inverse):
    total = jnp.mean(grad, axis=1, keepdims=True)
    cross = jnp.mean(grad * normed, axis=1, keepdims=True)
    return inverse * (grad - total - normed * cross)


def place():
    feat = lax.axis_index("feat")
    return feat // cores, feat % cores


def pair(mine, other, core):
    return jnp.where(core == 0, jnp.concatenate([mine, other], 1), jnp.concatenate([other, mine], 1))


def lanes(group, width):
    return pl.ds(pl.multiple_of(group * width, width), width)


def stage(kernel, outs, operands, scalars=0, scratch=(), flops=1 << 24):
    specs = [pl.BlockSpec(memory_space=pltpu.VMEM)] * (len(operands) - scalars)
    specs += [pl.BlockSpec(memory_space=pltpu.SMEM)] * scalars
    moved = sum(o.size * o.dtype.itemsize for o in operands)
    return pl.pallas_call(
        kernel,
        out_shape=[jax.ShapeDtypeStruct(shape, kind) for shape, kind in outs],
        in_specs=specs,
        out_specs=[pl.BlockSpec(memory_space=pltpu.VMEM)] * len(outs),
        scratch_shapes=[pltpu.VMEM(shape, kind) for shape, kind in scratch],
        cost_estimate=pl.CostEstimate(flops=flops, bytes_accessed=moved, transcendentals=0),
        compiler_params=pltpu.CompilerParams(vmem_limit_bytes=kernel_vmem),
    )(*operands)


def gains(gain_e, gain_n, rows):
    shape = (rows, gain_e.shape[1])
    row = lax.broadcasted_iota(jnp.int32, shape, 0)
    e = jnp.broadcast_to(gain_e[...].astype(f32), shape)
    n = jnp.broadcast_to(gain_n[...].astype(f32), shape)
    return jnp.where(row == 0, e, n).astype(bf16)


def total(refs):
    value = refs[0][...]
    for ref in refs[1:]:
        value = value + ref[...].astype(f32)
    return value


def spread_latent(latent, spread):
    spread[...] = jnp.broadcast_to(latent[...][None], spread.shape)


def pack_extra(edge_cot, node_cot, gain_e, gain_n, pack):
    edge_dev = edge_cot.shape[0]
    nodes = node_cot.shape[0]
    pack[:edge_dev] = edge_cot[...]
    pack[edge_dev : edge_dev + nodes] = node_cot[...]
    pack[edge_dev + nodes :] = gains(gain_e, gain_n, nodes)


def half_rows(pack, core, half):
    rows = pack[pl.ds(pl.multiple_of(core * half, half), half)]
    if pack.shape[0] == cores * half:
        return rows
    return jnp.concatenate([rows, pack[cores * half :]], axis=0)


def send_half(groups, *refs):
    packs, sent = refs[:groups], refs[groups]
    _, core = place()
    width = packs[0].shape[1]
    half = packs[0].shape[0] - sent.shape[0]
    for step, pack in enumerate(packs):
        sent[:, step * width : (step + 1) * width] = half_rows(pack, 1 - core, half)


def prepare_edges(groups, *refs):
    packs = refs[:groups]
    theirs, mine, other, slot, receiver, send_rows, state, pre, pick, take = refs[groups:]
    group, core = place()
    block = lax.axis_index("nodes")
    features = state.shape[1]
    nodes, half = take.shape
    width = packs[0].shape[1]
    blocks, _, slots = send_rows.shape
    for step, pack in enumerate(packs):
        both = pair(half_rows(pack, core, half), theirs[:, step * width : (step + 1) * width], core)
        state[:, lanes(group ^ step, width * cores)] = both

    slot_row = slot[pl.ds(core, 1)]
    sender = block * nodes + slot_row
    for source in range(blocks):
        for k in range(slots):
            row = source * nodes + send_rows[source, block, k]
            sender = jnp.where(slot_row == nodes + source * slots + k, row, sender)
    pick[...] = (lax.broadcasted_iota(jnp.int32, pick.shape, 0) == sender).astype(f32).astype(bf16)
    here = receiver[pl.ds(core, 1)]
    take[...] = (lax.broadcasted_iota(jnp.int32, take.shape, 0) == here).astype(f32).astype(bf16)
    weight = jnp.concatenate([mine[:, :features], other[:, :features]], axis=0)
    pre[...] = dot_rows(state[...], weight)


def finish_edges(came, pre, pick, take, mine, other, out_mine, out_other, n_mine, n_other, edge_pre, part, sent, own, lat, table):
    block = lax.axis_index("nodes")
    count, nodes, width = came.shape
    rows, features = table.shape
    half, hidden = pre.shape
    feats = features // width
    for source in range(count):
        first, column = source // feats * nodes, source % feats * width
        table[first : first + nodes, column : column + width] = came[source]
    latent = table[pl.ds(pl.multiple_of(block * nodes, nodes), nodes)]
    own[...] = latent

    def weight(index):
        columns = slice(index * features, (index + 1) * features)
        return jnp.concatenate([mine[:, columns], other[:, columns]], axis=0)

    high, low = split(dot_rows(table[...], weight(1)))
    here_high, here_low = split(dot_rows(latent, weight(2)))
    chosen = jnp.concatenate([pick[...], pick[...], take[...], take[...]], axis=0)
    value = pre[...] + dot_cols(chosen, jnp.concatenate([high, low, here_high, here_low], axis=0))
    edge_pre[...] = value
    act = (value * sigmoid(value)).astype(bf16)
    out = dot(act, jnp.concatenate([out_mine[...], out_other[...]], axis=0))
    part[...] = out
    sent[:half] = out.astype(bf16)
    nodes_pre = dot_rows(latent, jnp.concatenate([n_mine[:, :features], n_other[:, :features]], axis=0))
    lat[...] = nodes_pre
    high, low = split(nodes_pre)
    sent[half:] = jnp.zeros((nodes, features), bf16)
    sent[half:, :hidden] = high
    sent[half:, hidden : 2 * hidden] = low


def update_edges(groups, *refs):
    part, lat, came, packs = refs[0], refs[1], refs[2 : groups + 1], refs[groups + 1 : 2 * groups + 1]
    theirs, state, take, normed, inverse, kept, lent, aggregate, lat_all, extra, next_all = refs[2 * groups + 1 :]
    group, core = place()
    nodes, half = take.shape
    width = kept.shape[1]
    hidden = lat.shape[1]
    for step, pack in enumerate(packs):
        both = pair(half_rows(pack, core, half), theirs[:, step * width : (step + 1) * width], core)
        extra[:, lanes(group ^ step, width * cores)] = both
    value = part[...]
    lat_all[:, :hidden] = lat[...]
    for step, ref in enumerate(came, 1):
        value = value + ref[:half].astype(f32)
        high, low = ref[half:, :hidden], ref[half:, hidden : 2 * hidden]
        lat_all[:, step * hidden : (step + 1) * hidden] = high.astype(f32) + low.astype(f32)
    normed_rows, inverse_rows = normalize(value)
    normed[...] = normed_rows
    inverse[...] = inverse_rows
    gain = extra[half + nodes :].astype(f32)[0:1]
    rows = (state[...].astype(f32) + normed_rows * gain).astype(bf16)
    aggregate[...] = dot(take[...], rows)
    next_all[...] = rows
    mine = next_all[:, lanes(group, width * cores)]
    kept[...] = jnp.where(core == 0, mine[:, :width], mine[:, width:])
    lent[...] = jnp.where(core == 0, mine[:, width:], mine[:, :width])


def turn(groups, *refs):
    count = cores * (groups - 1)
    far_in, far_out, refs = refs[:count], refs[count : 2 * count], refs[2 * count :]
    aggregate, aggregate2, own, lat_all, extra, take, pick, normed, inverse, edge_pre = refs[:10]
    e_mine, e_other, out_mine, out_other, in_mine, in_other, n_mine, n_other = refs[10:18]
    node_next, dpre_ref, total_ref, spread, next_all, grads = refs[18:]
    group, core = place()
    block = lax.axis_index("nodes")
    nodes, half = take.shape
    features = extra.shape[1]
    hidden = edge_pre.shape[1]
    width = node_next.shape[1]
    wide = width * cores
    gain_rows = extra[half + nodes :].astype(f32)
    edge_gain, node_gain = gain_rows[0:1], gain_rows[1:2]

    from_agg = jnp.concatenate(
        [in_mine[:, features:], in_other[:, features:]] + [f[...] for f in far_in], axis=0
    )
    to_out = jnp.concatenate([n_mine[...], n_other[...]] + [f[...] for f in far_out], axis=0)
    together = (aggregate[...] + aggregate2[...]).astype(bf16)
    pre = lat_all[...] + dot_rows(together, from_agg)
    act = (pre * sigmoid(pre)).astype(bf16)
    node_normed, node_inverse = normalize(dot(act, to_out))
    next_all[...] = (own[...].astype(f32) + node_normed * node_gain).astype(bf16)
    mine = next_all[:, lanes(group, wide)]
    node_next[...] = jnp.where(core == 0, mine[:, :width], mine[:, width:])
    cot = extra[half : half + nodes].astype(f32)
    node_dy = norm_back(cot * node_gain, node_normed, node_inverse).astype(bf16)
    node_dpre = (dot_rows(node_dy, to_out) * swish_slope(pre)).astype(bf16)
    high, low = split(dot(node_dpre, from_agg))

    taken = take[...]
    edge_total = extra[:half].astype(f32) + dot_cols(
        jnp.concatenate([taken, taken], axis=0), jnp.concatenate([high, low], axis=0)
    )
    dy = norm_back(edge_total * edge_gain, normed[...], inverse[...]).astype(bf16)
    back = dot_rows(dy, jnp.concatenate([out_mine[...], out_other[...]], axis=0))
    dpre = (back * swish_slope(edge_pre[...])).astype(bf16)

    dpre_ref[...] = dpre
    total_ref[...] = edge_total

    def weighted(values, index):
        columns = slice(index * features, (index + 1) * features)
        weight = jnp.concatenate([e_mine[:, columns], e_other[:, columns]], axis=0)
        both = dot(jnp.concatenate(split(values), axis=0), weight)
        return both[: values.shape[0]] + both[values.shape[0] :]

    grads[...] = weighted(dot(pick[...], dpre), 1)
    home = weighted(dot(taken, dpre), 2)
    node_weight = jnp.concatenate([in_mine[:, :features], in_other[:, :features]], axis=0)
    home = home + 0.5 * dot(node_dpre[:, :hidden], node_weight)
    grads[pl.ds(pl.multiple_of(block * nodes, nodes), nodes)] += home
    feats = features // width
    for target in range(spread.shape[0]):
        first, column = target // feats * nodes, target % feats * width
        spread[target] = grads[first : first + nodes, column : column + width].astype(bf16)


def turn_edges(dpre, edge_total, e_mine, e_other, kept, *refs):
    *sents, grads = refs
    group, _ = place()
    features = edge_total.shape[1]
    wide = kept.shape[1]
    grads[...] = dot(dpre[...], jnp.concatenate([e_mine[:, :features], e_other[:, :features]], axis=0))
    for step, sent in enumerate(sents, 1):
        sent[...] = grads[:, lanes(group ^ step, wide)].astype(bf16)
    kept[...] = grads[:, lanes(group, wide)] + edge_total[:, lanes(group, wide)]


def add_groups(groups, *refs):
    parts, (kept, sent) = refs[:groups], refs[groups:]
    _, core = place()
    width = kept.shape[1]
    value = total(parts)
    kept[...] = jnp.where(core == 0, value[:, :width], value[:, width:]).astype(bf16)
    sent[...] = jnp.where(core == 0, value[:, width:], value[:, :width]).astype(bf16)


def add_nodes(shares, node_cot, node_grad):
    value = node_cot[...].astype(f32)
    for source in range(shares.shape[0]):
        value = value + shares[source].astype(f32)
    node_grad[...] = value.astype(bf16)


def assemble(next_mine, next_came, grad_mine, grad_came, edge_next, edge_grad):
    _, core = place()
    half = next_mine.shape[0]
    mine = pl.ds(pl.multiple_of(core * half, half), half)
    theirs = pl.ds(pl.multiple_of((1 - core) * half, half), half)
    edge_next[mine] = next_mine[...]
    edge_next[theirs] = next_came[...]
    edge_grad[mine] = grad_mine[...]
    edge_grad[theirs] = grad_came[...]


def shards(
    latent,
    edge_state,
    send_rows,
    sender_slot,
    receiver_row,
    edge_in_weight,
    edge_out_weight,
    edge_gain,
    node_in_weight,
    node_out_weight,
    node_gain,
    edge_cot,
    node_cot,
):
    nodes, width = latent.shape
    edge_dev = edge_state.shape[0]
    half = edge_dev // cores
    blocks = send_rows.shape[0]
    feats = lax.axis_size("feat")
    groups = feats // cores
    features = width * feats
    wide = width * cores
    hidden = edge_in_weight.shape[0] * cores
    table = blocks * nodes
    everyone = ("nodes", "feat")

    def swapped(values, bits):
        return lax.ppermute(values, "feat", [(i, i ^ bits) for i in range(feats)])

    def over_cores(values):
        return swapped(values, 1)

    def over_groups(values):
        return [swapped(values, cores * step) for step in range(1, groups)]

    gain_e, gain_n = edge_gain.reshape(1, width), node_gain.reshape(1, width)
    slot_rows = sender_slot.reshape(cores, half)
    receiver_rows = receiver_row.reshape(cores, half)

    (spread,) = stage(spread_latent, [((blocks * feats, nodes, width), bf16)], [latent])
    latents = lax.all_to_all(spread, everyone, 0, 0)
    states = [edge_state] + over_groups(edge_state)
    e_in = (edge_in_weight, over_cores(edge_in_weight))
    e_out = (edge_out_weight, over_cores(edge_out_weight))
    n_in = (node_in_weight, over_cores(node_in_weight))
    n_out = (node_out_weight, over_cores(node_out_weight))
    far_out = [part for came in over_groups(node_out_weight) for part in (came, over_cores(came))]
    far_in = [part for came in over_groups(node_in_weight[:, features:]) for part in (came, over_cores(came))]
    far = far_in + far_out
    (sent,) = stage(functools.partial(send_half, groups), [((half, groups * width), bf16)], states)
    state, pre, pick, take = stage(
        functools.partial(prepare_edges, groups),
        [((half, features), bf16), ((half, hidden), f32), ((table, half), bf16), ((nodes, half), bf16)],
        [*states, over_cores(sent), *e_in, slot_rows, receiver_rows, send_rows],
        scalars=1,
    )
    rows = edge_dev + 2 * nodes
    (pack,) = stage(pack_extra, [((rows, width), bf16)], [edge_cot, node_cot, gain_e, gain_n])
    packs = [pack] + over_groups(pack)
    (sent,) = stage(functools.partial(send_half, groups), [((rows - half, groups * width), bf16)], packs)
    extra_came = over_cores(sent)
    edge_pre, part, sent, own, lat = stage(
        finish_edges,
        [
            ((half, hidden), f32),
            ((half, features), f32),
            ((half + nodes, features), bf16),
            ((nodes, features), bf16),
            ((nodes, hidden), f32),
        ],
        [latents, pre, pick, take, *e_in, *e_out, *n_in],
        scratch=[((table, features), bf16)],
    )
    normed, inverse, next_mine, next_sent, aggregate, lat_all, extra = stage(
        functools.partial(update_edges, groups),
        [
            ((half, features), f32),
            ((half, 1), f32),
            ((half, width), bf16),
            ((half, width), bf16),
            ((nodes, features), f32),
            ((nodes, features), f32),
            ((half + 2 * nodes, features), bf16),
        ],
        [part, lat, *over_groups(sent), *packs, extra_came, state, take],
        scratch=[((half, features), bf16)],
    )
    aggregate2 = over_cores(aggregate)
    next_came = over_cores(next_sent)
    node_next, dpre, edge_total, spread = stage(
        functools.partial(turn, groups),
        [
            ((nodes, width), bf16),
            ((half, hidden), bf16),
            ((half, features), f32),
            ((blocks * feats, nodes, width), bf16),
        ],
        [*far, aggregate, aggregate2, own, lat_all, extra, take, pick, normed, inverse, edge_pre]
        + [*e_in, *e_out, *n_in, *n_out],
        scratch=[((nodes, features), bf16), ((table, features), f32)],
    )
    kept, *sents = stage(
        turn_edges,
        [((half, wide), f32)] + [((half, wide), bf16)] * (groups - 1),
        [dpre, edge_total, *e_in],
        scratch=[((half, features), f32)],
    )
    sents = [swapped(s, cores * k) for k, s in enumerate(sents, 1)]
    shares = lax.all_to_all(spread, everyone, 0, 0)
    grad_mine, grad_sent = stage(
        functools.partial(add_groups, groups),
        [((half, width), bf16), ((half, width), bf16)],
        [kept, *sents],
    )
    edge_next, edge_grad = stage(
        assemble,
        [((edge_dev, width), bf16), ((edge_dev, width), bf16)],
        [next_mine, next_came, grad_mine, over_cores(grad_sent)],
    )
    (node_grad,) = stage(add_nodes, [((nodes, width), bf16)], [shares, node_cot])
    return (edge_next, node_next, edge_grad, node_grad)


def solution(mesh):
    rows = P(("groups", "nodes"), "feat")
    flat = P(("groups", "nodes"))
    matrix = P("feat", None)
    vector = P("feat")
    return jax.shard_map(
        shards,
        mesh=mesh,
        in_specs=(
            rows,
            rows,
            P("groups", None, None),
            flat,
            flat,
            matrix,
            matrix,
            vector,
            matrix,
            matrix,
            vector,
            rows,
            rows,
        ),
        out_specs=(rows, rows, rows, rows),
        check_vma=False,
    )
```

```python
import functools

import jax
import jax.numpy as jnp
from jax import lax
from jax.experimental import pallas as pl
from jax.experimental.pallas import tpu as pltpu
from jax.sharding import PartitionSpec as P

epsilon = 1e-05
f32 = jnp.float32
bf16 = jnp.bfloat16
cores = 2
kernel_vmem = 8 << 20


def dot(left, right):
    return jnp.dot(left, right, preferred_element_type=f32)


def dot_rows(left, right):
    return lax.dot_general(left, right, (((1,), (1,)), ((), ())), preferred_element_type=f32)


def dot_cols(left, right):
    return lax.dot_general(left, right, (((0,), (0,)), ((), ())), preferred_element_type=f32)


def split(values):
    high = values.astype(bf16)
    return high, (values - high.astype(f32)).astype(bf16)


def sigmoid(values):
    return 1.0 / (1.0 + jnp.exp(-values))


def swish_slope(pre_act):
    sigma = sigmoid(pre_act)
    return sigma * (1.0 + pre_act * (1.0 - sigma))


def normalize(values):
    mean = jnp.mean(values, axis=1, keepdims=True)
    square = jnp.mean(values * values, axis=1, keepdims=True)
    inverse = lax.rsqrt(square - mean * mean + epsilon)
    return (values - mean) * inverse, inverse


def norm_back(grad, normed, inverse):
    total = jnp.mean(grad, axis=1, keepdims=True)
    cross = jnp.mean(grad * normed, axis=1, keepdims=True)
    return inverse * (grad - total - normed * cross)


def place():
    feat = lax.axis_index("feat")
    return feat // cores, feat % cores


def pair(mine, other, core):
    return jnp.where(core == 0, jnp.concatenate([mine, other], 1), jnp.concatenate([other, mine], 1))


def lanes(group, width):
    return pl.ds(pl.multiple_of(group * width, width), width)


def stage(kernel, outs, operands, scalars=0, scratch=(), flops=1 << 24):
    specs = [pl.BlockSpec(memory_space=pltpu.VMEM)] * (len(operands) - scalars)
    specs += [pl.BlockSpec(memory_space=pltpu.SMEM)] * scalars
    moved = sum(o.size * o.dtype.itemsize for o in operands)
    return pl.pallas_call(
        kernel,
        out_shape=[jax.ShapeDtypeStruct(shape, kind) for shape, kind in outs],
        in_specs=specs,
        out_specs=[pl.BlockSpec(memory_space=pltpu.VMEM)] * len(outs),
        scratch_shapes=[pltpu.VMEM(shape, kind) for shape, kind in scratch],
        cost_estimate=pl.CostEstimate(flops=flops, bytes_accessed=moved, transcendentals=0),
        compiler_params=pltpu.CompilerParams(vmem_limit_bytes=kernel_vmem),
    )(*operands)


def gains(gain_e, gain_n, rows):
    shape = (rows, gain_e.shape[1])
    row = lax.broadcasted_iota(jnp.int32, shape, 0)
    e = jnp.broadcast_to(gain_e[...].astype(f32), shape)
    n = jnp.broadcast_to(gain_n[...].astype(f32), shape)
    return jnp.where(row == 0, e, n).astype(bf16)


def total(refs):
    value = refs[0][...]
    for ref in refs[1:]:
        value = value + ref[...].astype(f32)
    return value


def spread_latent(latent, spread):
    spread[...] = jnp.broadcast_to(latent[...][None], spread.shape)


def pack_extra(edge_cot, node_cot, gain_e, gain_n, pack):
    edge_dev = edge_cot.shape[0]
    nodes = node_cot.shape[0]
    pack[:edge_dev] = edge_cot[...]
    pack[edge_dev : edge_dev + nodes] = node_cot[...]
    pack[edge_dev + nodes :] = gains(gain_e, gain_n, nodes)


def half_rows(pack, core, half):
    rows = pack[pl.ds(pl.multiple_of(core * half, half), half)]
    if pack.shape[0] == cores * half:
        return rows
    return jnp.concatenate([rows, pack[cores * half :]], axis=0)


def send_half(groups, *refs):
    packs, sent = refs[:groups], refs[groups]
    _, core = place()
    width = packs[0].shape[1]
    half = packs[0].shape[0] - sent.shape[0]
    for step, pack in enumerate(packs):
        sent[:, step * width : (step + 1) * width] = half_rows(pack, 1 - core, half)


def prepare_edges(groups, *refs):
    packs = refs[:groups]
    theirs, mine, other, slot, receiver, send_rows, state, pre, pick, take = refs[groups:]
    group, core = place()
    block = lax.axis_index("nodes")
    features = state.shape[1]
    nodes, half = take.shape
    width = packs[0].shape[1]
    blocks, _, slots = send_rows.shape
    for step, pack in enumerate(packs):
        both = pair(half_rows(pack, core, half), theirs[:, step * width : (step + 1) * width], core)
        state[:, lanes(group ^ step, width * cores)] = both

    slot_row = slot[pl.ds(core, 1)]
    sender = block * nodes + slot_row
    for source in range(blocks):
        for k in range(slots):
            row = source * nodes + send_rows[source, block, k]
            sender = jnp.where(slot_row == nodes + source * slots + k, row, sender)
    pick[...] = (lax.broadcasted_iota(jnp.int32, pick.shape, 0) == sender).astype(f32).astype(bf16)
    here = receiver[pl.ds(core, 1)]
    take[...] = (lax.broadcasted_iota(jnp.int32, take.shape, 0) == here).astype(f32).astype(bf16)
    weight = jnp.concatenate([mine[:, :features], other[:, :features]], axis=0)
    pre[...] = dot_rows(state[...], weight)


def finish_edges(came, pre, pick, take, mine, other, out_mine, out_other, n_mine, n_other, edge_pre, part, sent, own, lat, table):
    block = lax.axis_index("nodes")
    count, nodes, width = came.shape
    rows, features = table.shape
    half, hidden = pre.shape
    feats = features // width
    for source in range(count):
        first, column = source // feats * nodes, source % feats * width
        table[first : first + nodes, column : column + width] = came[source]
    latent = table[pl.ds(pl.multiple_of(block * nodes, nodes), nodes)]
    own[...] = latent

    def weight(index):
        columns = slice(index * features, (index + 1) * features)
        return jnp.concatenate([mine[:, columns], other[:, columns]], axis=0)

    high, low = split(dot_rows(table[...], weight(1)))
    here_high, here_low = split(dot_rows(latent, weight(2)))
    chosen = jnp.concatenate([pick[...], pick[...], take[...], take[...]], axis=0)
    value = pre[...] + dot_cols(chosen, jnp.concatenate([high, low, here_high, here_low], axis=0))
    edge_pre[...] = value
    act = (value * sigmoid(value)).astype(bf16)
    out = dot(act, jnp.concatenate([out_mine[...], out_other[...]], axis=0))
    part[...] = out
    sent[:half] = out.astype(bf16)
    nodes_pre = dot_rows(latent, jnp.concatenate([n_mine[:, :features], n_other[:, :features]], axis=0))
    lat[...] = nodes_pre
    high, low = split(nodes_pre)
    sent[half:] = jnp.zeros((nodes, features), bf16)
    sent[half:, :hidden] = high
    sent[half:, hidden : 2 * hidden] = low


def update_edges(groups, *refs):
    part, lat, came, packs = refs[0], refs[1], refs[2 : groups + 1], refs[groups + 1 : 2 * groups + 1]
    theirs, state, take, normed, inverse, kept, lent, aggregate, lat_all, extra, next_all = refs[2 * groups + 1 :]
    group, core = place()
    nodes, half = take.shape
    width = kept.shape[1]
    hidden = lat.shape[1]
    for step, pack in enumerate(packs):
        both = pair(half_rows(pack, core, half), theirs[:, step * width : (step + 1) * width], core)
        extra[:, lanes(group ^ step, width * cores)] = both
    value = part[...]
    lat_all[:, :hidden] = lat[...]
    for step, ref in enumerate(came, 1):
        value = value + ref[:half].astype(f32)
        high, low = ref[half:, :hidden], ref[half:, hidden : 2 * hidden]
        lat_all[:, step * hidden : (step + 1) * hidden] = high.astype(f32) + low.astype(f32)
    normed_rows, inverse_rows = normalize(value)
    normed[...] = normed_rows
    inverse[...] = inverse_rows
    gain = extra[half + nodes :].astype(f32)[0:1]
    rows = (state[...].astype(f32) + normed_rows * gain).astype(bf16)
    aggregate[...] = dot(take[...], rows)
    next_all[...] = rows
    mine = next_all[:, lanes(group, width * cores)]
    kept[...] = jnp.where(core == 0, mine[:, :width], mine[:, width:])
    lent[...] = jnp.where(core == 0, mine[:, width:], mine[:, :width])


def turn(groups, *refs):
    far, refs = refs[: 2 * (groups - 1)], refs[2 * (groups - 1) :]
    aggregate, aggregate2, own, lat_all, extra, take, pick, normed, inverse, edge_pre = refs[:10]
    e_mine, e_other, out_mine, out_other, in_mine, in_other, n_mine, n_other = refs[10:18]
    node_next, dpre_ref, total_ref, spread, next_all, grads = refs[18:]
    group, core = place()
    block = lax.axis_index("nodes")
    nodes, half = take.shape
    features = extra.shape[1]
    hidden = edge_pre.shape[1]
    width = node_next.shape[1]
    wide = width * cores
    gain_rows = extra[half + nodes :].astype(f32)
    edge_gain, node_gain = gain_rows[0:1], gain_rows[1:2]

    from_agg = jnp.concatenate(
        [in_mine[:, features:], in_other[:, features:]] + [f[:, :features] for f in far], axis=0
    )
    to_out = jnp.concatenate([n_mine[...], n_other[...]] + [f[:, features:] for f in far], axis=0)
    together = (aggregate[...] + aggregate2[...]).astype(bf16)
    pre = lat_all[...] + dot_rows(together, from_agg)
    act = (pre * sigmoid(pre)).astype(bf16)
    node_normed, node_inverse = normalize(dot(act, to_out))
    next_all[...] = (own[...].astype(f32) + node_normed * node_gain).astype(bf16)
    mine = next_all[:, lanes(group, wide)]
    node_next[...] = jnp.where(core == 0, mine[:, :width], mine[:, width:])
    cot = extra[half : half + nodes].astype(f32)
    node_dy = norm_back(cot * node_gain, node_normed, node_inverse).astype(bf16)
    node_dpre = (dot_rows(node_dy, to_out) * swish_slope(pre)).astype(bf16)
    high, low = split(dot(node_dpre, from_agg))

    taken = take[...]
    edge_total = extra[:half].astype(f32) + dot_cols(
        jnp.concatenate([taken, taken], axis=0), jnp.concatenate([high, low], axis=0)
    )
    dy = norm_back(edge_total * edge_gain, normed[...], inverse[...]).astype(bf16)
    back = dot_rows(dy, jnp.concatenate([out_mine[...], out_other[...]], axis=0))
    dpre = (back * swish_slope(edge_pre[...])).astype(bf16)

    dpre_ref[...] = dpre
    total_ref[...] = edge_total

    def weighted(values, index):
        columns = slice(index * features, (index + 1) * features)
        weight = jnp.concatenate([e_mine[:, columns], e_other[:, columns]], axis=0)
        return dot(values.astype(bf16), weight)

    grads[...] = weighted(dot(pick[...], dpre), 1)
    home = weighted(dot(taken, dpre), 2)
    node_weight = jnp.concatenate([in_mine[:, :features], in_other[:, :features]], axis=0)
    home = home + 0.5 * dot(node_dpre[:, :hidden], node_weight)
    grads[pl.ds(pl.multiple_of(block * nodes, nodes), nodes)] += home
    feats = features // width
    for target in range(spread.shape[0]):
        first, column = target // feats * nodes, target % feats * width
        spread[target] = grads[first : first + nodes, column : column + width].astype(bf16)


def turn_edges(dpre, edge_total, e_mine, e_other, kept, *refs):
    *sents, grads = refs
    group, _ = place()
    features = edge_total.shape[1]
    wide = kept.shape[1]
    grads[...] = dot(dpre[...], jnp.concatenate([e_mine[:, :features], e_other[:, :features]], axis=0))
    for step, sent in enumerate(sents, 1):
        sent[...] = grads[:, lanes(group ^ step, wide)].astype(bf16)
    kept[...] = grads[:, lanes(group, wide)] + edge_total[:, lanes(group, wide)]


def add_groups(groups, *refs):
    parts, (kept, sent) = refs[:groups], refs[groups:]
    _, core = place()
    width = kept.shape[1]
    value = total(parts)
    kept[...] = jnp.where(core == 0, value[:, :width], value[:, width:]).astype(bf16)
    sent[...] = jnp.where(core == 0, value[:, width:], value[:, :width]).astype(bf16)


def add_nodes(shares, node_cot, node_grad):
    value = node_cot[...].astype(f32)
    for source in range(shares.shape[0]):
        value = value + shares[source].astype(f32)
    node_grad[...] = value.astype(bf16)


def assemble(next_mine, next_came, grad_mine, grad_came, edge_next, edge_grad):
    _, core = place()
    half = next_mine.shape[0]
    mine = pl.ds(pl.multiple_of(core * half, half), half)
    theirs = pl.ds(pl.multiple_of((1 - core) * half, half), half)
    edge_next[mine] = next_mine[...]
    edge_next[theirs] = next_came[...]
    edge_grad[mine] = grad_mine[...]
    edge_grad[theirs] = grad_came[...]


def shards(
    latent,
    edge_state,
    send_rows,
    sender_slot,
    receiver_row,
    edge_in_weight,
    edge_out_weight,
    edge_gain,
    node_in_weight,
    node_out_weight,
    node_gain,
    edge_cot,
    node_cot,
):
    nodes, width = latent.shape
    edge_dev = edge_state.shape[0]
    half = edge_dev // cores
    blocks = send_rows.shape[0]
    feats = lax.axis_size("feat")
    groups = feats // cores
    features = width * feats
    wide = width * cores
    hidden = edge_in_weight.shape[0] * cores
    table = blocks * nodes
    everyone = ("nodes", "feat")

    def swapped(values, bits):
        return lax.ppermute(values, "feat", [(i, i ^ bits) for i in range(feats)])

    def over_cores(values):
        return swapped(values, 1)

    def over_groups(values):
        return [swapped(values, cores * step) for step in range(1, groups)]

    gain_e, gain_n = edge_gain.reshape(1, width), node_gain.reshape(1, width)
    slot_rows = sender_slot.reshape(cores, half)
    receiver_rows = receiver_row.reshape(cores, half)

    (spread,) = stage(spread_latent, [((blocks * feats, nodes, width), bf16)], [latent])
    latents = lax.all_to_all(spread, everyone, 0, 0)
    states = [edge_state] + over_groups(edge_state)
    e_in = (edge_in_weight, over_cores(edge_in_weight))
    e_out = (edge_out_weight, over_cores(edge_out_weight))
    n_in = (node_in_weight, over_cores(node_in_weight))
    n_out = (node_out_weight, over_cores(node_out_weight))
    far = []
    for weights in over_groups(jnp.concatenate([node_in_weight[:, features:], node_out_weight], axis=1)):
        far += [weights, over_cores(weights)]
    (sent,) = stage(functools.partial(send_half, groups), [((half, groups * width), bf16)], states)
    state, pre, pick, take = stage(
        functools.partial(prepare_edges, groups),
        [((half, features), bf16), ((half, hidden), f32), ((table, half), bf16), ((nodes, half), bf16)],
        [*states, over_cores(sent), *e_in, slot_rows, receiver_rows, send_rows],
        scalars=1,
    )
    rows = edge_dev + 2 * nodes
    (pack,) = stage(pack_extra, [((rows, width), bf16)], [edge_cot, node_cot, gain_e, gain_n])
    packs = [pack] + over_groups(pack)
    (sent,) = stage(functools.partial(send_half, groups), [((rows - half, groups * width), bf16)], packs)
    extra_came = over_cores(sent)
    edge_pre, part, sent, own, lat = stage(
        finish_edges,
        [
            ((half, hidden), f32),
            ((half, features), f32),
            ((half + nodes, features), bf16),
            ((nodes, features), bf16),
            ((nodes, hidden), f32),
        ],
        [latents, pre, pick, take, *e_in, *e_out, *n_in],
        scratch=[((table, features), bf16)],
    )
    normed, inverse, next_mine, next_sent, aggregate, lat_all, extra = stage(
        functools.partial(update_edges, groups),
        [
            ((half, features), f32),
            ((half, 1), f32),
            ((half, width), bf16),
            ((half, width), bf16),
            ((nodes, features), f32),
            ((nodes, features), f32),
            ((half + 2 * nodes, features), bf16),
        ],
        [part, lat, *over_groups(sent), *packs, extra_came, state, take],
        scratch=[((half, features), bf16)],
    )
    aggregate2 = over_cores(aggregate)
    next_came = over_cores(next_sent)
    node_next, dpre, edge_total, spread = stage(
        functools.partial(turn, groups),
        [
            ((nodes, width), bf16),
            ((half, hidden), bf16),
            ((half, features), f32),
            ((blocks * feats, nodes, width), bf16),
        ],
        [*far, aggregate, aggregate2, own, lat_all, extra, take, pick, normed, inverse, edge_pre]
        + [*e_in, *e_out, *n_in, *n_out],
        scratch=[((nodes, features), bf16), ((table, features), f32)],
    )
    kept, *sents = stage(
        turn_edges,
        [((half, wide), f32)] + [((half, wide), bf16)] * (groups - 1),
        [dpre, edge_total, *e_in],
        scratch=[((half, features), f32)],
    )
    sents = [swapped(s, cores * k) for k, s in enumerate(sents, 1)]
    shares = lax.all_to_all(spread, everyone, 0, 0)
    grad_mine, grad_sent = stage(
        functools.partial(add_groups, groups),
        [((half, width), bf16), ((half, width), bf16)],
        [kept, *sents],
    )
    edge_next, edge_grad = stage(
        assemble,
        [((edge_dev, width), bf16), ((edge_dev, width), bf16)],
        [next_mine, next_came, grad_mine, over_cores(grad_sent)],
    )
    (node_grad,) = stage(add_nodes, [((nodes, width), bf16)], [shares, node_cot])
    return (edge_next, node_next, edge_grad, node_grad)


def solution(mesh):
    rows = P(("groups", "nodes"), "feat")
    flat = P(("groups", "nodes"))
    matrix = P("feat", None)
    vector = P("feat")
    return jax.shard_map(
        shards,
        mesh=mesh,
        in_specs=(
            rows,
            rows,
            P("groups", None, None),
            flat,
            flat,
            matrix,
            matrix,
            vector,
            matrix,
            matrix,
            vector,
            rows,
            rows,
        ),
        out_specs=(rows, rows, rows, rows),
        check_vma=False,
    )
```
